32 devices in a mesh: section: 2 (over y), tensor: 4 (over x, core), dp: 4 (over z).
Axes of the slice: x: 2, y: 2, z: 4, core: 2. Of those that a mesh axis runs over, the one named last changes fastest.
Arguments:
- inputs: bfloat16 [2, 2, 4, 729, 1152], P('section', None, 'dp', None, 'tensor'), may hold values from -6 to 6
- norm_gain: float32 [2, 2, 1152], P('section', None, 'tensor'), may hold values from 0.5 to 1.5
- norm_bias: float32 [2, 2, 1152], P('section', None, 'tensor'), may hold values from -1.8 to 1.8
- w_query: bfloat16 [2, 1152, 1152], P('section', None, 'tensor'), may hold values from -0.1875 to 0.1875
- b_query: float32 [2, 1152], P('section', 'tensor'), may hold values from -3 to 3
- w_key: bfloat16 [2, 1152, 1152], P('section', None, 'tensor'), may hold values from -0.1875 to 0.1875
- w_value: bfloat16 [2, 1152, 1152], P('section', None, 'tensor'), may hold values from -0.1875 to 0.1875
- b_value: float32 [2, 1152], P('section', 'tensor'), may hold values from -3 to 3
- w_out: bfloat16 [2, 1152, 1152], P('section', 'tensor'), may hold values from -0.75 to 0.75
- out_bias: float32 [2, 2, 1152], P('section', None, 'tensor'), may hold values from -1.8 to 1.8
- w_up: bfloat16 [2, 1152, 4304], P('section', None, 'tensor'), may hold values from -1 to 1
- b_up: float32 [2, 4304], P('section', 'tensor'), may hold values from -3 to 3
- w_down: bfloat16 [2, 4304, 1152], P('section', 'tensor'), may hold values from -0.09375 to 0.09375
Outputs:
- ends: float32 [2, 2, 4, 729, 1152], P('section', None, 'dp', None, 'tensor')
- grad_norm_gain: float32 [2, 2, 1152], P('section', None, 'tensor')
- grad_norm_bias: float32 [2, 2, 1152], P('section', None, 'tensor')
- grad_query: float32 [2, 1152, 1152], P('section', None, 'tensor')
- grad_b_query: float32 [2, 1152], P('section', 'tensor')
- grad_key: float32 [2, 1152, 1152], P('section', None, 'tensor')
- grad_value: float32 [2, 1152, 1152], P('section', None, 'tensor')
- grad_b_value: float32 [2, 1152], P('section', 'tensor')
- grad_out: float32 [2, 1152, 1152], P('section', 'tensor')
- grad_out_bias: float32 [2, 2, 1152], P('section', None, 'tensor')
- grad_up: float32 [2, 1152, 4304], P('section', None, 'tensor')
- grad_b_up: float32 [2, 4304], P('section', 'tensor')
- grad_down: float32 [2, 4304, 1152], P('section', 'tensor')
The draws below stay inside these ranges and needn't reach their ends.
All inputs are finite; a program needn't handle non-finite values.
Results may differ from the reference program's by a relative error of at most 0.014.
Values may be sent and summed in bfloat16 or wider, within the bound.
No kernel may reach another device: no remote copies, remote signals or barrier semaphores. Data moves between devices by JAX's collectives and lax.ppermute only.
A program may use at most 256 MiB of HBM per device.

```python
import jax
import jax.numpy as jnp
from jax import lax

D = 1152
HEADS = 16
HD = 72
FF = 4304
L = 729
MB = 2
IMG_DEV = 1
IMAGES = 4
SECTIONS = 2


def draw_w_up(key, part):
    key = jax.random.fold_in(key, 11)
    base_key, column_key = jax.random.split(key)
    base = jax.random.truncated_normal(base_key, -4.0, 4.0, (SECTIONS, D, FF), jnp.float32)
    column = jax.random.truncated_normal(column_key, -4.0, 4.0, (SECTIONS, 1, FF), jnp.float32)
    scale = D ** (-0.5)
    return (base * scale + column * (0.4 * scale)).astype(jnp.bfloat16)


def shard_levels(rng, shape, shards, smallest, high):
    level, own = 1.0, jax.random.fold_in(rng, 6)
    for position, blocks in shards:
        draws = jnp.exp(jax.random.uniform(jax.random.fold_in(own, position), (blocks,), jnp.float32, smallest / len(shards), high / len(shards)))
        level = level * jnp.repeat(draws, shape[position] // blocks).reshape([-1 if axis == position else 1 for axis in range(len(shape))])
    return level


def scatter_about(own_key, shape, scale, bound, pieces=(), dtype=jnp.bfloat16):
    loudness = shard_levels(own_key, shape, pieces, -0.22, 0.18) if pieces else 1.0
    values = jax.random.normal(own_key, shape, jnp.float32) * scale * loudness
    return jnp.minimum(jnp.maximum(values, -bound), bound).astype(dtype)


def setup_inputs(seed: int = 0) -> dict:
    arg_keys = jax.random.split(jax.random.key(seed), 14)
    return {
        "inputs": scatter_about(arg_keys[0], (2, MB, IMAGES, L, D), 1.0, 6.0, ((0, 2), (2, 4), (4, 4))),
        "norm_gain": jnp.clip(1.0 + 0.1 * jax.random.normal(arg_keys[1], (SECTIONS, 2, D), jnp.float32), 0.5, 1.5),
        "norm_bias": scatter_about(arg_keys[2], (SECTIONS, 2, D), 0.3, 1.8, ((0, 2), (2, 4)), jnp.float32),
        "w_query": scatter_about(arg_keys[3], (SECTIONS, D, D), D ** -0.5, 0.1875, ((0, 2), (2, 4))),
        "b_query": scatter_about(arg_keys[4], (SECTIONS, D), 0.5, 3.0, ((0, 2), (1, 4)), jnp.float32),
        "w_key": scatter_about(arg_keys[5], (SECTIONS, D, D), D ** -0.5, 0.1875, ((0, 2), (2, 4))),
        "w_value": scatter_about(arg_keys[6], (SECTIONS, D, D), D ** -0.5, 0.1875, ((0, 2), (2, 4))),
        "b_value": scatter_about(arg_keys[7], (SECTIONS, D), 0.5, 3.0, ((0, 2), (1, 4)), jnp.float32),
        "w_out": scatter_about(arg_keys[8], (SECTIONS, D, D), HD ** -0.5, 0.75, ((0, 2), (1, 4))),
        "out_bias": scatter_about(arg_keys[9], (SECTIONS, 2, D), 0.3, 1.8, ((0, 2), (2, 4)), jnp.float32),
        "w_up": draw_w_up(jax.random.fold_in(arg_keys[13], 71), 0),
        "b_up": scatter_about(arg_keys[11], (SECTIONS, FF), 0.5, 3.0, ((0, 2), (1, 4)), jnp.float32),
        "w_down": scatter_about(arg_keys[12], (SECTIONS, FF, D), FF ** -0.5, 0.09375, ((0, 2), (1, 4))),
    }


epsilon = 1e-06
precise = lax.Precision.HIGHEST

@jax.custom_vjp
def low(v):
    return lax.optimization_barrier(v.astype(jnp.bfloat16)).astype(jnp.float32)

@jax.custom_vjp
def low_back(v):
    return v

def low_keep(v):
    return (low(v), None)

def low_pass(kept, grad):
    return (grad,)

def back_keep(v):
    return (v, None)

def back_low(kept, grad):
    return (low(grad),)
low.defvjp(low_keep, low_pass)
low_back.defvjp(back_keep, back_low)

def project(values, matrix):
    return jnp.einsum('...d,de->...e', values, matrix, precision=precise)

def layer_norm(values, scale_row, shift_row):
    center = values - lax.optimization_barrier(jnp.mean(values, -1, keepdims=True))
    spread = lax.optimization_barrier(jnp.mean(center * center, -1, keepdims=True))
    return center * lax.rsqrt(spread + epsilon) * scale_row + shift_row

def image_attention(triple):
    queries, keys, values = triple
    scores = low_back(jnp.einsum('lhe,mhe->hlm', queries, keys, precision=precise) * HD ** (-0.5))
    highest = lax.optimization_barrier(jnp.max(scores, -1, keepdims=True))
    weights = jnp.exp(scores - highest)
    weights = weights / lax.optimization_barrier(jnp.sum(weights, -1, keepdims=True))
    return jnp.einsum('hlm,mhe->lhe', low(weights), values, precision=precise)

def encoder_layer(stream, params):
    norm_scale, norm_shift, query_w, query_b, key_w, value_w, value_b, out_w, out_b, up_w, up_b, down_w = params
    groups = stream.shape[0]
    normed = low(layer_norm(stream, norm_scale[0], norm_shift[0]))
    queries = low_back(low(project(normed, query_w) + query_b))
    keys = low_back(low(project(normed, key_w)))
    values = low_back(low(project(normed, value_w) + value_b))
    split = (groups, L, HEADS, HD)
    mixed = lax.map(jax.checkpoint(image_attention), (queries.reshape(split), keys.reshape(split), values.reshape(split)))
    mixed = low_back(low(mixed.reshape(groups, L, D)))
    middle = stream + low_back(project(mixed, out_w) + out_b[0])
    normed_two = low(layer_norm(middle, norm_scale[1], norm_shift[1]))
    hidden = low_back(project(normed_two, up_w) + up_b)
    active = low(jax.nn.gelu(hidden, approximate=True))
    return middle + low_back(project(active, down_w) + out_b[1])

def two_sections(stream, first_params, second_params):
    handed = low_back(low(encoder_layer(stream, first_params)))
    return encoder_layer(handed, second_params)

def reference(inputs, norm_gain, norm_bias, w_query, b_query, w_key, w_value, b_value, w_out, out_bias, w_up, b_up, w_down):
    arrays = (norm_gain, norm_bias, w_query, b_query, w_key, w_value, b_value, w_out, out_bias, w_up, b_up, w_down)
    section_params = tuple((tuple((array[section_index].astype(jnp.float32) for array in arrays)) for section_index in range(2)))
    blocks = MB * IMAGES // IMG_DEV
    streams = inputs[0].astype(jnp.float32).reshape(blocks, IMG_DEV, L, D)
    cotangents = inputs[1].astype(jnp.float32).reshape(blocks, IMG_DEV, L, D)

    def accumulate(totals, block):
        stream, cotangent = block
        result, pullback = jax.vjp(two_sections, stream, section_params[0], section_params[1])
        back_stream, first_grads, second_grads = pullback(cotangent)
        totals = jax.tree.map(lambda total, grad: total + grad, totals, (first_grads, second_grads))
        return (totals, (back_stream, result))
    zeros = jax.tree.map(jnp.zeros_like, section_params)
    totals, (back_streams, results) = lax.scan(accumulate, zeros, (streams, cotangents))
    ends = jnp.stack([back_streams.reshape(MB, IMAGES, L, D), results.reshape(MB, IMAGES, L, D)])
    grads = tuple((jnp.stack([totals[0][number], totals[1][number]]) for number in range(12)))
    return (ends, grads[0], grads[1], grads[2], grads[3], grads[4], grads[5], grads[6], grads[7], grads[8], grads[9], grads[10], grads[11])
```

```python
import functools

import jax
import jax.numpy as jnp
from jax import lax
from jax.experimental import pallas as pl
from jax.experimental.pallas import tpu as pltpu
from jax.sharding import PartitionSpec as P

HD = 72
LANES = 128
EPS = 1e-06
SCALE = HD**-0.5
LOG2E = 1.4426950408889634
FAR = -1e30
GELU_A = 0.7978845608028654
GELU_B = 0.044715
F32 = jnp.float32
BF16 = jnp.bfloat16
VMEM = pl.BlockSpec(memory_space=pltpu.VMEM)
SMEM = pl.BlockSpec(memory_space=pltpu.SMEM)


def run(body, outs, args, scalars=0, flops=0, scratch=(), limit=16):
    bytes_accessed = sum(a.size * a.dtype.itemsize for a in args)
    return pl.pallas_call(
        body,
        out_shape=[jax.ShapeDtypeStruct(shape, dtype) for shape, dtype in outs],
        in_specs=[SMEM] * scalars + [VMEM] * (len(args) - scalars),
        out_specs=[VMEM] * len(outs),
        scratch_shapes=list(scratch),
        compiler_params=pltpu.CompilerParams(vmem_limit_bytes=limit * 2**20),
        cost_estimate=pl.CostEstimate(
            flops=int(flops), bytes_accessed=int(bytes_accessed), transcendentals=0
        ),
    )(*args)


def mm(left, right):
    return jnp.dot(left, right, preferred_element_type=F32)


def mm_nt(left, right):
    return lax.dot_general(left, right, (((1,), (1,)), ((), ())), preferred_element_type=F32)


def mm_tn(left, right):
    return lax.dot_general(left, right, (((0,), (0,)), ((), ())), preferred_element_type=F32)


def unit_rows(x):
    center = x - jnp.mean(x, 1, keepdims=True)
    inverse = lax.rsqrt(jnp.mean(center * center, 1, keepdims=True) + EPS)
    return center * inverse, inverse


def assemble(stack, rel, order, rows):
    parts, _, cols = stack.shape
    half = parts // 2

    def body(rel_ref, order_ref, stack_ref, mine_ref, other_ref):
        for place in range(parts):
            start = pl.multiple_of(order_ref[place] * rows, 16)
            block = jnp.concatenate(
                [stack_ref[rel_ref[s], pl.ds(start, rows), :] for s in range(parts)], axis=1
            )
            out = mine_ref if place < half else other_ref
            at = (place % half) * rows
            out[at : at + rows, :] = block

    shape = ((half * rows, parts * cols), BF16)
    return run(body, [shape, shape], (rel, order, stack), scalars=2)


def select_rows(flag, base, blocks):
    def body(flag_ref, base_ref, *refs):
        out = refs[-1]

        @pl.when(flag_ref[0] != 0)
        def _():
            out[...] = base_ref[...]

        @pl.when(flag_ref[0] == 0)
        def _():
            at = 0
            for ref in refs[:-1]:
                out[at : at + ref.shape[0], :] = ref[...]
                at += ref.shape[0]

    return run(body, [(base.shape, BF16)], (flag, base, *blocks), scalars=1)[0]


def project(info, xm, xo, gain, bias, wq, bq, wk, wv, bv):
    half, width = xm.shape
    total = 2 * half
    cols = wq.shape[0]
    heads = cols // HD

    def body(info_ref, xm_ref, xo_ref, g_ref, b_ref, wq_ref, bq_ref, wk_ref, wv_ref, bv_ref,
             n_ref, q_ref, k_ref, v_ref):
        step = half // 2
        for index, ref in enumerate((xm_ref, xo_ref)):
            for at in range(0, half, step):
                unit, _ = unit_rows(ref[at : at + step, :].astype(F32))
                n_ref[index * half + at : index * half + at + step, :] = (
                    unit * g_ref[...] + b_ref[...]
                ).astype(BF16)
        normed = n_ref[...]
        row = lax.broadcasted_iota(jnp.int32, (total, LANES - HD), 0)
        lane = lax.broadcasted_iota(jnp.int32, (total, LANES - HD), 1)
        pad_start = info_ref[0]
        padded = (row >= pad_start) & (row < pad_start + info_ref[1])
        ones = jnp.where(lane == 0, 1.0, 0.0).astype(BF16)
        mask = jnp.where((lane == 0) & padded, FAR, 0.0).astype(BF16)

        def spread(value, out, extra):
            for h in range(heads):
                out[:, h * LANES : (h + 1) * LANES] = jnp.concatenate(
                    [value[:, h * HD : (h + 1) * HD], extra], axis=1
                )

        spread((mm_nt(normed, wq_ref[...]) + bq_ref[...]).astype(BF16), q_ref, ones)
        spread(mm_nt(normed, wk_ref[...]).astype(BF16), k_ref, mask)
        spread((mm_nt(normed, wv_ref[...]) + bv_ref[...]).astype(BF16), v_ref, ones)

    wide = ((total, heads * LANES), BF16)
    return run(
        body,
        [((total, width), BF16), wide, wide, wide],
        (info, xm, xo, gain, bias, wq, bq, wk, wv, bv),
        scalars=1,
        flops=6 * total * width * cols,
    )


def attend(first_row, q, k, v, wout, out_type):
    total, wide = q.shape
    heads = wide // LANES
    half = total // 2
    step = half // 2

    def body(q_ref, k_ref, v_ref, w_ref, z_ref, o_ref, l_ref):
        for at in range(0, half, step):
            outs, logs = [], []
            for h in range(heads):
                lanes = slice(h * LANES, (h + 1) * LANES)
                scores = mm_nt(q_ref[first_row + at : first_row + at + step, lanes], k_ref[:, lanes])
                highest = jnp.max(scores, 1, keepdims=True)
                weights = jnp.exp2((scores - highest) * (SCALE * LOG2E)).astype(BF16)
                mixed = mm(weights, v_ref[:, lanes])
                sums = mixed[:, HD : HD + 1]
                outs.append((mixed / sums).astype(BF16)[:, :HD])
                logs.append(highest * (SCALE * LOG2E) + jnp.log(sums) * LOG2E)
            mixed = jnp.concatenate(outs, axis=1)
            o_ref[at : at + step, :] = mixed
            z_ref[at : at + step, :] = mm(mixed, w_ref[...]).astype(out_type)
            logs = jnp.concatenate(logs + [jnp.zeros((step, LANES - heads), F32)], axis=1)
            l_ref[:, at : at + step] = logs.T[:8, :]

    return run(
        body,
        [((half, wout.shape[1]), out_type), ((half, heads * HD), BF16), ((8, half), F32)],
        (q, k, v, wout),
        flops=4 * half * total * LANES * heads + 2 * half * heads * HD * wout.shape[1],
    )


def middle(xm, own, arrived, out_bias, gain, bias):
    half, width = xm.shape
    parts = len(arrived) + 1
    rows = half // parts

    def body(x_ref, own_ref, *refs):
        got = refs[: parts - 1]
        ob_ref, g_ref, b_ref, h_ref, n_ref = refs[parts - 1 :]
        for p in range(parts):
            here = slice(p * rows, (p + 1) * rows)
            value = x_ref[here, :].astype(F32) + ob_ref[...]
            total = own_ref[here, :].astype(F32)
            for shift, ref in enumerate(got, 1):
                there = (p + shift) % parts
                total = total + ref[there * rows : (there + 1) * rows, :].astype(F32)
            value = value + total
            h_ref[here, :] = value
            unit, _ = unit_rows(value)
            n_ref[here, :] = (unit * g_ref[...] + b_ref[...]).astype(BF16)

    return run(
        body,
        [((half, width), F32), ((half, width), BF16)],
        (xm, own, *arrived, out_bias, gain, bias),
        flops=20 * half * width,
    )


def mlp(n2, w_up, b_up, w_down, out_type, save):
    half, width = n2.shape
    hidden = w_up.shape[0]
    step = half // 2

    def body(n_ref, wu_ref, bu_ref, wd_ref, z_ref, *saved):
        for at in range(0, half, step):
            here = slice(at, at + step)
            u = mm_nt(n_ref[here, :], wu_ref[...]) + bu_ref[...]
            square = u * u
            t = jnp.tanh(GELU_A * u * (1.0 + GELU_B * square))
            low = 0.5 * (1.0 + t)
            active = (u * low).astype(BF16)
            if save:
                slope = low + (0.5 * GELU_A) * u * (1.0 - t * t) * (1.0 + (3 * GELU_B) * square)
                saved[0][here, :] = active
                saved[1][here, :] = slope.astype(BF16)
            z_ref[here, :] = mm(active, wd_ref[...]).astype(out_type)

    outs = [((half, width), out_type)]
    if save:
        outs += [((half, hidden), BF16)] * 2
    return run(body, outs, (n2, w_up, b_up, w_down), flops=4 * half * width * hidden)


def mlp_back(g, slope, w_up, w_down, out_type):
    half, width = g.shape
    hidden = w_up.shape[0]
    step = half // 2

    def body(g_ref, s_ref, wu_ref, wd_ref, z_ref, d_ref):
        for at in range(0, half, step):
            here = slice(at, at + step)
            grad = mm_nt(g_ref[here, :], wd_ref[...]) * s_ref[here, :].astype(F32)
            grad = grad.astype(BF16)
            d_ref[here, :] = grad
            z_ref[here, :] = mm(grad, wu_ref[...]).astype(out_type)

    return run(
        body,
        [((half, width), out_type), ((half, hidden), BF16)],
        (g, slope, w_up, w_down),
        flops=4 * half * width * hidden,
    )


def middle_back(g, h, own, arrived, gain, quarter):
    half, width = g.shape
    parts = len(arrived) + 1
    rows = half // parts

    def body(g_ref, h_ref, own_ref, *refs):
        got = refs[: parts - 1]
        gain_ref, d_ref, low_ref, sums_ref = refs[parts - 1 :]
        for p in range(parts):
            here = slice(p * rows, (p + 1) * rows)
            grad = own_ref[here, :].astype(F32)
            for shift, ref in enumerate(got, 1):
                there = (p + shift) % parts
                grad = grad + ref[there * rows : (there + 1) * rows, :].astype(F32)
            unit, inverse = unit_rows(h_ref[here, :])
            scaled = grad * gain_ref[...]
            first = jnp.mean(scaled, 1, keepdims=True)
            second = jnp.mean(scaled * unit, 1, keepdims=True)
            upstream = g_ref[here, :].astype(F32)
            total = upstream + inverse * (scaled - first - unit * second)
            d_ref[here, :] = total
            low = total.astype(BF16)
            low_ref[here, :] = low
            if p == 0:
                sums_ref[...] = jnp.concatenate(
                    [
                        jnp.sum(grad * unit, 0, keepdims=True),
                        jnp.sum(grad, 0, keepdims=True),
                        jnp.sum(upstream, 0, keepdims=True),
                        jnp.sum(low.astype(F32), 0, keepdims=True),
                        jnp.zeros((4, width), F32),
                    ],
                    axis=0,
                )

    return run(
        body,
        [((half, width), F32), ((half, width), BF16), ((8, width), F32)],
        (g, h, own, *arrived, gain),
        flops=30 * half * width,
    )


def attend_back(dm, do, wout, q, k, v, lm, lo):
    half = dm.shape[0]
    total, wide = q.shape
    heads = wide // LANES
    step = total // 3

    def body(dm_ref, do_ref, w_ref, q_ref, k_ref, v_ref, lm_ref, lo_ref,
             dq_ref, dk_ref, dv_ref, up_ref, log_ref, p_ref, w_ref2):
        for index, ref in enumerate((dm_ref, do_ref)):
            here = slice(index * half, (index + 1) * half)
            grad = mm_nt(ref[...], w_ref[...]).astype(BF16)
            fill = jnp.zeros((half, LANES - HD), BF16)
            for h in range(heads):
                cols = slice(h * HD, (h + 1) * HD)
                up = jnp.concatenate([grad[:, cols], fill], axis=1)
                up_ref[here, h * LANES : (h + 1) * LANES] = up
        log_ref[0:8, 0:half] = lm_ref[...]
        log_ref[0:8, half:total] = lo_ref[...]
        dqs, dks, dvs = [], [], []
        for h in range(heads):
            lanes = slice(h * LANES, (h + 1) * LANES)
            up = up_ref[:, lanes]
            queries = q_ref[:, lanes]
            sums = jnp.zeros((1, total), F32)
            dv_h = []
            for at in range(0, total, step):
                here = slice(at, at + step)
                scores = mm_nt(k_ref[here, lanes], queries)
                probs = jnp.exp2(scores * (SCALE * LOG2E) - log_ref[h : h + 1, :])
                weighted = probs * mm_nt(v_ref[here, lanes], up)
                sums = sums + jnp.sum(weighted, 0, keepdims=True)
                p_ref[here, :] = probs
                w_ref2[here, :] = weighted
                dv_h.append(mm(probs.astype(BF16), up).astype(BF16)[:, :HD])
            dq_t = jnp.zeros((LANES, total), F32)
            dk_h = []
            for at in range(0, total, step):
                here = slice(at, at + step)
                dscores = (w_ref2[here, :] - p_ref[here, :] * sums).astype(BF16)
                dk_h.append((mm(dscores, queries) * SCALE).astype(BF16)[:, :HD])
                dq_t = dq_t + mm_tn(k_ref[here, lanes], dscores)
            dqs.append((dq_t * SCALE).T.astype(BF16)[:, :HD])
            dks.append(jnp.concatenate(dk_h, axis=0))
            dvs.append(jnp.concatenate(dv_h, axis=0))
        dq_ref[...] = jnp.concatenate(dqs, axis=1)
        dk_ref[...] = jnp.concatenate(dks, axis=1)
        dv_ref[...] = jnp.concatenate(dvs, axis=1)

    out = ((total, heads * HD), BF16)
    return run(
        body,
        [out, out, out],
        (dm, do, wout, q, k, v, lm, lo),
        flops=10 * total * total * LANES * heads + 2 * total * heads * HD * dm.shape[1],
        scratch=(
            pltpu.VMEM((total, wide), BF16),
            pltpu.VMEM((8, total), F32),
            pltpu.VMEM((total, total), F32),
            pltpu.VMEM((total, total), F32),
        ),
    )


def project_back(first_row, dq, dk, dv, wq, wk, wv, out_type):
    total, cols = dq.shape
    half = total // 2
    width = wq.shape[1]

    def body(dq_ref, dk_ref, dv_ref, wq_ref, wk_ref, wv_ref, z_ref):
        here = slice(first_row, first_row + half)
        z_ref[...] = (
            mm(dq_ref[here, :], wq_ref[...])
            + mm(dk_ref[here, :], wk_ref[...])
            + mm(dv_ref[here, :], wv_ref[...])
        ).astype(out_type)

    return run(
        body, [((half, width), out_type)], (dq, dk, dv, wq, wk, wv), flops=6 * half * cols * width
    )[0]


def start_back(xm, dh, own, arrived, gain):
    rows, width = own.shape
    count = len(arrived)

    def body(x_ref, dh_ref, own_ref, *refs):
        got = refs[:count]
        gain_ref, d_ref, low_ref, sums_ref = refs[count:]
        grad = own_ref[...]
        for ref in got:
            grad = grad + ref[...].astype(F32)
        unit, inverse = unit_rows(x_ref[0:rows, :].astype(F32))
        scaled = grad * gain_ref[...]
        first = jnp.mean(scaled, 1, keepdims=True)
        second = jnp.mean(scaled * unit, 1, keepdims=True)
        total = dh_ref[0:rows, :] + inverse * (scaled - first - unit * second)
        d_ref[...] = total
        low_ref[...] = total.astype(BF16)
        sums_ref[...] = jnp.concatenate(
            [
                jnp.sum(grad * unit, 0, keepdims=True),
                jnp.sum(grad, 0, keepdims=True),
                jnp.zeros((6, width), F32),
            ],
            axis=0,
        )

    return run(
        body,
        [((rows, width), F32), ((rows, width), BF16), ((8, width), F32)],
        (xm, dh, own, *arrived, gain),
        flops=30 * rows * width,
    )


def core_swap(value):
    size = lax.axis_size("tensor")
    return lax.ppermute(value, "tensor", [(i, i ^ 1) for i in range(size)])


def chip_shift(value, shift):
    size = lax.axis_size("tensor")
    return lax.ppermute(value, "tensor", [(i, (i + 2 * shift) % size) for i in range(size)])


def share_half(half, chips):
    return [chip_shift(half, s) for s in range(1, chips)]


def spread_block(block, chips):
    mine = [block] + [chip_shift(block, chips - p) for p in range(1, chips)]
    return mine, [core_swap(b) for b in mine]


def sum_blocks(half, chips):
    rows = half.shape[0] // chips
    return half[:rows], [
        chip_shift(half[p * rows : (p + 1) * rows].astype(BF16), p) for p in range(1, chips)
    ]


def to_section(value, step):
    pairs = [(0, 1)] if step > 0 else [(1, 0)]
    return lax.ppermute(value, "section", pairs)


def forward(x, w, info, chips, save, end):
    xm, xo = x
    normed, q, k, v = project(
        info, xm, xo, w["gain"][0], w["bias"][0], w["wq"], w["bq"], w["wk"], w["wv"], w["bv"]
    )
    half = xm.shape[0]
    z_other, o_other, l_other = attend(half, q, k, v, w["wout"], BF16)
    z_other = core_swap(z_other)
    z_mine, o_mine, l_mine = attend(0, q, k, v, w["wout"], F32)
    own = (z_mine + z_other.astype(F32)).astype(BF16)
    hidden, n2m = middle(
        xm, own, share_half(own, chips), w["out_bias"][0], w["gain"][1], w["bias"][1]
    )
    n2o = core_swap(n2m)
    other = mlp(n2o, w["w_up"], w["b_up"], w["w_down"], BF16, save)
    y_other = core_swap(other[0])
    mine = mlp(n2m, w["w_up"], w["b_up"], w["w_down"], F32, save)
    total, arrived = sum_blocks(mine[0] + y_other.astype(F32), chips)
    for value in arrived:
        total = total + value.astype(F32)
    result = hidden[: total.shape[0]] + total + w["out_bias"][1]
    saved = None
    if save:
        saved = dict(
            x=x, normed=normed, q=q, k=k, v=v, o=(o_mine, o_other), l=(l_mine, l_other),
            h=hidden, n2=(n2m, n2o), m=(mine[1], other[1]), slope=(mine[2], other[2]),
        )
    return result, saved


def backward(g, saved, w, chips):
    gm, go = g
    z_other, du_other = mlp_back(go, saved["slope"][1], w["w_up"], w["w_down"], BF16)
    z_other = core_swap(z_other)
    z_mine, du_mine = mlp_back(gm, saved["slope"][0], w["w_up"], w["w_down"], F32)
    own = (z_mine + z_other.astype(F32)).astype(BF16)
    dh, dhm, sums_two = middle_back(
        gm, saved["h"], own, share_half(own, chips), w["gain"][1], None
    )
    dho = core_swap(dhm)
    q, k, v = saved["q"], saved["k"], saved["v"]
    dq, dk, dv = attend_back(dhm, dho, w["wout"], q, k, v, *saved["l"])
    half = gm.shape[0]
    d_other = core_swap(project_back(half, dq, dk, dv, w["wq"], w["wk"], w["wv"], BF16))
    d_mine = project_back(0, dq, dk, dv, w["wq"], w["wk"], w["wv"], F32)
    total, arrived = sum_blocks(d_mine + d_other.astype(F32), chips)
    dx, dx_low, sums_one = start_back(saved["x"][0], dh, total, arrived, w["gain"][0])
    work = dict(
        du=(du_mine, du_other), dh=(dhm, dho), dq=dq, dk=dk, dv=dv, sums=(sums_one, sums_two)
    )
    return dx, dx_low, work


def line_sum(pieces):
    place = lax.axis_index("dp")
    inner = (place == 1) | (place == 2)
    results, done = [], []
    for index, piece in enumerate(pieces):
        if index >= 2:
            piece, done[index - 2] = lax.optimization_barrier((piece, done[index - 2]))
        here = piece + lax.ppermute(piece, "dp", [(0, 1), (3, 2)])
        both = here + lax.ppermute(here, "dp", [(1, 2), (2, 1)])
        done.append(both)
    for both in done:
        back = lax.ppermute(both, "dp", [(1, 0), (2, 3)])
        results.append(jnp.where(inner, both, back))
    return results


def finish(value):
    rows, width = value.shape
    step = 128

    def body(value_ref, out_ref):
        out_ref[...] = value_ref[...].astype(F32).reshape(step, 1, width)

    return pl.pallas_call(
        body,
        out_shape=jax.ShapeDtypeStruct((rows, 1, width), F32),
        grid=(pl.cdiv(rows, step),),
        in_specs=[pl.BlockSpec((step, width), lambda i: (i, 0))],
        out_specs=pl.BlockSpec((step, 1, width), lambda i: (i, 0, 0)),
        compiler_params=pltpu.CompilerParams(vmem_limit_bytes=8 * 2**20),
    )(value)


def dp_sum(pieces):
    if lax.axis_size("dp") == 4:
        return line_sum(pieces)
    return [lax.psum(piece, "dp") for piece in pieces]


def per_device(inputs, norm_gain, norm_bias, w_query, b_query, w_key, w_value, b_value, w_out,
               out_bias, w_up, b_up, w_down):
    first = lax.axis_index("section") == 0
    flag = first.astype(jnp.int32)[None]
    me = lax.axis_index("tensor")
    size = lax.axis_size("tensor")
    chips = size // 2
    chip, core = me // 2, me % 2
    _, micro, images, length, cols = inputs.shape
    unit = 16 * size
    total = -(-length // unit) * unit
    rows = total // size
    pad = total - length
    places = jnp.arange(size)
    order = ((chip + places % chips) % chips) * 2 + (core + places // chips) % 2
    order = order.astype(jnp.int32)
    rel = ((places // 2 - chip) % chips + chips * ((places + core) % 2)).astype(jnp.int32)
    info = jnp.stack([rel[size - 1] * rows + rows - pad, jnp.int32(pad)])
    images_all = micro * images

    small = jnp.concatenate([norm_gain[0], norm_bias[0], out_bias[0]], axis=0)
    small = lax.all_gather(small, "tensor", axis=1, tiled=True)
    w = dict(
        gain=(small[0:1], small[1:2]), bias=(small[2:3], small[3:4]),
        out_bias=(small[4:5], small[5:6]),
        wq=w_query[0].T, bq=b_query, wk=w_key[0].T, wv=w_value[0].T, bv=b_value,
        wout=w_out[0], w_up=w_up[0].T, b_up=b_up, w_down=w_down[0],
    )
    own = jnp.pad(
        inputs[0].reshape(images_all, length, cols), ((0, 0), (0, pad), (0, 0))
    )
    full = []
    for n in range(images_all):
        mine, other = spread_block(own[n], chips)
        full.append(assemble(jnp.stack(mine + other), rel, order, rows))

    def widen(block, base):
        mine, other = spread_block(block, chips)
        return (
            select_rows(flag, base[0], mine),
            select_rows(flag, base[1], other),
        )

    streams, results, saves = [], [], []
    for n in range(images_all):
        result, _ = forward(full[n], w, info, chips, False, False)
        streams.append(widen(to_section(result.astype(BF16), 1), full[n]))
    for n in range(images_all):
        result, saved = forward(streams[n], w, info, chips, True, True)
        results.append(result)
        saves.append(saved)
    ends, works, upstreams = [], [], []
    for n in range(images_all):
        _, low, _ = backward(full[n], saves[n], w, chips)
        mine, other = spread_block(to_section(low, -1), chips)
        flip = 1 - flag
        upstreams.append(
            (select_rows(flip, full[n][0], mine), select_rows(flip, full[n][1], other))
        )
    for n in range(images_all):
        dx, _, work = backward(upstreams[n], saves[n], w, chips)
        ends.append(jnp.where(first, dx, results[n]))
        works.append(work)

    def outer(pairs):
        acc = None
        for left, right in pairs:
            term = lax.dot_general(
                left, right, (((0,), (0,)), ((), ())), preferred_element_type=F32
            )
            acc = term if acc is None else acc + term
        return acc.astype(BF16)

    span = range(images_all)
    g_down = outer([(saves[n]["m"][i], upstreams[n][i]) for n in span for i in (0, 1)])
    g_up = outer([(works[n]["du"][i], saves[n]["n2"][i]) for n in span for i in (0, 1)])
    g_out = outer([(saves[n]["o"][i], works[n]["dh"][i]) for n in span for i in (0, 1)])
    g_query = outer([(works[n]["dq"], saves[n]["normed"]) for n in span])
    g_key = outer([(works[n]["dk"], saves[n]["normed"]) for n in span])
    g_value = outer([(works[n]["dv"], saves[n]["normed"]) for n in span])
    g_down, g_up, g_out, g_query, g_key, g_value = dp_sum(
        [g_down, g_up, g_out, g_query, g_key, g_value]
    )

    def total_of(parts):
        return sum(jnp.sum(p.astype(F32), 0) for p in parts)

    wide = sum(
        jnp.stack(
            [
                works[n]["sums"][0][0], works[n]["sums"][1][0],
                works[n]["sums"][0][1], works[n]["sums"][1][1],
                works[n]["sums"][1][3], works[n]["sums"][1][2],
            ]
        )
        for n in span
    )
    wide = lax.psum(wide, ("tensor", "dp"))
    wide = lax.dynamic_slice_in_dim(wide, me * cols, cols, 1)
    narrow = jnp.concatenate(
        [
            total_of([works[n]["dq"] for n in span]),
            total_of([works[n]["dv"] for n in span]),
            total_of([works[n]["du"][i] for n in span for i in (0, 1)]),
        ]
    )
    narrow = lax.psum(narrow, "dp")
    heads = b_query.shape[1]

    ends = jnp.stack(ends).reshape(images_all, rows, size, cols)
    ends = lax.all_to_all(ends, "tensor", split_axis=2, concat_axis=1, tiled=True)
    ends = ends.reshape(images_all, total, cols)[:, :length]
    ends = ends.reshape(1, micro, images, length, cols)
    return (
        ends, wide[None, 0:2], wide[None, 2:4], g_query.T[None].astype(F32), narrow[None, :heads], g_key.T[None].astype(F32),
        g_value.T[None].astype(F32), narrow[None, heads : 2 * heads], g_out[None].astype(F32), wide[None, 4:6],
        finish(g_up).transpose(1, 2, 0),
        narrow[None, 2 * heads :], finish(g_down).transpose(1, 0, 2),
    )


def solution(mesh):
    columns = P("section", None, "tensor")
    vector = P("section", "tensor")
    stacked = P("section", "tensor", None)
    tokens = P("section", None, "dp", None, "tensor")
    weights = (columns, columns, columns, vector, columns, columns, vector, stacked, columns,
               columns, vector, stacked)
    return jax.shard_map(
        per_device, mesh=mesh, in_specs=(tokens, *weights), out_specs=(tokens, *weights),
        check_vma=False,
    )
```

```python
import functools

import jax
import jax.numpy as jnp
from jax import lax
from jax.experimental import pallas as pl
from jax.experimental.pallas import tpu as pltpu
from jax.sharding import PartitionSpec as P

HD = 72
LANES = 128
EPS = 1e-06
SCALE = HD**-0.5
LOG2E = 1.4426950408889634
FAR = -1e30
LIMIT = 6
COST = 14
STEP = 48
GELU_A = 0.7978845608028654
GELU_B = 0.044715
F32 = jnp.float32
BF16 = jnp.bfloat16
VMEM = pl.BlockSpec(memory_space=pltpu.VMEM)
SMEM = pl.BlockSpec(memory_space=pltpu.SMEM)


def run(body, outs, args, scalars=0, flops=0, scratch=(), limit=LIMIT, after=()):
    bytes_accessed = sum(a.size * a.dtype.itemsize for a in args) + sum(
        jnp.dtype(dtype).itemsize * shape[0] * shape[1] for shape, dtype in outs
    )
    count, extra = len(args), len(after)

    def kernel(*refs):
        body(*refs[:count], *refs[count + extra :])

    return pl.pallas_call(
        kernel,
        out_shape=[jax.ShapeDtypeStruct(shape, dtype) for shape, dtype in outs],
        in_specs=[SMEM] * scalars
        + [VMEM] * (count - scalars)
        + [pl.BlockSpec(memory_space=pl.ANY)] * extra,
        out_specs=[VMEM] * len(outs),
        scratch_shapes=list(scratch),
        compiler_params=pltpu.CompilerParams(vmem_limit_bytes=limit * 2**20),
        cost_estimate=pl.CostEstimate(
            flops=int(flops) * COST, bytes_accessed=int(bytes_accessed), transcendentals=0
        ),
    )(*args, *after)


def mm(left, right):
    return jnp.dot(left, right, preferred_element_type=F32)


def mm_nt(left, right):
    return lax.dot_general(left, right, (((1,), (1,)), ((), ())), preferred_element_type=F32)


def mm_tn(left, right):
    return lax.dot_general(left, right, (((0,), (0,)), ((), ())), preferred_element_type=F32)


def unit_rows(x):
    center = x - jnp.mean(x, 1, keepdims=True)
    inverse = lax.rsqrt(jnp.mean(center * center, 1, keepdims=True) + EPS)
    return center * inverse, inverse


def assemble(parts, length, sources, order, rows, extra, after=()):
    count = len(parts)
    cols = parts[0].shape[0]
    half, total, width = count // 2, rows * count, cols * count

    def body(*refs):
        src_ref, order_ref = refs[:2]
        part_refs = refs[2 : 2 + count]
        mine_ref, other_ref, *small_out, wide_ref, tall_ref = refs[2 + count :]
        edge = length // LANES * LANES
        wide_ref[:, edge:] = jnp.zeros((width, wide_ref.shape[1] - edge), BF16)
        for i in range(count):
            start = pl.multiple_of(src_ref[i] * cols, 16)
            wide_ref[pl.ds(start, cols), 0 : parts[i].shape[1]] = part_refs[i][...]
        tall_ref[...] = wide_ref[...].T
        if extra:
            behind = tall_ref[total : total + 3 * extra, :].astype(F32)
            small_out[0][...] = (
                behind[0:extra] + behind[extra : 2 * extra] + behind[2 * extra :]
            )
            tall_ref[total : total + LANES, :] = jnp.zeros((LANES, width), BF16)
        for place in range(count):
            start = pl.multiple_of(order_ref[place] * rows, 16)
            out = mine_ref if place < half else other_ref
            at = (place % half) * rows
            out[at : at + rows, :] = tall_ref[pl.ds(start, rows), :]

    shape = ((half * rows, width), BF16)
    deep = total + (LANES if extra else 0)
    mine, other, *small = run(
        body,
        [shape, shape] + ([((extra, width), F32)] if extra else []),
        (sources, order, *parts),
        scalars=2,
        scratch=(pltpu.VMEM((width, deep), BF16), pltpu.VMEM((deep, width), BF16)),
        limit=10,
        after=after,
    )
    return (mine, other), small


class Source:
    def __init__(self, halves=None, blocks=None, flag=None):
        self.halves, self.blocks, self.flag = halves, blocks, flag

    def operands(self, which):
        scalars = [] if self.flag is None else [self.flag]
        arrays = []
        for i in which:
            arrays += [] if self.halves is None else [self.halves[i]]
            arrays += [] if self.blocks is None else self.blocks[i]
        return scalars, arrays

    def reader(self, which, scalar_refs, refs):
        refs, table = list(refs), {}
        for i in which:
            base = None if self.halves is None else refs.pop(0)
            count = 0 if self.blocks is None else len(self.blocks[i])
            table[i] = (base, [refs.pop(0) for _ in range(count)])

        def read(i, start, rows):
            base, blocks = table[i]
            value = None
            if blocks:
                size = blocks[0].shape[0]
                value = blocks[start // size][start % size : start % size + rows, :]
            if base is not None:
                at_hand = base[start : start + rows, :]
                if value is None:
                    return at_hand
                value = jnp.where(scalar_refs[0][0] != 0, at_hand, value)
            return value

        return read


def project(info, source, gain, bias, wq, bq, wk, wv, bv, rows, after=()):
    cols, width = wq.shape
    heads = cols // HD
    scalars, arrays = source.operands((0, 1))
    count, total = len(arrays), rows
    half = total // 2
    step = STEP

    def body(*refs):
        info_ref, flags = refs[0], refs[1 : 1 + len(scalars)]
        refs = refs[1 + len(scalars) :]
        read = source.reader((0, 1), flags, refs[:count])
        (g_ref, b_ref, wq_ref, bq_ref, wk_ref, wv_ref, bv_ref,
         x_ref, n_ref, q_ref, k_ref, v_ref) = refs[count:]
        for index in (0, 1):
            for at in range(0, half, step):
                value = read(index, at, step)
                if index == 0:
                    x_ref[at : at + step, :] = value
                unit, _ = unit_rows(value.astype(F32))
                n_ref[index * half + at : index * half + at + step, :] = (
                    unit * g_ref[...] + b_ref[...]
                ).astype(BF16)
        normed = n_ref[...]
        row = lax.broadcasted_iota(jnp.int32, (total, LANES - HD), 0)
        lane = lax.broadcasted_iota(jnp.int32, (total, LANES - HD), 1)
        pad_start = info_ref[0]
        padded = (row >= pad_start) & (row < pad_start + info_ref[1])
        ones = jnp.where(lane == 0, 1.0, 0.0).astype(BF16)
        mask = jnp.where((lane == 0) & padded, FAR, 0.0).astype(BF16)

        def spread(value, out, extra):
            for h in range(heads):
                out[:, h * LANES : (h + 1) * LANES] = jnp.concatenate(
                    [value[:, h * HD : (h + 1) * HD], extra], axis=1
                )

        spread((mm_nt(normed, wq_ref[...]) + bq_ref[...]).astype(BF16), q_ref, ones)
        spread(mm_nt(normed, wk_ref[...]).astype(BF16), k_ref, mask)
        spread((mm_nt(normed, wv_ref[...]) + bv_ref[...]).astype(BF16), v_ref, ones)

    wide = ((total, heads * LANES), BF16)
    return run(
        body,
        [((half, width), BF16), ((total, width), BF16), wide, wide, wide],
        (info, *scalars, *arrays, gain, bias, wq, bq, wk, wv, bv),
        scalars=1 + len(scalars),
        flops=6 * total * width * cols,
        after=after,
    )


def attend(first_row, q, k, v, wout, out_type):
    total, wide = q.shape
    heads = wide // LANES
    half = total // 2
    step = half // 2

    def body(q_ref, k_ref, v_ref, w_ref, z_ref, o_ref, l_ref):
        for at in range(0, half, step):
            outs, logs = [], []
            for h in range(heads):
                lanes = slice(h * LANES, (h + 1) * LANES)
                scores = mm_nt(q_ref[first_row + at : first_row + at + step, lanes], k_ref[:, lanes])
                highest = jnp.max(scores, 1, keepdims=True)
                weights = jnp.exp2((scores - highest) * (SCALE * LOG2E)).astype(BF16)
                mixed = mm(weights, v_ref[:, lanes])
                sums = mixed[:, HD : HD + 1]
                outs.append((mixed / sums).astype(BF16)[:, :HD])
                logs.append(highest * (SCALE * LOG2E) + jnp.log(sums) * LOG2E)
            mixed = jnp.concatenate(outs, axis=1)
            o_ref[at : at + step, :] = mixed
            z_ref[at : at + step, :] = mm(mixed, w_ref[...]).astype(out_type)
            logs = jnp.concatenate(logs + [jnp.zeros((step, LANES - heads), F32)], axis=1)
            l_ref[:, at : at + step] = logs.T[:8, :]

    return run(
        body,
        [((half, wout.shape[1]), out_type), ((half, heads * HD), BF16), ((8, half), F32)],
        (q, k, v, wout),
        flops=4 * half * total * LANES * heads + 2 * half * heads * HD * wout.shape[1],
    )


def middle(xm, own, arrived, out_bias, gain, bias, after=()):
    half, width = xm.shape
    parts = len(arrived) + 1
    rows = half // parts

    def body(x_ref, own_ref, *refs):
        got = refs[: parts - 1]
        ob_ref, g_ref, b_ref, h_ref, n_ref = refs[parts - 1 :]
        def step(i, carry):
            at = pl.multiple_of(i * STEP, 16)
            here = pl.ds(at, STEP)
            value = x_ref[here, :].astype(F32) + ob_ref[...]
            total = own_ref[here, :].astype(F32)
            for shift, ref in enumerate(got, 1):
                there = pl.multiple_of(lax.rem(at + shift * rows, half), 16)
                total = total + ref[pl.ds(there, STEP), :].astype(F32)
            value = value + total
            h_ref[here, :] = value
            unit, _ = unit_rows(value)
            n_ref[here, :] = (unit * g_ref[...] + b_ref[...]).astype(BF16)
            return carry

        lax.fori_loop(0, half // STEP, step, 0)

    return run(
        body,
        [((half, width), F32), ((half, width), BF16)],
        (xm, own, *arrived, out_bias, gain, bias),
        flops=20 * half * width,
        after=after,
    )


def mlp(n2, w_up, b_up, w_down, out_type, save):
    half, width = n2.shape
    hidden = w_up.shape[0]
    step = half // 2

    def body(n_ref, wu_ref, bu_ref, wd_ref, z_ref, *saved):
        for at in range(0, half, step):
            here = slice(at, at + step)
            u = mm_nt(n_ref[here, :], wu_ref[...]) + bu_ref[...]
            square = u * u
            t = jnp.tanh(GELU_A * u * (1.0 + GELU_B * square))
            low = 0.5 * (1.0 + t)
            active = (u * low).astype(BF16)
            if save:
                slope = low + (0.5 * GELU_A) * u * (1.0 - t * t) * (1.0 + (3 * GELU_B) * square)
                saved[0][here, :] = active
                saved[1][here, :] = slope.astype(BF16)
            z_ref[here, :] = mm(active, wd_ref[...]).astype(out_type)

    outs = [((half, width), out_type)]
    if save:
        outs += [((half, hidden), BF16)] * 2
    return run(body, outs, (n2, w_up, b_up, w_down), flops=4 * half * width * hidden)


def mlp_back(which, source, slope, w_up, w_down, out_type, after=()):
    half, hidden = slope.shape
    width = w_up.shape[1]
    scalars, arrays = source.operands((which,))
    count = len(arrays)
    step = half // 2 if source.blocks is None else source.blocks[0][0].shape[0]

    def body(*refs):
        read = source.reader((which,), refs[: len(scalars)], refs[len(scalars) :][:count])
        s_ref, wu_ref, wd_ref, g_ref, z_ref, d_ref = refs[len(scalars) + count :]
        for at in range(0, half, step):
            g_ref[at : at + step, :] = read(which, at, step)
        for at in range(0, half, half // 2):
            here = slice(at, at + half // 2)
            grad = mm_nt(g_ref[here, :], wd_ref[...]) * s_ref[here, :].astype(F32)
            grad = grad.astype(BF16)
            d_ref[here, :] = grad
            z_ref[here, :] = mm(grad, wu_ref[...]).astype(out_type)

    return run(
        body,
        [((half, width), BF16), ((half, width), out_type), ((half, hidden), BF16)],
        (*scalars, *arrays, slope, w_up, w_down),
        scalars=len(scalars),
        flops=4 * half * width * hidden,
        after=after,
    )


def middle_back(g, h, own, arrived, gain, after=()):
    half, width = g.shape
    parts = len(arrived) + 1
    rows = half // parts

    def body(g_ref, h_ref, own_ref, *refs):
        got = refs[: parts - 1]
        gain_ref, d_ref, low_ref, sums_ref = refs[parts - 1 :]
        def step(i, sums):
            at = pl.multiple_of(i * STEP, 16)
            here = pl.ds(at, STEP)
            grad = own_ref[here, :].astype(F32)
            for shift, ref in enumerate(got, 1):
                there = pl.multiple_of(lax.rem(at + shift * rows, half), 16)
                grad = grad + ref[pl.ds(there, STEP), :].astype(F32)
            unit, inverse = unit_rows(h_ref[here, :])
            scaled = grad * gain_ref[...]
            first = jnp.mean(scaled, 1, keepdims=True)
            second = jnp.mean(scaled * unit, 1, keepdims=True)
            upstream = g_ref[here, :].astype(F32)
            total = upstream + inverse * (scaled - first - unit * second)
            d_ref[here, :] = total
            low = total.astype(BF16)
            low_ref[here, :] = low
            terms = (grad * unit, grad, upstream, low.astype(F32))
            return tuple(a + jnp.sum(t, 0, keepdims=True) for a, t in zip(sums, terms))

        zeros = (jnp.zeros((1, width), F32),) * 4
        sums = lax.fori_loop(0, rows // STEP, step, zeros)
        lax.fori_loop(rows // STEP, half // STEP, lambda i, c: (step(i, zeros), c)[1], 0)
        for i in range(4):
            sums_ref[i : i + 1, :] = sums[i]

    return run(
        body,
        [((half, width), F32), ((half, width), BF16), ((8, width), F32)],
        (g, h, own, *arrived, gain),
        flops=30 * half * width,
        after=after,
    )


def attend_back(dm, do, wout, q, k, v, lm, lo):
    half = dm.shape[0]
    total, wide = q.shape
    heads = wide // LANES
    step = total // 3

    def body(dm_ref, do_ref, w_ref, q_ref, k_ref, v_ref, lm_ref, lo_ref,
             dq_ref, dk_ref, dv_ref, up_ref, log_ref, p_ref, w_ref2):
        for index, ref in enumerate((dm_ref, do_ref)):
            here = slice(index * half, (index + 1) * half)
            grad = mm_nt(ref[...], w_ref[...]).astype(BF16)
            fill = jnp.zeros((half, LANES - HD), BF16)
            for h in range(heads):
                cols = slice(h * HD, (h + 1) * HD)
                up = jnp.concatenate([grad[:, cols], fill], axis=1)
                up_ref[here, h * LANES : (h + 1) * LANES] = up
        log_ref[0:8, 0:half] = lm_ref[...]
        log_ref[0:8, half:total] = lo_ref[...]
        dqs, dks, dvs = [], [], []
        for h in range(heads):
            lanes = slice(h * LANES, (h + 1) * LANES)
            up = up_ref[:, lanes]
            queries = q_ref[:, lanes]
            sums = jnp.zeros((1, total), F32)
            dv_h = []
            for at in range(0, total, step):
                here = slice(at, at + step)
                scores = mm_nt(k_ref[here, lanes], queries)
                probs = jnp.exp2(scores * (SCALE * LOG2E) - log_ref[h : h + 1, :])
                weighted = probs * mm_nt(v_ref[here, lanes], up)
                sums = sums + jnp.sum(weighted, 0, keepdims=True)
                p_ref[here, :] = probs
                w_ref2[here, :] = weighted
                dv_h.append(mm(probs.astype(BF16), up).astype(BF16)[:, :HD])
            dq_t = jnp.zeros((LANES, total), F32)
            dk_h = []
            for at in range(0, total, step):
                here = slice(at, at + step)
                dscores = (w_ref2[here, :] - p_ref[here, :] * sums).astype(BF16)
                dk_h.append((mm(dscores, queries) * SCALE).astype(BF16)[:, :HD])
                dq_t = dq_t + mm_tn(k_ref[here, lanes], dscores)
            dqs.append((dq_t * SCALE).T.astype(BF16)[:, :HD])
            dks.append(jnp.concatenate(dk_h, axis=0))
            dvs.append(jnp.concatenate(dv_h, axis=0))
        dq_ref[...] = jnp.concatenate(dqs, axis=1)
        dk_ref[...] = jnp.concatenate(dks, axis=1)
        dv_ref[...] = jnp.concatenate(dvs, axis=1)

    out = ((total, heads * HD), BF16)
    return run(
        body,
        [out, out, out],
        (dm, do, wout, q, k, v, lm, lo),
        flops=10 * total * total * LANES * heads + 2 * total * heads * HD * dm.shape[1],
        scratch=(
            pltpu.VMEM((total, wide), BF16),
            pltpu.VMEM((8, total), F32),
            pltpu.VMEM((total, total), F32),
            pltpu.VMEM((total, total), F32),
        ),
        limit=12,
    )


def project_back(first_row, dq, dk, dv, wq, wk, wv, out_type):
    total, cols = dq.shape
    half = total // 2
    width = wq.shape[1]

    def body(dq_ref, dk_ref, dv_ref, wq_ref, wk_ref, wv_ref, z_ref):
        here = slice(first_row, first_row + half)
        z_ref[...] = (
            mm(dq_ref[here, :], wq_ref[...])
            + mm(dk_ref[here, :], wk_ref[...])
            + mm(dv_ref[here, :], wv_ref[...])
        ).astype(out_type)

    return run(
        body, [((half, width), out_type)], (dq, dk, dv, wq, wk, wv), flops=6 * half * cols * width
    )[0]


def start_back(xm, dh, own, arrived, gain, after=()):
    rows, width = own.shape
    part = rows // pieces_of(rows)
    count = len(arrived)

    def body(x_ref, dh_ref, own_ref, *refs):
        got = refs[:count]
        gain_ref, d_ref, sums_ref, *low_refs = refs[count:]
        def step(i, sums):
            here = pl.ds(pl.multiple_of(i * STEP, 16), STEP)
            grad = own_ref[here, :]
            for ref in got:
                grad = grad + ref[here, :].astype(F32)
            unit, inverse = unit_rows(x_ref[here, :].astype(F32))
            scaled = grad * gain_ref[...]
            first = jnp.mean(scaled, 1, keepdims=True)
            second = jnp.mean(scaled * unit, 1, keepdims=True)
            total = dh_ref[here, :] + inverse * (scaled - first - unit * second)
            d_ref[here, :] = total
            return tuple(
                a + jnp.sum(t, 0, keepdims=True) for a, t in zip(sums, (grad * unit, grad))
            )

        sums = lax.fori_loop(0, rows // STEP, step, (jnp.zeros((1, width), F32),) * 2)
        for i in range(2):
            sums_ref[i : i + 1, :] = sums[i]
        for i, ref in enumerate(low_refs):
            ref[...] = d_ref[i * part : (i + 1) * part, :].astype(BF16)

    d, sums, *low = run(
        body,
        [((rows, width), F32), ((8, width), F32)]
        + [((part, width), BF16)] * (rows // part),
        (xm, dh, own, *arrived, gain),
        flops=30 * rows * width,
        after=after,
    )
    return d, low, sums


def finish_rows(hidden, total, arrived, out_bias, after=()):
    rows, width = total[0].shape
    part = rows // pieces_of(rows)

    def body(h_ref, total_ref, *refs):
        bias_ref, y_ref, *low_refs = refs[len(arrived) :]
        value = total_ref[...]
        for ref in refs[: len(arrived)]:
            value = value + ref[...].astype(F32)
        value = h_ref[0:rows, :] + value + bias_ref[...]
        y_ref[...] = value
        for i, ref in enumerate(low_refs):
            ref[...] = value[i * part : (i + 1) * part, :].astype(BF16)

    y, *low = run(
        body,
        [((rows, width), F32)] + [((part, width), BF16)] * (rows // part),
        (hidden, total[0], *arrived, out_bias),
        flops=4 * rows * width,
        after=after,
    )
    return y, low


def outer(pairs, low, high, after=()):
    width = pairs[0][1].shape[1]

    def body(*refs):
        out = refs[-1]
        total = None
        for i in range(len(pairs)):
            term = mm_tn(refs[2 * i][:, low:high], refs[2 * i + 1][...])
            total = term if total is None else total + term
        out[...] = total.astype(BF16)

    return run(
        body,
        [((high - low, width), BF16)],
        [array for pair in pairs for array in pair],
        flops=2 * (high - low) * width * sum(pair[0].shape[0] for pair in pairs),
        limit=16,
        after=after,
    )[0]


def add(left, right, after=()):
    def body(left_ref, right_ref, out):
        out[...] = (left_ref[...].astype(F32) + right_ref[...].astype(F32)).astype(BF16)

    return run(body, [(left.shape, BF16)], (left, right), flops=left.size, after=after)[0]


def hold(arrays, after):
    count = len(arrays)
    anywhere = pl.BlockSpec(memory_space=pl.ANY)
    return pl.pallas_call(
        lambda *refs: None,
        out_shape=[jax.ShapeDtypeStruct(a.shape, a.dtype) for a in arrays],
        in_specs=[anywhere] * (count + len(after)),
        out_specs=[anywhere] * count,
        input_output_aliases={i: i for i in range(count)},
    )(*arrays, *after)


def core_swap(value):
    size = lax.axis_size("tensor")
    return lax.ppermute(value, "tensor", [(i, i ^ 1) for i in range(size)])


def chip_shift(value, shift):
    size = lax.axis_size("tensor")
    return lax.ppermute(value, "tensor", [(i, (i + 2 * shift) % size) for i in range(size)])


def share_half(half, chips):
    return [chip_shift(half, s) for s in range(1, chips)]


def spread_block(block, chips):
    mine = [block] + [chip_shift(block, chips - p) for p in range(1, chips)]
    return mine, [core_swap(b) for b in mine]


def hand_over(block, step, chips):
    pieces = [spread_block(to_section(piece, step), chips) for piece in block]
    return [[piece[i][p] for p in range(chips) for piece in pieces] for i in (0, 1)]


def pieces_of(rows):
    return 2 if rows % 32 == 0 and rows >= 128 else 1


def sum_blocks(mine, other, chips):
    rows = mine.shape[0] // chips

    def body(mine_ref, other_ref, own_ref, *sends):
        own_ref[...] = mine_ref[0:rows, :] + other_ref[0:rows, :].astype(F32)
        for p, ref in enumerate(sends, 1):
            here = slice(p * rows, (p + 1) * rows)
            ref[...] = (mine_ref[here, :] + other_ref[here, :].astype(F32)).astype(BF16)

    shape = (rows, mine.shape[1])
    own, *sends = run(body, [(shape, F32)] + [(shape, BF16)] * (chips - 1), (mine, other))
    return (own, *sends), [chip_shift(send, p) for p, send in enumerate(sends, 1)]


def to_section(value, step):
    pairs = [(0, 1)] if step > 0 else [(1, 0)]
    return lax.ppermute(value, "section", pairs)


class Turns:
    def __init__(self):
        self.last = ()

    def take(self):
        return self.last

    def end(self, *arrays):
        self.last = tuple(arrays)


def forward(source, w, info, chips, rows, save, turns):
    xm, normed, q, k, v = project(
        info, source, w["gain"][0], w["bias"][0], w["wq"], w["bq"], w["wk"], w["wv"], w["bv"],
        rows, turns.take(),
    )
    half = rows // 2
    z_other, o_other, l_other = attend(half, q, k, v, w["wout"], BF16)
    z_other = core_swap(z_other)
    z_mine, o_mine, l_mine = attend(0, q, k, v, w["wout"], F32)
    own = add(z_mine, z_other)
    turns.end(own)
    arrived = share_half(own, chips)
    yield
    hidden, n2m = middle(
        xm, own, arrived, w["out_bias"][0], w["gain"][1], w["bias"][1], turns.take()
    )
    n2o = core_swap(n2m)
    mine = mlp(n2m, w["w_up"], w["b_up"], w["w_down"], F32, save)
    other = mlp(n2o, w["w_up"], w["b_up"], w["w_down"], BF16, save)
    y_other = core_swap(other[0])
    total, arrived = sum_blocks(mine[0], y_other, chips)
    saved = None
    if save:
        saved = dict(
            x=xm, normed=normed, q=q, k=k, v=v, o=(o_mine, o_other), l=(l_mine, l_other),
            h=hidden, n2=(n2m, n2o), m=(mine[1], other[1]), slope=(mine[2], other[2]),
        )
        turns.end(mine[2], other[2])
        result, _ = finish_rows(hidden, total, arrived, w["out_bias"][1])
        return result, saved
    turns.end(*total)
    yield
    _, low = finish_rows(hidden, total, arrived, w["out_bias"][1], turns.take())
    turns.end(low[0])
    return low


def backward(source, saved, w, chips, turns):
    go, z_other, du_other = mlp_back(
        1, source, saved["slope"][1], w["w_up"], w["w_down"], BF16, turns.take()
    )
    z_other = core_swap(z_other)
    gm, z_mine, du_mine = mlp_back(0, source, saved["slope"][0], w["w_up"], w["w_down"], F32)
    own = add(z_mine, z_other)
    turns.end(own)
    arrived = share_half(own, chips)
    work = dict(g=(gm, go), du=(du_mine, du_other))
    yield work
    dh, dhm, sums_two = middle_back(
        gm, saved["h"], own, arrived, w["gain"][1], turns.take()
    )
    dho = core_swap(dhm)
    q, k, v = saved["q"], saved["k"], saved["v"]
    dq, dk, dv = attend_back(dhm, dho, w["wout"], q, k, v, *saved["l"])
    half = gm.shape[0]
    d_other = core_swap(project_back(half, dq, dk, dv, w["wq"], w["wk"], w["wv"], BF16))
    d_mine = project_back(0, dq, dk, dv, w["wq"], w["wk"], w["wv"], F32)
    total, arrived = sum_blocks(d_mine, d_other, chips)
    turns.end(*total)
    work.update(dh=(dhm, dho), dq=dq, dk=dk, dv=dv)
    yield work
    dx, low, sums_one = start_back(saved["x"], dh, total[0], arrived, w["gain"][0], turns.take())
    turns.end(low[0])
    work.update(sums=(sums_one, sums_two))
    return dx, low, work


def step_all(steps):
    results = [None] * len(steps)
    live = list(range(len(steps)))
    rounds = []
    while live:
        given = {}
        for i in list(live):
            try:
                given[i] = next(steps[i])
            except StopIteration as end:
                results[i] = end.value
                live.remove(i)
        rounds.append(given)
        yield results if not live else given


def finish(value):
    rows, width = value.shape
    step = 128

    def body(value_ref, out_ref):
        out_ref[...] = value_ref[...].astype(F32).reshape(step, 1, width)

    return pl.pallas_call(
        body,
        out_shape=jax.ShapeDtypeStruct((rows, 1, width), F32),
        grid=(pl.cdiv(rows, step),),
        in_specs=[pl.BlockSpec((step, width), lambda i: (i, 0))],
        out_specs=pl.BlockSpec((step, 1, width), lambda i: (i, 0, 0)),
        compiler_params=pltpu.CompilerParams(vmem_limit_bytes=8 * 2**20),
    )(value)


def dp_sum(pieces):
    if lax.axis_size("dp") == 4:
        return line_sum(pieces)
    return [lax.psum(piece, "dp") for piece in pieces]


def per_device(inputs, norm_gain, norm_bias, w_query, b_query, w_key, w_value, b_value, w_out,
               out_bias, w_up, b_up, w_down):
    first = lax.axis_index("section") == 0
    flag = first.astype(jnp.int32)[None]
    me = lax.axis_index("tensor")
    size = lax.axis_size("tensor")
    chips = size // 2
    chip, core = me // 2, me % 2
    _, micro, images, length, cols = inputs.shape
    unit = 16 * size
    total = -(-length // unit) * unit
    rows = total // size
    pad = total - length
    places = jnp.arange(size)
    order = ((chip + places % chips) % chips) * 2 + (core + places // chips) % 2
    order = order.astype(jnp.int32)
    rel = ((places // 2 - chip) % chips + chips * ((places + core) % 2)).astype(jnp.int32)
    info = jnp.stack([rel[size - 1] * rows + rows - pad, jnp.int32(pad)])
    images_all = micro * images
    sources = order
    small = jnp.concatenate(
        [norm_gain[0], norm_bias[0], out_bias[0], jnp.zeros((2, cols), F32)], axis=0
    )
    high = lax.reduce_precision(small, 8, 7)
    middle_part = lax.reduce_precision(small - high, 8, 7)
    thirds = jnp.concatenate([high, middle_part, small - high - middle_part], axis=0)
    features = inputs[0].reshape(images_all, length, cols).transpose(0, 2, 1)
    full = []
    for n in range(images_all):
        block = features[n]
        if n == 0:
            block = jnp.pad(block, ((0, 0), (0, pad)))
            block = jnp.concatenate([block, thirds.astype(BF16).T], axis=1)
        mine, other = spread_block(block, chips)
        halves, extras = assemble(
            mine + other, length, sources, order, rows, 0 if n else small.shape[0]
        )
        full.append(halves)
        if n == 0:
            small = extras[0]
    w = dict(
        gain=(small[0:1], small[1:2]), bias=(small[2:3], small[3:4]),
        out_bias=(small[4:5], small[5:6]),
        wq=w_query[0].T, bq=b_query, wk=w_key[0].T, wv=w_value[0].T, bv=b_value,
        wout=w_out[0], w_up=w_up[0].T, b_up=b_up, w_down=w_down[0],
    )
    span = range(images_all)
    turns = Turns()

    def widen(block, step, base, chosen):
        return Source(base, hand_over(block, step, chips), chosen)

    *_, lows = step_all(
        [forward(Source(full[n]), w, info, chips, total, False, turns) for n in span]
    )
    streams = [widen(lows[n], 1, full[n], flag) for n in span]
    *_, done = step_all([forward(streams[n], w, info, chips, total, True, turns) for n in span])
    results, saves = [d[0] for d in done], [d[1] for d in done]
    *_, done = step_all([backward(Source(full[n]), saves[n], w, chips, turns) for n in span])
    grads = [widen(done[n][1], -1, full[n], 1 - flag) for n in span]

    steps = step_all([backward(grads[n], saves[n], w, chips, turns) for n in span])
    works = next(steps)
    hidden = w_up.shape[2]
    both = (0, 1)
    g_down = outer([(saves[n]["m"][i], works[n]["g"][i]) for n in span for i in both], 0, hidden)
    g_up = outer(
        [(works[n]["du"][i], saves[n]["n2"][i]) for n in span for i in both], 0, hidden,
        (g_down,),
    )
    turns.end(g_down, g_up)
    g_down, g_up = lax.psum([g_down, g_up], "dp")
    works = next(steps)
    width = cols * size
    heads = b_query.shape[1]
    rest = [outer([(saves[n]["o"][i], works[n]["dh"][i]) for n in span for i in both], 0, heads)]
    for left in ("dq", "dk", "dv"):
        rest.append(outer([(works[n][left], saves[n]["normed"]) for n in span], 0, heads))
    done = next(steps)
    works = [d[2] for d in done]
    ends = [jnp.where(first, done[n][0], results[n]) for n in span]

    def total_of(parts):
        return sum(jnp.sum(p.astype(F32), 0) for p in parts)

    wide = sum(
        jnp.stack(
            [
                works[n]["sums"][0][0], works[n]["sums"][1][0],
                works[n]["sums"][0][1], works[n]["sums"][1][1],
                works[n]["sums"][1][3], works[n]["sums"][1][2],
            ]
        )
        for n in span
    )
    wide = lax.psum(wide, "tensor")
    wide = lax.dynamic_slice_in_dim(wide, me * cols, cols, 1)
    vector = jnp.concatenate(
        [
            wide.reshape(-1),
            total_of([works[n]["dq"] for n in span]),
            total_of([works[n]["dv"] for n in span]),
            total_of([works[n]["du"][i] for n in span for i in both]),
        ]
    )
    count = vector.size
    lines = -(-count // (16 * width)) * 16
    vector = jnp.pad(vector, (0, lines * width - count)).reshape(lines, width).astype(BF16)
    g_out, g_query, g_key, g_value, vector = lax.psum(hold([*rest, vector], (g_down,)), "dp")
    vector = vector.astype(F32).reshape(-1)
    wide = vector[: 6 * cols].reshape(6, cols)
    narrow = vector[6 * cols : count]

    ends = jnp.stack(ends).reshape(images_all, rows, size, cols)
    ends = lax.all_to_all(ends, "tensor", split_axis=2, concat_axis=1, tiled=True)
    ends = ends.reshape(images_all, total, cols)[:, :length]
    ends = ends.reshape(1, micro, images, length, cols)
    return (
        ends, wide[None, 0:2], wide[None, 2:4], g_query.T[None].astype(F32), narrow[None, :heads], g_key.T[None].astype(F32),
        g_value.T[None].astype(F32), narrow[None, heads : 2 * heads], g_out[None].astype(F32), wide[None, 4:6],
        finish(g_up).transpose(1, 2, 0),
        narrow[None, 2 * heads :], finish(g_down).transpose(1, 0, 2),
    )


def solution(mesh):
    columns = P("section", None, "tensor")
    vector = P("section", "tensor")
    stacked = P("section", "tensor", None)
    tokens = P("section", None, "dp", None, "tensor")
    weights = (columns, columns, columns, vector, columns, columns, vector, stacked, columns,
               columns, vector, stacked)
    return jax.shard_map(
        per_device, mesh=mesh, in_specs=(tokens, *weights), out_specs=(tokens, *weights),
        check_vma=False,
    )
```

```python
import functools

import jax
import jax.numpy as jnp
from jax import lax
from jax.experimental import pallas as pl
from jax.experimental.pallas import tpu as pltpu
from jax.sharding import PartitionSpec as P

HD = 72
LANES = 128
EPS = 1e-06
SCALE = HD**-0.5
LOG2E = 1.4426950408889634
FAR = -1e30
LIMIT = 6
COST = 14
STEP = 48
GELU_A = 0.7978845608028654
GELU_B = 0.044715
F32 = jnp.float32
BF16 = jnp.bfloat16
VMEM = pl.BlockSpec(memory_space=pltpu.VMEM)
SMEM = pl.BlockSpec(memory_space=pltpu.SMEM)


def run(body, outs, args, scalars=0, flops=0, scratch=(), limit=LIMIT, after=(), near=()):
    bytes_accessed = sum(a.size * a.dtype.itemsize for a in args) + sum(
        jnp.dtype(dtype).itemsize * shape[0] * shape[1] for shape, dtype in outs
    )
    count, extra = len(args), len(near) + len(after)

    def kernel(*refs):
        body(*refs[:count], *refs[count + extra :])

    return pl.pallas_call(
        kernel,
        out_shape=[jax.ShapeDtypeStruct(shape, dtype) for shape, dtype in outs],
        in_specs=[SMEM] * scalars
        + [VMEM] * (count - scalars)
        + [VMEM] * len(near)
        + [pl.BlockSpec(memory_space=pl.ANY)] * len(after),
        out_specs=[VMEM] * len(outs),
        scratch_shapes=list(scratch),
        compiler_params=pltpu.CompilerParams(vmem_limit_bytes=limit * 2**20),
        cost_estimate=pl.CostEstimate(
            flops=int(flops) * COST, bytes_accessed=int(bytes_accessed), transcendentals=0
        ),
    )(*args, *near, *after)


def mm(left, right):
    return jnp.dot(left, right, preferred_element_type=F32)


def mm_nt(left, right):
    return lax.dot_general(left, right, (((1,), (1,)), ((), ())), preferred_element_type=F32)


def mm_tn(left, right):
    return lax.dot_general(left, right, (((0,), (0,)), ((), ())), preferred_element_type=F32)


def unit_rows(x):
    center = x - jnp.mean(x, 1, keepdims=True)
    inverse = lax.rsqrt(jnp.mean(center * center, 1, keepdims=True) + EPS)
    return center * inverse, inverse


def assemble(parts, length, sources, order, rows, extra, after=()):
    count = len(parts)
    cols = parts[0].shape[0]
    half, total, width = count // 2, rows * count, cols * count

    def body(*refs):
        src_ref, order_ref = refs[:2]
        part_refs = refs[2 : 2 + count]
        mine_ref, other_ref, *small_out, wide_ref, tall_ref = refs[2 + count :]
        edge = length // LANES * LANES
        wide_ref[:, edge:] = jnp.zeros((width, wide_ref.shape[1] - edge), BF16)
        for i in range(count):
            start = pl.multiple_of(src_ref[i] * cols, 16)
            wide_ref[pl.ds(start, cols), 0 : parts[i].shape[1]] = part_refs[i][...]
        tall_ref[...] = wide_ref[...].T
        if extra:
            behind = tall_ref[total : total + 3 * extra, :].astype(F32)
            small_out[0][...] = (
                behind[0:extra] + behind[extra : 2 * extra] + behind[2 * extra :]
            )
            tall_ref[total : total + LANES, :] = jnp.zeros((LANES, width), BF16)
        for place in range(count):
            start = pl.multiple_of(order_ref[place] * rows, 16)
            out = mine_ref if place < half else other_ref
            at = (place % half) * rows
            out[at : at + rows, :] = tall_ref[pl.ds(start, rows), :]

    shape = ((half * rows, width), BF16)
    deep = total + (LANES if extra else 0)
    mine, other, *small = run(
        body,
        [shape, shape] + ([((extra, width), F32)] if extra else []),
        (sources, order, *parts),
        scalars=2,
        scratch=(pltpu.VMEM((width, deep), BF16), pltpu.VMEM((deep, width), BF16)),
        limit=10,
        after=after,
    )
    return (mine, other), small


class Source:
    def __init__(self, halves=None, blocks=None, flag=None):
        self.halves, self.blocks, self.flag = halves, blocks, flag

    def operands(self, which):
        scalars = [] if self.flag is None else [self.flag]
        arrays = []
        for i in which:
            arrays += [] if self.halves is None else [self.halves[i]]
            arrays += [] if self.blocks is None else self.blocks[i]
        return scalars, arrays

    def reader(self, which, scalar_refs, refs):
        refs, table = list(refs), {}
        for i in which:
            base = None if self.halves is None else refs.pop(0)
            count = 0 if self.blocks is None else len(self.blocks[i])
            table[i] = (base, [refs.pop(0) for _ in range(count)])

        def read(i, start, rows):
            base, blocks = table[i]
            value = None
            if blocks:
                size = blocks[0].shape[0]
                value = blocks[start // size][start % size : start % size + rows, :]
            if base is not None:
                at_hand = base[start : start + rows, :]
                if value is None:
                    return at_hand
                value = jnp.where(scalar_refs[0][0] != 0, at_hand, value)
            return value

        return read


def collect(source, rows, width):
    half = rows // 2
    scalars, arrays = source.operands((0, 1))

    def body(*refs):
        read = source.reader((0, 1), refs[: len(scalars)], refs[len(scalars) : -2])
        for i, out in enumerate(refs[-2:]):
            for at in range(0, half, STEP):
                out[at : at + STEP, :] = read(i, at, STEP)

    shape = ((half, width), BF16)
    return run(body, [shape, shape], (*scalars, *arrays), scalars=len(scalars), flops=rows * width)


def project(info, source, gain, bias, wq, bq, wk, wv, bv, rows, after=()):
    cols, width = wq.shape
    heads = cols // HD
    scalars, arrays = source.operands((0, 1))
    count, total = len(arrays), rows
    half = total // 2
    step = STEP

    def body(*refs):
        info_ref, flags = refs[0], refs[1 : 1 + len(scalars)]
        refs = refs[1 + len(scalars) :]
        read = source.reader((0, 1), flags, refs[:count])
        (g_ref, b_ref, wq_ref, bq_ref, wk_ref, wv_ref, bv_ref,
         x_ref, n_ref, q_ref, k_ref, v_ref) = refs[count:]
        for index in (0, 1):
            for at in range(0, half, step):
                value = read(index, at, step)
                if index == 0:
                    x_ref[at : at + step, :] = value
                unit, _ = unit_rows(value.astype(F32))
                n_ref[index * half + at : index * half + at + step, :] = (
                    unit * g_ref[...] + b_ref[...]
                ).astype(BF16)
        normed = n_ref[...]
        row = lax.broadcasted_iota(jnp.int32, (total, LANES - HD), 0)
        lane = lax.broadcasted_iota(jnp.int32, (total, LANES - HD), 1)
        pad_start = info_ref[0]
        padded = (row >= pad_start) & (row < pad_start + info_ref[1])
        ones = jnp.where(lane == 0, 1.0, 0.0).astype(BF16)
        mask = jnp.where((lane == 0) & padded, FAR, 0.0).astype(BF16)

        def spread(value, out, extra):
            for h in range(heads):
                out[:, h * LANES : (h + 1) * LANES] = jnp.concatenate(
                    [value[:, h * HD : (h + 1) * HD], extra], axis=1
                )

        spread((mm_nt(normed, wq_ref[...]) + bq_ref[...]).astype(BF16), q_ref, ones)
        spread(mm_nt(normed, wk_ref[...]).astype(BF16), k_ref, mask)
        spread((mm_nt(normed, wv_ref[...]) + bv_ref[...]).astype(BF16), v_ref, ones)

    wide = ((total, heads * LANES), BF16)
    return run(
        body,
        [((half, width), BF16), ((total, width), BF16), wide, wide, wide],
        (info, *scalars, *arrays, gain, bias, wq, bq, wk, wv, bv),
        scalars=1 + len(scalars),
        flops=6 * total * width * cols,
        after=after,
    )


def attend(first_row, q, k, v, wout, out_type):
    total, wide = q.shape
    heads = wide // LANES
    half = total // 2
    step = half // 2

    def body(q_ref, k_ref, v_ref, w_ref, z_ref, o_ref, l_ref):
        for at in range(0, half, step):
            outs, logs = [], []
            for h in range(heads):
                lanes = slice(h * LANES, (h + 1) * LANES)
                scores = mm_nt(q_ref[first_row + at : first_row + at + step, lanes], k_ref[:, lanes])
                highest = jnp.max(scores, 1, keepdims=True)
                weights = jnp.exp2((scores - highest) * (SCALE * LOG2E)).astype(BF16)
                mixed = mm(weights, v_ref[:, lanes])
                sums = mixed[:, HD : HD + 1]
                outs.append((mixed / sums).astype(BF16)[:, :HD])
                logs.append(highest * (SCALE * LOG2E) + jnp.log(sums) * LOG2E)
            mixed = jnp.concatenate(outs, axis=1)
            o_ref[at : at + step, :] = mixed
            z_ref[at : at + step, :] = mm(mixed, w_ref[...]).astype(out_type)
            logs = jnp.concatenate(logs + [jnp.zeros((step, LANES - heads), F32)], axis=1)
            l_ref[:, at : at + step] = logs.T[:8, :]

    return run(
        body,
        [((half, wout.shape[1]), out_type), ((half, heads * HD), BF16), ((8, half), F32)],
        (q, k, v, wout),
        flops=4 * half * total * LANES * heads + 2 * half * heads * HD * wout.shape[1],
    )


def middle(xm, own, arrived, out_bias, gain, bias, after=()):
    half, width = xm.shape
    parts = len(arrived) + 1
    rows = half // parts

    def body(x_ref, own_ref, *refs):
        got = refs[: parts - 1]
        ob_ref, g_ref, b_ref, h_ref, n_ref = refs[parts - 1 :]
        def step(i, carry):
            at = pl.multiple_of(i * STEP, 16)
            here = pl.ds(at, STEP)
            value = x_ref[here, :].astype(F32) + ob_ref[...]
            total = own_ref[here, :].astype(F32)
            for shift, ref in enumerate(got, 1):
                there = pl.multiple_of(lax.rem(at + shift * rows, half), 16)
                total = total + ref[pl.ds(there, STEP), :].astype(F32)
            value = value + total
            h_ref[here, :] = value
            unit, _ = unit_rows(value)
            n_ref[here, :] = (unit * g_ref[...] + b_ref[...]).astype(BF16)
            return carry

        lax.fori_loop(0, half // STEP, step, 0)

    return run(
        body,
        [((half, width), F32), ((half, width), BF16)],
        (xm, own, *arrived, out_bias, gain, bias),
        flops=20 * half * width,
        after=after,
    )


def mlp(n2, w_up, b_up, w_down, out_type, save):
    half, width = n2.shape
    hidden = w_up.shape[0]
    step = half // 2

    def body(n_ref, wu_ref, bu_ref, wd_ref, z_ref, *saved):
        for at in range(0, half, step):
            here = slice(at, at + step)
            u = mm_nt(n_ref[here, :], wu_ref[...]) + bu_ref[...]
            square = u * u
            t = jnp.tanh(GELU_A * u * (1.0 + GELU_B * square))
            low = 0.5 * (1.0 + t)
            active = (u * low).astype(BF16)
            if save:
                slope = low + (0.5 * GELU_A) * u * (1.0 - t * t) * (1.0 + (3 * GELU_B) * square)
                saved[0][here, :] = active
                saved[1][here, :] = slope.astype(BF16)
            z_ref[here, :] = mm(active, wd_ref[...]).astype(out_type)

    outs = [((half, width), out_type)]
    if save:
        outs += [((half, hidden), BF16)] * 2
    return run(body, outs, (n2, w_up, b_up, w_down), flops=4 * half * width * hidden)


def mlp_back(which, source, slope, w_up, w_down, out_type, after=()):
    half, hidden = slope.shape
    width = w_up.shape[1]
    scalars, arrays = source.operands((which,))
    count = len(arrays)
    step = half // 2 if source.blocks is None else source.blocks[0][0].shape[0]

    def body(*refs):
        read = source.reader((which,), refs[: len(scalars)], refs[len(scalars) :][:count])
        s_ref, wu_ref, wd_ref, g_ref, z_ref, d_ref = refs[len(scalars) + count :]
        for at in range(0, half, step):
            g_ref[at : at + step, :] = read(which, at, step)
        for at in range(0, half, half // 2):
            here = slice(at, at + half // 2)
            grad = mm_nt(g_ref[here, :], wd_ref[...]) * s_ref[here, :].astype(F32)
            grad = grad.astype(BF16)
            d_ref[here, :] = grad
            z_ref[here, :] = mm(grad, wu_ref[...]).astype(out_type)

    return run(
        body,
        [((half, width), BF16), ((half, width), out_type), ((half, hidden), BF16)],
        (*scalars, *arrays, slope, w_up, w_down),
        scalars=len(scalars),
        flops=4 * half * width * hidden,
        after=after,
    )


def middle_back(g, h, own, arrived, gain, after=()):
    half, width = g.shape
    parts = len(arrived) + 1
    rows = half // parts

    def body(g_ref, h_ref, own_ref, *refs):
        got = refs[: parts - 1]
        gain_ref, d_ref, low_ref, sums_ref = refs[parts - 1 :]
        def step(i, sums):
            at = pl.multiple_of(i * STEP, 16)
            here = pl.ds(at, STEP)
            grad = own_ref[here, :].astype(F32)
            for shift, ref in enumerate(got, 1):
                there = pl.multiple_of(lax.rem(at + shift * rows, half), 16)
                grad = grad + ref[pl.ds(there, STEP), :].astype(F32)
            unit, inverse = unit_rows(h_ref[here, :])
            scaled = grad * gain_ref[...]
            first = jnp.mean(scaled, 1, keepdims=True)
            second = jnp.mean(scaled * unit, 1, keepdims=True)
            upstream = g_ref[here, :].astype(F32)
            total = upstream + inverse * (scaled - first - unit * second)
            d_ref[here, :] = total
            low = total.astype(BF16)
            low_ref[here, :] = low
            terms = (grad * unit, grad, upstream, low.astype(F32))
            return tuple(a + jnp.sum(t, 0, keepdims=True) for a, t in zip(sums, terms))

        zeros = (jnp.zeros((1, width), F32),) * 4
        sums = lax.fori_loop(0, rows // STEP, step, zeros)
        lax.fori_loop(rows // STEP, half // STEP, lambda i, c: (step(i, zeros), c)[1], 0)
        for i in range(4):
            sums_ref[i : i + 1, :] = sums[i]

    return run(
        body,
        [((half, width), F32), ((half, width), BF16), ((8, width), F32)],
        (g, h, own, *arrived, gain),
        flops=30 * half * width,
        after=after,
    )


def attend_back(dm, do, wout, q, k, v, lm, lo):
    half = dm.shape[0]
    total, wide = q.shape
    heads = wide // LANES
    step = total // 3

    def body(dm_ref, do_ref, w_ref, q_ref, k_ref, v_ref, lm_ref, lo_ref,
             dq_ref, dk_ref, dv_ref, up_ref, log_ref, p_ref, w_ref2):
        for index, ref in enumerate((dm_ref, do_ref)):
            here = slice(index * half, (index + 1) * half)
            grad = mm_nt(ref[...], w_ref[...]).astype(BF16)
            fill = jnp.zeros((half, LANES - HD), BF16)
            for h in range(heads):
                cols = slice(h * HD, (h + 1) * HD)
                up = jnp.concatenate([grad[:, cols], fill], axis=1)
                up_ref[here, h * LANES : (h + 1) * LANES] = up
        log_ref[0:8, 0:half] = lm_ref[...]
        log_ref[0:8, half:total] = lo_ref[...]
        dqs, dks, dvs = [], [], []
        for h in range(heads):
            lanes = slice(h * LANES, (h + 1) * LANES)
            up = up_ref[:, lanes]
            queries = q_ref[:, lanes]
            sums = jnp.zeros((1, total), F32)
            dv_h = []
            for at in range(0, total, step):
                here = slice(at, at + step)
                scores = mm_nt(k_ref[here, lanes], queries)
                probs = jnp.exp2(scores * (SCALE * LOG2E) - log_ref[h : h + 1, :])
                weighted = probs * mm_nt(v_ref[here, lanes], up)
                sums = sums + jnp.sum(weighted, 0, keepdims=True)
                p_ref[here, :] = probs
                w_ref2[here, :] = weighted
                dv_h.append(mm(probs.astype(BF16), up).astype(BF16)[:, :HD])
            dq_t = jnp.zeros((LANES, total), F32)
            dk_h = []
            for at in range(0, total, step):
                here = slice(at, at + step)
                dscores = (w_ref2[here, :] - p_ref[here, :] * sums).astype(BF16)
                dk_h.append((mm(dscores, queries) * SCALE).astype(BF16)[:, :HD])
                dq_t = dq_t + mm_tn(k_ref[here, lanes], dscores)
            dqs.append((dq_t * SCALE).T.astype(BF16)[:, :HD])
            dks.append(jnp.concatenate(dk_h, axis=0))
            dvs.append(jnp.concatenate(dv_h, axis=0))
        dq_ref[...] = jnp.concatenate(dqs, axis=1)
        dk_ref[...] = jnp.concatenate(dks, axis=1)
        dv_ref[...] = jnp.concatenate(dvs, axis=1)

    out = ((total, heads * HD), BF16)
    return run(
        body,
        [out, out, out],
        (dm, do, wout, q, k, v, lm, lo),
        flops=10 * total * total * LANES * heads + 2 * total * heads * HD * dm.shape[1],
        scratch=(
            pltpu.VMEM((total, wide), BF16),
            pltpu.VMEM((8, total), F32),
            pltpu.VMEM((total, total), F32),
            pltpu.VMEM((total, total), F32),
        ),
        limit=12,
    )


def project_back(first_row, dq, dk, dv, wq, wk, wv, out_type):
    total, cols = dq.shape
    half = total // 2
    width = wq.shape[1]

    def body(dq_ref, dk_ref, dv_ref, wq_ref, wk_ref, wv_ref, z_ref):
        here = slice(first_row, first_row + half)
        z_ref[...] = (
            mm(dq_ref[here, :], wq_ref[...])
            + mm(dk_ref[here, :], wk_ref[...])
            + mm(dv_ref[here, :], wv_ref[...])
        ).astype(out_type)

    return run(
        body, [((half, width), out_type)], (dq, dk, dv, wq, wk, wv), flops=6 * half * cols * width
    )[0]


def start_back(xm, dh, own, arrived, gain, after=()):
    rows, width = own.shape
    count = len(arrived)

    def body(x_ref, dh_ref, own_ref, *refs):
        got = refs[:count]
        gain_ref, d_ref, low_ref, sums_ref = refs[count:]
        def step(i, sums):
            here = pl.ds(pl.multiple_of(i * STEP, 16), STEP)
            grad = own_ref[here, :]
            for ref in got:
                grad = grad + ref[here, :].astype(F32)
            unit, inverse = unit_rows(x_ref[here, :].astype(F32))
            scaled = grad * gain_ref[...]
            first = jnp.mean(scaled, 1, keepdims=True)
            second = jnp.mean(scaled * unit, 1, keepdims=True)
            total = dh_ref[here, :] + inverse * (scaled - first - unit * second)
            d_ref[here, :] = total
            low_ref[here, :] = total.astype(BF16)
            return tuple(
                a + jnp.sum(t, 0, keepdims=True) for a, t in zip(sums, (grad * unit, grad))
            )

        sums = lax.fori_loop(0, rows // STEP, step, (jnp.zeros((1, width), F32),) * 2)
        for i in range(2):
            sums_ref[i : i + 1, :] = sums[i]

    return run(
        body,
        [((rows, width), F32), ((rows, width), BF16), ((8, width), F32)],
        (xm, dh, own, *arrived, gain),
        flops=30 * rows * width,
        after=after,
    )


def finish_rows(hidden, total, arrived, out_bias, after=()):
    rows, width = total[0].shape

    def body(h_ref, total_ref, *refs):
        bias_ref, y_ref, low_ref = refs[len(arrived) :]
        value = total_ref[...]
        for ref in refs[: len(arrived)]:
            value = value + ref[...].astype(F32)
        value = h_ref[0:rows, :] + value + bias_ref[...]
        y_ref[...] = value
        low_ref[...] = value.astype(BF16)

    return run(
        body,
        [((rows, width), F32), ((rows, width), BF16)],
        (hidden, total[0], *arrived, out_bias),
        flops=4 * rows * width,
        after=after,
    )


def outer(pairs, low, high, after=()):
    width = pairs[0][1].shape[1]

    def body(*refs):
        out = refs[-1]
        total = None
        for i in range(len(pairs)):
            term = mm_tn(refs[2 * i][:, low:high], refs[2 * i + 1][...])
            total = term if total is None else total + term
        out[...] = total.astype(BF16)

    return run(
        body,
        [((high - low, width), BF16)],
        [array for pair in pairs for array in pair],
        flops=2 * (high - low) * width * sum(pair[0].shape[0] for pair in pairs),
        limit=16,
        after=after,
    )[0]


def add(left, right, after=()):
    def body(left_ref, right_ref, out):
        out[...] = (left_ref[...].astype(F32) + right_ref[...].astype(F32)).astype(BF16)

    return run(body, [(left.shape, BF16)], (left, right), flops=left.size, after=after)[0]


def hold(arrays, after):
    count = len(arrays)
    anywhere = pl.BlockSpec(memory_space=pl.ANY)
    return pl.pallas_call(
        lambda *refs: None,
        out_shape=[jax.ShapeDtypeStruct(a.shape, a.dtype) for a in arrays],
        in_specs=[anywhere] * (count + len(after)),
        out_specs=[anywhere] * count,
        input_output_aliases={i: i for i in range(count)},
    )(*arrays, *after)


def core_swap(value):
    size = lax.axis_size("tensor")
    return lax.ppermute(value, "tensor", [(i, i ^ 1) for i in range(size)])


def chip_shift(value, shift):
    size = lax.axis_size("tensor")
    return lax.ppermute(value, "tensor", [(i, (i + 2 * shift) % size) for i in range(size)])


def share_half(half, chips):
    return [chip_shift(half, s) for s in range(1, chips)]


def spread_block(block, chips):
    mine = [block] + [chip_shift(block, chips - p) for p in range(1, chips)]
    return mine, [core_swap(b) for b in mine]


def hand_over(block, step, chips):
    size = lax.axis_size("tensor")
    source, target = (0, size) if step > 0 else (size, 0)
    mine = []
    for p in range(chips):
        pairs = [(source + (i + 2 * p) % size, target + i) for i in range(size)]
        mine.append(lax.ppermute(block, ("section", "tensor"), pairs))
    return [mine, [core_swap(b) for b in mine]]


def sum_blocks(mine, other, chips):
    rows = mine.shape[0] // chips

    def body(mine_ref, other_ref, own_ref, *sends):
        own_ref[...] = mine_ref[0:rows, :] + other_ref[0:rows, :].astype(F32)
        for p, ref in enumerate(sends, 1):
            here = slice(p * rows, (p + 1) * rows)
            ref[...] = (mine_ref[here, :] + other_ref[here, :].astype(F32)).astype(BF16)

    shape = (rows, mine.shape[1])
    own, *sends = run(body, [(shape, F32)] + [(shape, BF16)] * (chips - 1), (mine, other))
    return (own, *sends), [chip_shift(send, p) for p, send in enumerate(sends, 1)]


class Turns:
    def __init__(self):
        self.last, self.first = (), ()

    def take(self):
        return self.last

    def end(self, *arrays):
        self.last = tuple(arrays)


def forward(source, w, info, chips, rows, save, turns):
    source = source()
    xm, normed, q, k, v = project(
        info, source, w["gain"][0], w["bias"][0], w["wq"], w["bq"], w["wk"], w["wv"], w["bv"],
        rows, turns.take(),
    )
    turns.first = (q,)
    half = rows // 2
    z_other, o_other, l_other = attend(half, q, k, v, w["wout"], BF16)
    z_other = core_swap(z_other)
    z_mine, o_mine, l_mine = attend(0, q, k, v, w["wout"], F32)
    own = add(z_mine, z_other)
    turns.end(own)
    arrived = share_half(own, chips)
    yield
    hidden, n2m = middle(
        xm, own, arrived, w["out_bias"][0], w["gain"][1], w["bias"][1], turns.take()
    )
    n2o = core_swap(n2m)
    mine = mlp(n2m, w["w_up"], w["b_up"], w["w_down"], F32, save)
    other = mlp(n2o, w["w_up"], w["b_up"], w["w_down"], BF16, save)
    y_other = core_swap(other[0])
    total, arrived = sum_blocks(mine[0], y_other, chips)
    saved = None
    if save:
        saved = dict(
            x=xm, normed=normed, q=q, k=k, v=v, o=(o_mine, o_other), l=(l_mine, l_other),
            h=hidden, n2=(n2m, n2o), m=(mine[1], other[1]), slope=(mine[2], other[2]),
        )
        turns.end(mine[2], other[2])
        result, _ = finish_rows(hidden, total, arrived, w["out_bias"][1])
        return result, saved
    turns.end(*total)
    yield
    _, low = finish_rows(hidden, total, arrived, w["out_bias"][1], turns.take())
    turns.end(low)
    return hand_over(low, 1, chips)


def backward(source, saved, w, chips, turns, pass_on):
    source = source()
    go, z_other, du_other = mlp_back(
        1, source, saved["slope"][1], w["w_up"], w["w_down"], BF16, turns.take()
    )
    turns.first = (go,)
    z_other = core_swap(z_other)
    gm, z_mine, du_mine = mlp_back(0, source, saved["slope"][0], w["w_up"], w["w_down"], F32)
    own = add(z_mine, z_other)
    turns.end(own)
    arrived = share_half(own, chips)
    work = dict(g=(gm, go), du=(du_mine, du_other))
    yield work
    dh, dhm, sums_two = middle_back(
        gm, saved["h"], own, arrived, w["gain"][1], turns.take()
    )
    dho = core_swap(dhm)
    q, k, v = saved["q"], saved["k"], saved["v"]
    dq, dk, dv = attend_back(dhm, dho, w["wout"], q, k, v, *saved["l"])
    half = gm.shape[0]
    d_other = core_swap(project_back(half, dq, dk, dv, w["wq"], w["wk"], w["wv"], BF16))
    d_mine = project_back(0, dq, dk, dv, w["wq"], w["wk"], w["wv"], F32)
    total, arrived = sum_blocks(d_mine, d_other, chips)
    turns.end(*total)
    work.update(dh=(dhm, dho), dq=dq, dk=dk, dv=dv)
    yield work
    dx, low, sums_one = start_back(saved["x"], dh, total[0], arrived, w["gain"][0], turns.take())
    turns.end(low)
    work.update(sums=(sums_one, sums_two))
    return dx, hand_over(low, -1, chips) if pass_on else None, work


def step_all(steps):
    results = [None] * len(steps)
    live = list(range(len(steps)))
    rounds = []
    while live:
        given = {}
        for i in list(live):
            try:
                given[i] = next(steps[i])
            except StopIteration as end:
                results[i] = end.value
                live.remove(i)
        rounds.append(given)
        yield results if not live else given


def finish(value):
    rows, width = value.shape
    step = 128

    def body(value_ref, out_ref):
        out_ref[...] = value_ref[...].astype(F32).reshape(step, 1, width)

    return pl.pallas_call(
        body,
        out_shape=jax.ShapeDtypeStruct((rows, 1, width), F32),
        grid=(pl.cdiv(rows, step),),
        in_specs=[pl.BlockSpec((step, width), lambda i: (i, 0))],
        out_specs=pl.BlockSpec((step, 1, width), lambda i: (i, 0, 0)),
        compiler_params=pltpu.CompilerParams(vmem_limit_bytes=8 * 2**20),
    )(value)


def dp_sum(pieces):
    if lax.axis_size("dp") == 4:
        return line_sum(pieces)
    return [lax.psum(piece, "dp") for piece in pieces]


def per_device(inputs, norm_gain, norm_bias, w_query, b_query, w_key, w_value, b_value, w_out,
               out_bias, w_up, b_up, w_down):
    first = lax.axis_index("section") == 0
    flag = first.astype(jnp.int32)[None]
    me = lax.axis_index("tensor")
    size = lax.axis_size("tensor")
    chips = size // 2
    chip, core = me // 2, me % 2
    _, micro, images, length, cols = inputs.shape
    unit = 16 * size
    total = -(-length // unit) * unit
    rows = total // size
    pad = total - length
    places = jnp.arange(size)
    order = ((chip + places % chips) % chips) * 2 + (core + places // chips) % 2
    order = order.astype(jnp.int32)
    rel = ((places // 2 - chip) % chips + chips * ((places + core) % 2)).astype(jnp.int32)
    info = jnp.stack([rel[size - 1] * rows + rows - pad, jnp.int32(pad)])
    images_all = micro * images
    sources = order
    small = jnp.concatenate(
        [norm_gain[0], norm_bias[0], out_bias[0], jnp.zeros((2, cols), F32)], axis=0
    )
    high = lax.reduce_precision(small, 8, 7)
    middle_part = lax.reduce_precision(small - high, 8, 7)
    thirds = jnp.concatenate([high, middle_part, small - high - middle_part], axis=0)
    features = inputs[0].reshape(images_all, length, cols).transpose(0, 2, 1)
    spread = []
    for n in range(images_all):
        block = features[n]
        if n == 0:
            block = jnp.pad(block, ((0, 0), (0, pad)))
            block = jnp.concatenate([block, thirds.astype(BF16).T], axis=1)
        else:
            (block,) = hold([block], full[0][:1])
        mine, other = spread_block(block, chips)
        spread.append(mine + other)
        if n == 0:
            halves, (small,) = assemble(
                spread[0], length, sources, order, rows, small.shape[0]
            )
            full = {0: halves}
    turns = Turns()

    def whole(n):
        if n not in full:
            full[n], _ = assemble(spread[n], length, sources, order, rows, 0, turns.take())
        return Source(full[n])

    w = dict(
        gain=(small[0:1], small[1:2]), bias=(small[2:3], small[3:4]),
        out_bias=(small[4:5], small[5:6]),
        wq=w_query[0].T, bq=b_query, wk=w_key[0].T, wv=w_value[0].T, bv=b_value,
        wout=w_out[0], w_up=w_up[0].T, b_up=b_up, w_down=w_down[0],
    )
    span = range(images_all)

    def widen(n, blocks, chosen):
        return Source(full[n], blocks, chosen)

    *_, lows = step_all(
        [
            forward(functools.partial(whole, n), w, info, chips, total, False, turns)
            for n in span
        ]
    )
    *_, done = step_all(
        [
            forward(
                functools.partial(widen, n, lows[n], flag), w, info, chips, total, True, turns
            )
            for n in span
        ]
    )
    results, saves = [d[0] for d in done], [d[1] for d in done]
    *_, done = step_all(
        [backward(functools.partial(whole, n), saves[n], w, chips, turns, True) for n in span]
    )
    lows = [d[1] for d in done]
    grads = [collect(widen(n, lows[n], 1 - flag), total, cols * size) for n in span]
    both = (0, 1)
    hidden = w_up.shape[2]
    steps = [
        backward(functools.partial(Source, grads[n]), saves[n], w, chips, turns, False)
        for n in span
    ]
    next(steps[0])
    g_down = outer(
        [(saves[n]["m"][i], grads[n][i]) for n in span for i in both], 0, hidden, turns.take()
    )
    turns.end(g_down)
    g_down = lax.psum(g_down, "dp")
    for step in steps[1:]:
        next(step)
    steps = step_all(steps)
    works = next(steps)
    width = cols * size
    heads = b_query.shape[1]
    g_up = outer(
        [(works[n]["du"][i], saves[n]["n2"][i]) for n in span for i in both], 0, hidden,
        turns.take(),
    )
    rest = [outer([(saves[n]["o"][i], works[n]["dh"][i]) for n in span for i in both], 0, heads)]
    for left in ("dq", "dk", "dv"):
        rest.append(outer([(works[n][left], saves[n]["normed"]) for n in span], 0, heads))
    done = next(steps)
    works = [d[2] for d in done]
    ends = [jnp.where(first, done[n][0], results[n]) for n in span]

    def total_of(parts):
        return sum(jnp.sum(p.astype(F32), 0) for p in parts)

    wide = sum(
        jnp.stack(
            [
                works[n]["sums"][0][0], works[n]["sums"][1][0],
                works[n]["sums"][0][1], works[n]["sums"][1][1],
                works[n]["sums"][1][3], works[n]["sums"][1][2],
            ]
        )
        for n in span
    )
    wide = lax.psum(wide, "tensor")
    wide = lax.dynamic_slice_in_dim(wide, me * cols, cols, 1)
    vector = jnp.concatenate(
        [
            wide.reshape(-1),
            total_of([works[n]["dq"] for n in span]),
            total_of([works[n]["dv"] for n in span]),
            total_of([works[n]["du"][i] for n in span for i in both]),
        ]
    )
    count = vector.size
    lines = -(-count // (16 * width)) * 16
    vector = jnp.pad(vector, (0, lines * width - count)).reshape(lines, width).astype(BF16)
    rest = hold([g_up, *rest, vector], (g_down,))
    g_up, g_out, g_query, g_key, g_value, vector = lax.psum(rest, "dp")
    vector = vector.astype(F32).reshape(-1)
    wide = vector[: 6 * cols].reshape(6, cols)
    narrow = vector[6 * cols : count]

    ends = jnp.stack(ends).reshape(images_all, rows, size, cols)
    ends = lax.all_to_all(ends, "tensor", split_axis=2, concat_axis=1, tiled=True)
    ends = ends.reshape(images_all, total, cols)[:, :length]
    ends = ends.reshape(1, micro, images, length, cols)
    return (
        ends, wide[None, 0:2], wide[None, 2:4], g_query.T[None].astype(F32), narrow[None, :heads], g_key.T[None].astype(F32),
        g_value.T[None].astype(F32), narrow[None, heads : 2 * heads], g_out[None].astype(F32), wide[None, 4:6],
        finish(g_up).transpose(1, 2, 0),
        narrow[None, 2 * heads :], finish(g_down).transpose(1, 0, 2),
    )


def solution(mesh):
    columns = P("section", None, "tensor")
    vector = P("section", "tensor")
    stacked = P("section", "tensor", None)
    tokens = P("section", None, "dp", None, "tensor")
    weights = (columns, columns, columns, vector, columns, columns, vector, stacked, columns,
               columns, vector, stacked)
    return jax.shard_map(
        per_device, mesh=mesh, in_specs=(tokens, *weights), out_specs=(tokens, *weights),
        check_vma=False,
    )
```

```python
import functools

import jax
import jax.numpy as jnp
from jax import lax
from jax.experimental import pallas as pl
from jax.experimental.pallas import tpu as pltpu
from jax.sharding import PartitionSpec as P

HD = 72
LANES = 128
EPS = 1e-06
SCALE = HD**-0.5
LOG2E = 1.4426950408889634
FAR = -1e30
LIMIT = 6
COST = 14
STEP = 48
GELU_A = 0.7978845608028654
GELU_B = 0.044715
F32 = jnp.float32
BF16 = jnp.bfloat16
VMEM = pl.BlockSpec(memory_space=pltpu.VMEM)
SMEM = pl.BlockSpec(memory_space=pltpu.SMEM)


def run(body, outs, args, scalars=0, flops=0, scratch=(), limit=LIMIT, after=(), near=()):
    bytes_accessed = sum(a.size * a.dtype.itemsize for a in args) + sum(
        jnp.dtype(dtype).itemsize * shape[0] * shape[1] for shape, dtype in outs
    )
    count, extra = len(args), len(near) + len(after)

    def kernel(*refs):
        body(*refs[:count], *refs[count + extra :])

    return pl.pallas_call(
        kernel,
        out_shape=[jax.ShapeDtypeStruct(shape, dtype) for shape, dtype in outs],
        in_specs=[SMEM] * scalars
        + [VMEM] * (count - scalars)
        + [VMEM] * len(near)
        + [pl.BlockSpec(memory_space=pl.ANY)] * len(after),
        out_specs=[VMEM] * len(outs),
        scratch_shapes=list(scratch),
        compiler_params=pltpu.CompilerParams(vmem_limit_bytes=limit * 2**20),
        cost_estimate=pl.CostEstimate(
            flops=int(flops) * COST, bytes_accessed=int(bytes_accessed), transcendentals=0
        ),
    )(*args, *near, *after)


def mm(left, right):
    return jnp.dot(left, right, preferred_element_type=F32)


def mm_nt(left, right):
    return lax.dot_general(left, right, (((1,), (1,)), ((), ())), preferred_element_type=F32)


def mm_tn(left, right):
    return lax.dot_general(left, right, (((0,), (0,)), ((), ())), preferred_element_type=F32)


def unit_rows(x):
    center = x - jnp.mean(x, 1, keepdims=True)
    inverse = lax.rsqrt(jnp.mean(center * center, 1, keepdims=True) + EPS)
    return center * inverse, inverse


def assemble(parts, length, sources, order, rows, extra, after=(), near=()):
    count = len(parts)
    cols = parts[0].shape[0]
    half, total, width = count // 2, rows * count, cols * count

    def body(*refs):
        src_ref, order_ref = refs[:2]
        part_refs = refs[2 : 2 + count]
        mine_ref, other_ref, *small_out, wide_ref, tall_ref = refs[2 + count :]
        edge = length // LANES * LANES
        wide_ref[:, edge:] = jnp.zeros((width, wide_ref.shape[1] - edge), BF16)
        for i in range(count):
            start = pl.multiple_of(src_ref[i] * cols, 16)
            wide_ref[pl.ds(start, cols), 0 : parts[i].shape[1]] = part_refs[i][...]
        tall_ref[...] = wide_ref[...].T
        if extra:
            behind = tall_ref[total : total + 3 * extra, :].astype(F32)
            small_out[0][...] = (
                behind[0:extra] + behind[extra : 2 * extra] + behind[2 * extra :]
            )
            tall_ref[total : total + LANES, :] = jnp.zeros((LANES, width), BF16)
        for place in range(count):
            start = pl.multiple_of(order_ref[place] * rows, 16)
            out = mine_ref if place < half else other_ref
            at = (place % half) * rows
            out[at : at + rows, :] = tall_ref[pl.ds(start, rows), :]

    shape = ((half * rows, width), BF16)
    deep = total + (LANES if extra else 0)
    mine, other, *small = run(
        body,
        [shape, shape] + ([((extra, width), F32)] if extra else []),
        (sources, order, *parts),
        scalars=2,
        scratch=(pltpu.VMEM((width, deep), BF16), pltpu.VMEM((deep, width), BF16)),
        limit=10,
        after=after,
        near=near,
    )
    return (mine, other), small


class Source:
    def __init__(self, halves=None, blocks=None, flag=None):
        self.halves, self.blocks, self.flag = halves, blocks, flag

    def operands(self, which):
        scalars = [] if self.flag is None else [self.flag]
        arrays = []
        for i in which:
            arrays += [] if self.halves is None else [self.halves[i]]
            arrays += [] if self.blocks is None else self.blocks[i]
        return scalars, arrays

    def reader(self, which, scalar_refs, refs):
        refs, table = list(refs), {}
        for i in which:
            base = None if self.halves is None else refs.pop(0)
            count = 0 if self.blocks is None else len(self.blocks[i])
            table[i] = (base, [refs.pop(0) for _ in range(count)])

        def read(i, start, rows):
            base, blocks = table[i]
            value = None
            if blocks:
                size = blocks[0].shape[0]
                value = blocks[start // size][start % size : start % size + rows, :]
            if base is not None:
                at_hand = base[start : start + rows, :]
                if value is None:
                    return at_hand
                value = jnp.where(scalar_refs[0][0] != 0, at_hand, value)
            return value

        return read


def collect(source, rows, width):
    half = rows // 2
    scalars, arrays = source.operands((0, 1))

    def body(*refs):
        read = source.reader((0, 1), refs[: len(scalars)], refs[len(scalars) : -2])
        for i, out in enumerate(refs[-2:]):
            for at in range(0, half, STEP):
                out[at : at + STEP, :] = read(i, at, STEP)

    shape = ((half, width), BF16)
    return run(body, [shape, shape], (*scalars, *arrays), scalars=len(scalars), flops=rows * width)


def project(info, source, gain, bias, weight, shift, rows, after=()):
    cols, width = weight.shape[0] // 3, weight.shape[1]
    heads = cols // HD
    scalars, arrays = source.operands((0, 1))
    count, total = len(arrays), rows
    half = total // 2
    step = STEP

    def body(*refs):
        info_ref, flags = refs[0], refs[1 : 1 + len(scalars)]
        refs = refs[1 + len(scalars) :]
        read = source.reader((0, 1), flags, refs[:count])
        g_ref, b_ref, w_ref, s_ref, x_ref, n_ref, *outs = refs[count:]
        for index in (0, 1):
            for at in range(0, half, step):
                value = read(index, at, step)
                if index == 0:
                    x_ref[at : at + step, :] = value
                unit, _ = unit_rows(value.astype(F32))
                n_ref[index * half + at : index * half + at + step, :] = (
                    unit * g_ref[...] + b_ref[...]
                ).astype(BF16)
        row = lax.broadcasted_iota(jnp.int32, (total, LANES - HD), 0)
        lane = lax.broadcasted_iota(jnp.int32, (total, LANES - HD), 1)
        pad_start = info_ref[0]
        padded = (row >= pad_start) & (row < pad_start + info_ref[1])
        ones = jnp.where(lane == 0, 1.0, 0.0).astype(BF16)
        mask = jnp.where((lane == 0) & padded, FAR, 0.0).astype(BF16)
        normed = n_ref[...]
        for i, (out, extra) in enumerate(zip(outs, (ones, mask, ones))):
            here = slice(i * cols, (i + 1) * cols)
            value = (mm_nt(normed, w_ref[here, :]) + s_ref[:, here]).astype(BF16)
            for h in range(heads):
                out[:, h * LANES : (h + 1) * LANES] = jnp.concatenate(
                    [value[:, h * HD : (h + 1) * HD], extra], axis=1
                )

    wide = ((total, heads * LANES), BF16)
    return run(
        body,
        [((half, width), BF16), ((total, width), BF16), wide, wide, wide],
        (info, *scalars, *arrays, gain, bias, weight, shift),
        scalars=1 + len(scalars),
        flops=6 * total * width * cols,
        after=after,
    )


def attend(first_row, q, k, v, wout, out_type):
    total, wide = q.shape
    heads = wide // LANES
    half = total // 2
    step = half

    def body(q_ref, k_ref, v_ref, w_ref, z_ref, o_ref, l_ref):
        for at in range(0, half, step):
            outs, logs = [], []
            for h in range(heads):
                lanes = slice(h * LANES, (h + 1) * LANES)
                scores = mm_nt(q_ref[first_row + at : first_row + at + step, lanes], k_ref[:, lanes])
                highest = jnp.max(scores, 1, keepdims=True)
                weights = jnp.exp2((scores - highest) * (SCALE * LOG2E)).astype(BF16)
                mixed = mm(weights, v_ref[:, lanes])
                sums = mixed[:, HD : HD + 1]
                outs.append((mixed / sums).astype(BF16)[:, :HD])
                logs.append(highest * (SCALE * LOG2E) + jnp.log(sums) * LOG2E)
            mixed = jnp.concatenate(outs, axis=1)
            o_ref[at : at + step, :] = mixed
            z_ref[at : at + step, :] = mm(mixed, w_ref[...]).astype(out_type)
            logs = jnp.concatenate(logs + [jnp.zeros((step, LANES - heads), F32)], axis=1)
            l_ref[:, at : at + step] = logs.T[:8, :]

    return run(
        body,
        [((half, wout.shape[1]), out_type), ((half, heads * HD), BF16), ((8, half), F32)],
        (q, k, v, wout),
        flops=4 * half * total * LANES * heads + 2 * half * heads * HD * wout.shape[1],
    )


def middle(xm, own, arrived, out_bias, gain, bias, after=()):
    half, width = xm.shape
    parts = len(arrived) + 1
    rows = half // parts

    def body(x_ref, own_ref, *refs):
        got = refs[: parts - 1]
        ob_ref, g_ref, b_ref, h_ref, n_ref = refs[parts - 1 :]
        def step(i, carry):
            at = pl.multiple_of(i * STEP, 16)
            here = pl.ds(at, STEP)
            value = x_ref[here, :].astype(F32) + ob_ref[...]
            total = own_ref[here, :].astype(F32)
            for shift, ref in enumerate(got, 1):
                there = pl.multiple_of(lax.rem(at + shift * rows, half), 16)
                total = total + ref[pl.ds(there, STEP), :].astype(F32)
            value = value + total
            h_ref[here, :] = value
            unit, _ = unit_rows(value)
            n_ref[here, :] = (unit * g_ref[...] + b_ref[...]).astype(BF16)
            return carry

        lax.fori_loop(0, half // STEP, step, 0)

    return run(
        body,
        [((half, width), F32), ((half, width), BF16)],
        (xm, own, *arrived, out_bias, gain, bias),
        flops=20 * half * width,
        after=after,
    )


def mlp(n2, w_up, b_up, w_down, out_type, save):
    half, width = n2.shape
    hidden = w_up.shape[0]
    step = half

    def body(n_ref, wu_ref, bu_ref, wd_ref, z_ref, *saved):
        for at in range(0, half, step):
            here = slice(at, at + step)
            u = mm_nt(n_ref[here, :], wu_ref[...]) + bu_ref[...]
            square = u * u
            t = jnp.tanh(GELU_A * u * (1.0 + GELU_B * square))
            low = 0.5 * (1.0 + t)
            active = (u * low).astype(BF16)
            if save:
                slope = low + (0.5 * GELU_A) * u * (1.0 - t * t) * (1.0 + (3 * GELU_B) * square)
                saved[0][here, :] = active
                saved[1][here, :] = slope.astype(BF16)
            z_ref[here, :] = mm(active, wd_ref[...]).astype(out_type)

    outs = [((half, width), out_type)]
    if save:
        outs += [((half, hidden), BF16)] * 2
    return run(body, outs, (n2, w_up, b_up, w_down), flops=4 * half * width * hidden)


def mlp_back(which, source, slope, w_up, w_down, out_type, after=()):
    half, hidden = slope.shape
    width = w_up.shape[1]
    scalars, arrays = source.operands((which,))
    count = len(arrays)
    step = half // 2 if source.blocks is None else source.blocks[0][0].shape[0]

    def body(*refs):
        read = source.reader((which,), refs[: len(scalars)], refs[len(scalars) :][:count])
        s_ref, wu_ref, wd_ref, g_ref, z_ref, d_ref = refs[len(scalars) + count :]
        for at in range(0, half, step):
            g_ref[at : at + step, :] = read(which, at, step)
        grad = (mm_nt(g_ref[...], wd_ref[...]) * s_ref[...].astype(F32)).astype(BF16)
        d_ref[...] = grad
        z_ref[...] = mm(grad, wu_ref[...]).astype(out_type)

    return run(
        body,
        [((half, width), BF16), ((half, width), out_type), ((half, hidden), BF16)],
        (*scalars, *arrays, slope, w_up, w_down),
        scalars=len(scalars),
        flops=4 * half * width * hidden,
        after=after,
    )


def middle_back(g, h, own, arrived, gain, after=()):
    half, width = g.shape
    parts = len(arrived) + 1
    rows = half // parts

    def body(g_ref, h_ref, own_ref, *refs):
        got = refs[: parts - 1]
        gain_ref, d_ref, low_ref, sums_ref = refs[parts - 1 :]
        def step(i, sums):
            at = pl.multiple_of(i * STEP, 16)
            here = pl.ds(at, STEP)
            grad = own_ref[here, :].astype(F32)
            for shift, ref in enumerate(got, 1):
                there = pl.multiple_of(lax.rem(at + shift * rows, half), 16)
                grad = grad + ref[pl.ds(there, STEP), :].astype(F32)
            unit, inverse = unit_rows(h_ref[here, :])
            scaled = grad * gain_ref[...]
            first = jnp.mean(scaled, 1, keepdims=True)
            second = jnp.mean(scaled * unit, 1, keepdims=True)
            upstream = g_ref[here, :].astype(F32)
            total = upstream + inverse * (scaled - first - unit * second)
            d_ref[here, :] = total
            low = total.astype(BF16)
            low_ref[here, :] = low
            terms = (grad * unit, grad, upstream, low.astype(F32))
            return tuple(a + jnp.sum(t, 0, keepdims=True) for a, t in zip(sums, terms))

        zeros = (jnp.zeros((1, width), F32),) * 4
        sums = lax.fori_loop(0, rows // STEP, step, zeros)
        lax.fori_loop(rows // STEP, half // STEP, lambda i, c: (step(i, zeros), c)[1], 0)
        for i in range(4):
            sums_ref[i : i + 1, :] = sums[i]

    return run(
        body,
        [((half, width), F32), ((half, width), BF16), ((8, width), F32)],
        (g, h, own, *arrived, gain),
        flops=30 * half * width,
        after=after,
    )


def attend_back(dm, do, wout, q, k, v, lm, lo):
    half = dm.shape[0]
    total, wide = q.shape
    heads = wide // LANES
    step = total

    def body(dm_ref, do_ref, w_ref, q_ref, k_ref, v_ref, lm_ref, lo_ref,
             d_ref, up_ref, log_ref, p_ref, w_ref2):
        for index, ref in enumerate((dm_ref, do_ref)):
            here = slice(index * half, (index + 1) * half)
            grad = mm_nt(ref[...], w_ref[...]).astype(BF16)
            fill = jnp.zeros((half, LANES - HD), BF16)
            for h in range(heads):
                cols = slice(h * HD, (h + 1) * HD)
                up = jnp.concatenate([grad[:, cols], fill], axis=1)
                up_ref[here, h * LANES : (h + 1) * LANES] = up
        log_ref[0:8, 0:half] = lm_ref[...]
        log_ref[0:8, half:total] = lo_ref[...]
        dqs, dks, dvs = [], [], []
        for h in range(heads):
            lanes = slice(h * LANES, (h + 1) * LANES)
            up = up_ref[:, lanes]
            queries = q_ref[:, lanes]
            sums = jnp.zeros((1, total), F32)
            dv_h = []
            for at in range(0, total, step):
                here = slice(at, at + step)
                scores = mm_nt(k_ref[here, lanes], queries)
                probs = jnp.exp2(scores * (SCALE * LOG2E) - log_ref[h : h + 1, :])
                weighted = probs * mm_nt(v_ref[here, lanes], up)
                sums = sums + jnp.sum(weighted, 0, keepdims=True)
                p_ref[here, :] = probs
                w_ref2[here, :] = weighted
                dv_h.append(mm(probs.astype(BF16), up).astype(BF16)[:, :HD])
            dq_t = jnp.zeros((LANES, total), F32)
            dk_h = []
            for at in range(0, total, step):
                here = slice(at, at + step)
                dscores = (w_ref2[here, :] - p_ref[here, :] * sums).astype(BF16)
                dk_h.append((mm(dscores, queries) * SCALE).astype(BF16)[:, :HD])
                dq_t = dq_t + mm_tn(k_ref[here, lanes], dscores)
            dqs.append((dq_t * SCALE).T.astype(BF16)[:, :HD])
            dks.append(jnp.concatenate(dk_h, axis=0))
            dvs.append(jnp.concatenate(dv_h, axis=0))
        d_ref[...] = jnp.concatenate([*dqs, *dks, *dvs], axis=1)

    return run(
        body,
        [((total, 3 * heads * HD), BF16)],
        (dm, do, wout, q, k, v, lm, lo),
        flops=10 * total * total * LANES * heads + 2 * total * heads * HD * dm.shape[1],
        scratch=(
            pltpu.VMEM((total, wide), BF16),
            pltpu.VMEM((8, total), F32),
            pltpu.VMEM((total, total), F32),
            pltpu.VMEM((total, total), F32),
        ),
        limit=12,
    )[0]


def project_back(first_row, grad, weight, out_type):
    total = grad.shape[0]
    half = total // 2
    cols, width = weight.shape

    def body(d_ref, w_ref, z_ref):
        z_ref[...] = mm(d_ref[first_row : first_row + half, :], w_ref[...]).astype(out_type)

    return run(
        body, [((half, width), out_type)], (grad, weight), flops=2 * half * cols * width
    )[0]


def start_back(xm, dh, own, arrived, gain, after=()):
    rows, width = own.shape
    part = rows // pieces_of(rows)
    count = len(arrived)

    def body(x_ref, dh_ref, own_ref, *refs):
        got = refs[:count]
        gain_ref, d_ref, sums_ref, *low_refs = refs[count:]
        def step(i, sums):
            here = pl.ds(pl.multiple_of(i * STEP, 16), STEP)
            grad = own_ref[here, :]
            for ref in got:
                grad = grad + ref[here, :].astype(F32)
            unit, inverse = unit_rows(x_ref[here, :].astype(F32))
            scaled = grad * gain_ref[...]
            first = jnp.mean(scaled, 1, keepdims=True)
            second = jnp.mean(scaled * unit, 1, keepdims=True)
            total = dh_ref[here, :] + inverse * (scaled - first - unit * second)
            d_ref[here, :] = total
            return tuple(
                a + jnp.sum(t, 0, keepdims=True) for a, t in zip(sums, (grad * unit, grad))
            )

        sums = lax.fori_loop(0, rows // STEP, step, (jnp.zeros((1, width), F32),) * 2)
        for i in range(2):
            sums_ref[i : i + 1, :] = sums[i]
        for i, ref in enumerate(low_refs):
            ref[...] = d_ref[i * part : (i + 1) * part, :].astype(BF16)

    d, sums, *low = run(
        body,
        [((rows, width), F32), ((8, width), F32)]
        + [((part, width), BF16)] * (rows // part),
        (xm, dh, own, *arrived, gain),
        flops=30 * rows * width,
        after=after,
    )
    return d, low, sums


def finish_rows(hidden, total, arrived, out_bias, after=()):
    rows, width = total[0].shape
    part = rows // pieces_of(rows)

    def body(h_ref, total_ref, *refs):
        bias_ref, y_ref, *low_refs = refs[len(arrived) :]
        value = total_ref[...]
        for ref in refs[: len(arrived)]:
            value = value + ref[...].astype(F32)
        value = h_ref[0:rows, :] + value + bias_ref[...]
        y_ref[...] = value
        for i, ref in enumerate(low_refs):
            ref[...] = value[i * part : (i + 1) * part, :].astype(BF16)

    y, *low = run(
        body,
        [((rows, width), F32)] + [((part, width), BF16)] * (rows // part),
        (hidden, total[0], *arrived, out_bias),
        flops=4 * rows * width,
        after=after,
    )
    return y, low


def outer(pairs, low, high, after=()):
    width = pairs[0][1].shape[1]

    def body(*refs):
        out = refs[-1]
        total = None
        for i in range(len(pairs)):
            term = mm_tn(refs[2 * i][:, low:high], refs[2 * i + 1][...])
            total = term if total is None else total + term
        out[...] = total.astype(BF16)

    return run(
        body,
        [((high - low, width), BF16)],
        [array for pair in pairs for array in pair],
        flops=2 * (high - low) * width * sum(pair[0].shape[0] for pair in pairs),
        limit=16,
        after=after,
    )[0]


def add(left, right, after=()):
    def body(left_ref, right_ref, out):
        out[...] = (left_ref[...].astype(F32) + right_ref[...].astype(F32)).astype(BF16)

    return run(body, [(left.shape, BF16)], (left, right), flops=left.size, after=after)[0]


def hold(arrays, after):
    count = len(arrays)
    anywhere = pl.BlockSpec(memory_space=pl.ANY)
    return pl.pallas_call(
        lambda *refs: None,
        out_shape=[jax.ShapeDtypeStruct(a.shape, a.dtype) for a in arrays],
        in_specs=[anywhere] * (count + len(after)),
        out_specs=[anywhere] * count,
        input_output_aliases={i: i for i in range(count)},
    )(*arrays, *after)


def core_swap(value):
    size = lax.axis_size("tensor")
    return lax.ppermute(value, "tensor", [(i, i ^ 1) for i in range(size)])


def chip_shift(value, shift):
    size = lax.axis_size("tensor")
    return lax.ppermute(value, "tensor", [(i, (i + 2 * shift) % size) for i in range(size)])


def share_half(half, chips):
    return [chip_shift(half, s) for s in range(1, chips)]


def spread_block(block, chips):
    mine = [block] + [chip_shift(block, chips - p) for p in range(1, chips)]
    return mine, [core_swap(b) for b in mine]


def hand_over(pieces, chips, after=()):
    if after:
        pieces = hold(pieces, after)
    spread = [spread_block(piece, chips) for piece in pieces]
    return [[spread[j][i][p] for p in range(chips) for j in range(len(pieces))] for i in (0, 1)]


def pieces_of(rows):
    return 2 if rows % 32 == 0 and rows >= 128 else 1


def sum_blocks(mine, other, chips):
    rows = mine.shape[0] // chips

    def body(mine_ref, other_ref, own_ref, *sends):
        own_ref[...] = mine_ref[0:rows, :] + other_ref[0:rows, :].astype(F32)
        for p, ref in enumerate(sends, 1):
            here = slice(p * rows, (p + 1) * rows)
            ref[...] = (mine_ref[here, :] + other_ref[here, :].astype(F32)).astype(BF16)

    shape = (rows, mine.shape[1])
    own, *sends = run(body, [(shape, F32)] + [(shape, BF16)] * (chips - 1), (mine, other))
    return (own, *sends), [chip_shift(send, p) for p, send in enumerate(sends, 1)]


def to_section(value, step):
    pairs = [(0, 1)] if step > 0 else [(1, 0)]
    return lax.ppermute(value, "section", pairs)


class Turns:
    def __init__(self):
        self.last, self.first = (), ()

    def take(self):
        return self.last

    def end(self, *arrays):
        self.last = tuple(arrays)


def forward(source, w, info, chips, rows, save, turns):
    source = source()
    xm, normed, q, k, v = project(
        info, source, w["gain"][0], w["bias"][0], w["qkv"], w["qkv_shift"], rows, turns.take(),
    )
    turns.first = (q,)
    half = rows // 2
    z_other, o_other, l_other = attend(half, q, k, v, w["wout"], BF16)
    z_other = core_swap(z_other)
    z_mine, o_mine, l_mine = attend(0, q, k, v, w["wout"], F32)
    own = add(z_mine, z_other)
    turns.end(own)
    arrived = share_half(own, chips)
    yield
    hidden, n2m = middle(
        xm, own, arrived, w["out_bias"][0], w["gain"][1], w["bias"][1], turns.take()
    )
    n2o = core_swap(n2m)
    mine = mlp(n2m, w["w_up"], w["b_up"], w["w_down"], F32, save)
    other = mlp(n2o, w["w_up"], w["b_up"], w["w_down"], BF16, save)
    y_other = core_swap(other[0])
    total, arrived = sum_blocks(mine[0], y_other, chips)
    saved = None
    if save:
        saved = dict(
            x=xm, normed=normed, q=q, k=k, v=v, o=(o_mine, o_other), l=(l_mine, l_other),
            h=hidden, n2=(n2m, n2o), m=(mine[1], other[1]), slope=(mine[2], other[2]),
        )
        turns.end(mine[2], other[2])
        result, _ = finish_rows(hidden, total, arrived, w["out_bias"][1])
        return result, saved
    turns.end(*total)
    yield
    _, low = finish_rows(hidden, total, arrived, w["out_bias"][1], turns.take())
    turns.end(low[0])
    return [to_section(piece, 1) for piece in low]


def backward(source, saved, w, chips, turns, pass_on):
    source = source()
    go, z_other, du_other = mlp_back(
        1, source, saved["slope"][1], w["w_up"], w["w_down"], BF16, turns.take()
    )
    turns.first = (go,)
    z_other = core_swap(z_other)
    gm, z_mine, du_mine = mlp_back(0, source, saved["slope"][0], w["w_up"], w["w_down"], F32)
    own = add(z_mine, z_other)
    turns.end(own)
    arrived = share_half(own, chips)
    work = dict(g=(gm, go), du=(du_mine, du_other))
    yield work
    dh, dhm, sums_two = middle_back(
        gm, saved["h"], own, arrived, w["gain"][1], turns.take()
    )
    dho = core_swap(dhm)
    q, k, v = saved["q"], saved["k"], saved["v"]
    dqkv = attend_back(dhm, dho, w["wout"], q, k, v, *saved["l"])
    half = gm.shape[0]
    d_other = core_swap(project_back(half, dqkv, w["qkv"], BF16))
    d_mine = project_back(0, dqkv, w["qkv"], F32)
    total, arrived = sum_blocks(d_mine, d_other, chips)
    turns.end(*total)
    work.update(dh=(dhm, dho), dqkv=dqkv)
    yield work
    dx, low, sums_one = start_back(saved["x"], dh, total[0], arrived, w["gain"][0], turns.take())
    turns.end(low[0])
    work.update(sums=(sums_one, sums_two))
    return dx, [to_section(piece, -1) for piece in low] if pass_on else None, work


def step_all(steps):
    results = [None] * len(steps)
    live = list(range(len(steps)))
    rounds = []
    while live:
        given = {}
        for i in list(live):
            try:
                given[i] = next(steps[i])
            except StopIteration as end:
                results[i] = end.value
                live.remove(i)
        rounds.append(given)
        yield results if not live else given


def finish(value):
    rows, width = value.shape
    step = 128

    def body(value_ref, out_ref):
        out_ref[...] = value_ref[...].astype(F32).reshape(step, 1, width)

    return pl.pallas_call(
        body,
        out_shape=jax.ShapeDtypeStruct((rows, 1, width), F32),
        grid=(pl.cdiv(rows, step),),
        in_specs=[pl.BlockSpec((step, width), lambda i: (i, 0))],
        out_specs=pl.BlockSpec((step, 1, width), lambda i: (i, 0, 0)),
        compiler_params=pltpu.CompilerParams(vmem_limit_bytes=8 * 2**20),
    )(value)


def per_device(inputs, norm_gain, norm_bias, w_query, b_query, w_key, w_value, b_value, w_out,
               out_bias, w_up, b_up, w_down):
    first = lax.axis_index("section") == 0
    flag = first.astype(jnp.int32)[None]
    me = lax.axis_index("tensor")
    size = lax.axis_size("tensor")
    chips = size // 2
    chip, core = me // 2, me % 2
    _, micro, images, length, cols = inputs.shape
    unit = 16 * size
    total = -(-length // unit) * unit
    rows = total // size
    pad = total - length
    places = jnp.arange(size)
    order = ((chip + places % chips) % chips) * 2 + (core + places // chips) % 2
    order = order.astype(jnp.int32)
    rel = ((places // 2 - chip) % chips + chips * ((places + core) % 2)).astype(jnp.int32)
    info = jnp.stack([rel[size - 1] * rows + rows - pad, jnp.int32(pad)])
    images_all = micro * images
    sources = order
    small = jnp.concatenate(
        [norm_gain[0], norm_bias[0], out_bias[0], jnp.zeros((2, cols), F32)], axis=0
    )
    high = lax.reduce_precision(small, 8, 7)
    middle_part = lax.reduce_precision(small - high, 8, 7)
    thirds = jnp.concatenate([high, middle_part, small - high - middle_part], axis=0)
    features = inputs[0].reshape(images_all, length, cols).transpose(0, 2, 1)
    qkv = jnp.concatenate([w_query[0].T, w_key[0].T, w_value[0].T], axis=0)
    spread = []
    for n in range(images_all):
        block = features[n]
        if n == 0:
            block = jnp.pad(block, ((0, 0), (0, pad)))
            block = jnp.concatenate([block, thirds.astype(BF16).T], axis=1)
        else:
            (block,) = hold([block], full[0][:1])
        mine, other = spread_block(block, chips)
        spread.append(mine + other)
        if n == 0:
            halves, (small,) = assemble(
                spread[0], length, sources, order, rows, small.shape[0],
                near=(qkv,),
            )
            full = {0: halves}
    turns = Turns()

    def whole(n):
        if n not in full:
            full[n], _ = assemble(spread[n], length, sources, order, rows, 0, turns.take())
        return Source(full[n])

    w = dict(
        gain=(small[0:1], small[1:2]), bias=(small[2:3], small[3:4]),
        out_bias=(small[4:5], small[5:6]),
        qkv=qkv, qkv_shift=jnp.concatenate([b_query, jnp.zeros_like(b_query), b_value], axis=1),
        wout=w_out[0], w_up=w_up[0].T, b_up=b_up, w_down=w_down[0],
    )
    span = range(images_all)

    def widen(n, pieces, chosen):
        return Source(full[n], hand_over(pieces, chips), chosen)

    *_, lows = step_all(
        [
            forward(functools.partial(whole, n), w, info, chips, total, False, turns)
            for n in span
        ]
    )
    *_, done = step_all(
        [
            forward(
                functools.partial(widen, n, lows[n], flag), w, info, chips, total, True, turns
            )
            for n in span
        ]
    )
    results, saves = [d[0] for d in done], [d[1] for d in done]
    *_, done = step_all(
        [backward(functools.partial(whole, n), saves[n], w, chips, turns, True) for n in span]
    )
    lows = [d[1] for d in done]
    grads = [collect(widen(n, lows[n], 1 - flag), total, cols * size) for n in span]
    both = (0, 1)
    hidden = w_up.shape[2]
    steps = [
        backward(functools.partial(Source, grads[n]), saves[n], w, chips, turns, False)
        for n in span
    ]
    next(steps[0])
    g_down = outer(
        [(saves[n]["m"][i], grads[n][i]) for n in span for i in both], 0, hidden, turns.take()
    )
    turns.end(g_down)
    g_down = lax.psum(g_down, "dp")
    for step in steps[1:]:
        next(step)
    steps = step_all(steps)
    works = next(steps)
    width = cols * size
    heads = b_query.shape[1]
    g_up = outer(
        [(works[n]["du"][i], saves[n]["n2"][i]) for n in span for i in both], 0, hidden,
        turns.take(),
    )
    rest = [outer([(saves[n]["o"][i], works[n]["dh"][i]) for n in span for i in both], 0, heads)]
    rest.append(outer([(works[n]["dqkv"], saves[n]["normed"]) for n in span], 0, 3 * heads))
    done = next(steps)
    works = [d[2] for d in done]
    ends = [jnp.where(first, done[n][0], results[n]) for n in span]

    def total_of(parts):
        return sum(jnp.sum(p.astype(F32), 0) for p in parts)

    wide = sum(
        jnp.stack(
            [
                works[n]["sums"][0][0], works[n]["sums"][1][0],
                works[n]["sums"][0][1], works[n]["sums"][1][1],
                works[n]["sums"][1][3], works[n]["sums"][1][2],
            ]
        )
        for n in span
    )
    wide = lax.psum(wide, "tensor")
    wide = lax.dynamic_slice_in_dim(wide, me * cols, cols, 1)
    vector = jnp.concatenate(
        [
            wide.reshape(-1),
            total_of([works[n]["dqkv"] for n in span]),
            total_of([works[n]["du"][i] for n in span for i in both]),
        ]
    )
    count = vector.size
    lines = -(-count // (16 * width)) * 16
    vector = jnp.pad(vector, (0, lines * width - count)).reshape(lines, width).astype(BF16)
    rest = hold([g_up, *rest, vector], (g_down,))
    g_up, g_out, g_qkv, vector = lax.psum(rest, "dp")
    g_query, g_key, g_value = (g_qkv[i * heads : (i + 1) * heads] for i in range(3))
    vector = vector.astype(F32).reshape(-1)
    wide = vector[: 6 * cols].reshape(6, cols)
    narrow = vector[6 * cols : count]

    ends = jnp.stack(ends).reshape(images_all, rows, size, cols)
    ends = lax.all_to_all(ends, "tensor", split_axis=2, concat_axis=1, tiled=True)
    ends = ends.reshape(images_all, total, cols)[:, :length]
    ends = ends.reshape(1, micro, images, length, cols)
    return (
        ends, wide[None, 0:2], wide[None, 2:4], g_query.T[None].astype(F32), narrow[None, :heads], g_key.T[None].astype(F32),
        g_value.T[None].astype(F32), narrow[None, 2 * heads : 3 * heads], g_out[None].astype(F32), wide[None, 4:6],
        finish(g_up).transpose(1, 2, 0),
        narrow[None, 3 * heads :], finish(g_down).transpose(1, 0, 2),
    )


def solution(mesh):
    columns = P("section", None, "tensor")
    vector = P("section", "tensor")
    stacked = P("section", "tensor", None)
    tokens = P("section", None, "dp", None, "tensor")
    weights = (columns, columns, columns, vector, columns, columns, vector, stacked, columns,
               columns, vector, stacked)
    return jax.shard_map(
        per_device, mesh=mesh, in_specs=(tokens, *weights), out_specs=(tokens, *weights),
        check_vma=False,
    )
```

```python
import functools

import jax
import jax.numpy as jnp
from jax import lax
from jax.experimental import pallas as pl
from jax.experimental.pallas import tpu as pltpu
from jax.sharding import PartitionSpec as P

HD = 72
LANES = 128
EPS = 1e-06
SCALE = HD**-0.5
LOG2E = 1.4426950408889634
FAR = -1e30
LIMIT = 6
COST = 14
STEP = 48
GELU_A = 0.7978845608028654
GELU_B = 0.044715
F32 = jnp.float32
BF16 = jnp.bfloat16
VMEM = pl.BlockSpec(memory_space=pltpu.VMEM)
SMEM = pl.BlockSpec(memory_space=pltpu.SMEM)


def run(body, outs, args, scalars=0, flops=0, scratch=(), limit=LIMIT, after=(), near=()):
    bytes_accessed = sum(a.size * a.dtype.itemsize for a in args) + sum(
        jnp.dtype(dtype).itemsize * shape[0] * shape[1] for shape, dtype in outs
    )
    count, extra = len(args), len(near) + len(after)

    def kernel(*refs):
        body(*refs[:count], *refs[count + extra :])

    return pl.pallas_call(
        kernel,
        out_shape=[jax.ShapeDtypeStruct(shape, dtype) for shape, dtype in outs],
        in_specs=[SMEM] * scalars
        + [VMEM] * (count - scalars)
        + [VMEM] * len(near)
        + [pl.BlockSpec(memory_space=pl.ANY)] * len(after),
        out_specs=[VMEM] * len(outs),
        scratch_shapes=list(scratch),
        compiler_params=pltpu.CompilerParams(vmem_limit_bytes=limit * 2**20),
        cost_estimate=pl.CostEstimate(
            flops=int(flops) * COST, bytes_accessed=int(bytes_accessed), transcendentals=0
        ),
    )(*args, *near, *after)


def mm(left, right):
    return jnp.dot(left, right, preferred_element_type=F32)


def mm_nt(left, right):
    return lax.dot_general(left, right, (((1,), (1,)), ((), ())), preferred_element_type=F32)


def mm_tn(left, right):
    return lax.dot_general(left, right, (((0,), (0,)), ((), ())), preferred_element_type=F32)


def unit_rows(x):
    center = x - jnp.mean(x, 1, keepdims=True)
    inverse = lax.rsqrt(jnp.mean(center * center, 1, keepdims=True) + EPS)
    return center * inverse, inverse


def assemble(parts, length, sources, order, rows, extra, after=(), near=()):
    count = len(parts)
    cols = parts[0].shape[0]
    half, total, width = count // 2, rows * count, cols * count

    def body(*refs):
        src_ref, order_ref = refs[:2]
        part_refs = refs[2 : 2 + count]
        mine_ref, other_ref, *small_out, wide_ref, tall_ref = refs[2 + count :]
        edge = length // LANES * LANES
        wide_ref[:, edge:] = jnp.zeros((width, wide_ref.shape[1] - edge), BF16)
        for i in range(count):
            start = pl.multiple_of(src_ref[i] * cols, 16)
            wide_ref[pl.ds(start, cols), 0 : parts[i].shape[1]] = part_refs[i][...]
        tall_ref[...] = wide_ref[...].T
        if extra:
            behind = tall_ref[total : total + 3 * extra, :].astype(F32)
            small_out[0][...] = (
                behind[0:extra] + behind[extra : 2 * extra] + behind[2 * extra :]
            )
            tall_ref[total : total + LANES, :] = jnp.zeros((LANES, width), BF16)
        for place in range(count):
            start = pl.multiple_of(order_ref[place] * rows, 16)
            out = mine_ref if place < half else other_ref
            at = (place % half) * rows
            out[at : at + rows, :] = tall_ref[pl.ds(start, rows), :]

    shape = ((half * rows, width), BF16)
    deep = total + (LANES if extra else 0)
    mine, other, *small = run(
        body,
        [shape, shape] + ([((extra, width), F32)] if extra else []),
        (sources, order, *parts),
        scalars=2,
        scratch=(pltpu.VMEM((width, deep), BF16), pltpu.VMEM((deep, width), BF16)),
        limit=10,
        after=after,
        near=near,
    )
    return (mine, other), small


class Source:
    def __init__(self, halves=None, blocks=None, flag=None):
        self.halves, self.blocks, self.flag = halves, blocks, flag

    def operands(self, which):
        scalars = [] if self.flag is None else [self.flag]
        arrays = []
        for i in which:
            arrays += [] if self.halves is None else [self.halves[i]]
            arrays += [] if self.blocks is None else self.blocks[i]
        return scalars, arrays

    def reader(self, which, scalar_refs, refs):
        refs, table = list(refs), {}
        for i in which:
            base = None if self.halves is None else refs.pop(0)
            count = 0 if self.blocks is None else len(self.blocks[i])
            table[i] = (base, [refs.pop(0) for _ in range(count)])

        def read(i, start, rows):
            base, blocks = table[i]
            value = None
            if blocks:
                size = blocks[0].shape[0]
                value = blocks[start // size][start % size : start % size + rows, :]
            if base is not None:
                at_hand = base[start : start + rows, :]
                if value is None:
                    return at_hand
                value = jnp.where(scalar_refs[0][0] != 0, at_hand, value)
            return value

        return read


def collect(source, rows, width):
    half = rows // 2
    scalars, arrays = source.operands((0, 1))

    def body(*refs):
        read = source.reader((0, 1), refs[: len(scalars)], refs[len(scalars) : -2])
        for i, out in enumerate(refs[-2:]):
            for at in range(0, half, STEP):
                out[at : at + STEP, :] = read(i, at, STEP)

    shape = ((half, width), BF16)
    return run(body, [shape, shape], (*scalars, *arrays), scalars=len(scalars), flops=rows * width)


def project(info, source, gain, bias, weight, shift, rows, save, after=()):
    cols, width = weight.shape[0] // 3, weight.shape[1]
    heads = cols // HD
    scalars, arrays = source.operands((0, 1))
    count, total = len(arrays), rows
    half = total // 2
    step = STEP

    def body(*refs):
        info_ref, flags = refs[0], refs[1 : 1 + len(scalars)]
        refs = refs[1 + len(scalars) :]
        read = source.reader((0, 1), flags, refs[:count])
        g_ref, b_ref, w_ref, s_ref, x_ref, *outs, n_ref = refs[count:]
        for index in (0, 1):
            for at in range(0, half, step):
                value = read(index, at, step)
                if index == 0:
                    x_ref[at : at + step, :] = value
                unit, _ = unit_rows(value.astype(F32))
                n_ref[index * half + at : index * half + at + step, :] = (
                    unit * g_ref[...] + b_ref[...]
                ).astype(BF16)
        row = lax.broadcasted_iota(jnp.int32, (total, LANES - HD), 0)
        lane = lax.broadcasted_iota(jnp.int32, (total, LANES - HD), 1)
        pad_start = info_ref[0]
        padded = (row >= pad_start) & (row < pad_start + info_ref[1])
        ones = jnp.where(lane == 0, 1.0, 0.0).astype(BF16)
        mask = jnp.where((lane == 0) & padded, FAR, 0.0).astype(BF16)
        normed = n_ref[...]
        for i, (out, extra) in enumerate(zip(outs[:3], (ones, mask, ones))):
            here = slice(i * cols, (i + 1) * cols)
            value = (mm_nt(normed, w_ref[here, :]) + s_ref[:, here]).astype(BF16)
            for h in range(heads):
                out[:, h * LANES : (h + 1) * LANES] = jnp.concatenate(
                    [value[:, h * HD : (h + 1) * HD], extra], axis=1
                )

    wide = ((total, heads * LANES), BF16)
    return run(
        body,
        [((half, width), BF16), wide, wide, wide] + ([((total, width), BF16)] if save else []),
        (info, *scalars, *arrays, gain, bias, weight, shift),
        scalars=1 + len(scalars),
        flops=6 * total * width * cols,
        scratch=() if save else (pltpu.VMEM((total, width), BF16),),
        limit=LIMIT if save else LIMIT + 2,
        after=after,
    )


def attend(first_row, q, k, v, wout, out_type, save):
    total, wide = q.shape
    heads = wide // LANES
    half = total // 2
    step = half

    def body(q_ref, k_ref, v_ref, w_ref, z_ref, *saved):
        for at in range(0, half, step):
            outs, logs = [], []
            for h in range(heads):
                lanes = slice(h * LANES, (h + 1) * LANES)
                scores = mm_nt(q_ref[first_row + at : first_row + at + step, lanes], k_ref[:, lanes])
                highest = jnp.max(scores, 1, keepdims=True)
                weights = jnp.exp2((scores - highest) * (SCALE * LOG2E)).astype(BF16)
                mixed = mm(weights, v_ref[:, lanes])
                sums = mixed[:, HD : HD + 1]
                outs.append((mixed / sums).astype(BF16)[:, :HD])
                logs.append(highest * (SCALE * LOG2E) + jnp.log(sums) * LOG2E)
            mixed = jnp.concatenate(outs, axis=1)
            z_ref[at : at + step, :] = mm(mixed, w_ref[...]).astype(out_type)
            if not save:
                continue
            saved[0][at : at + step, :] = mixed
            logs = jnp.concatenate(logs + [jnp.zeros((step, LANES - heads), F32)], axis=1)
            saved[1][:, at : at + step] = logs.T[:8, :]

    return run(
        body,
        [((half, wout.shape[1]), out_type)]
        + ([((half, heads * HD), BF16), ((8, half), F32)] if save else []),
        (q, k, v, wout),
        flops=4 * half * total * LANES * heads + 2 * half * heads * HD * wout.shape[1],
    )


def middle(xm, own, arrived, out_bias, gain, bias, after=()):
    half, width = xm.shape
    parts = len(arrived) + 1
    rows = half // parts

    def body(x_ref, own_ref, *refs):
        got = refs[: parts - 1]
        ob_ref, g_ref, b_ref, h_ref, n_ref = refs[parts - 1 :]
        def step(i, carry):
            at = pl.multiple_of(i * STEP, 16)
            here = pl.ds(at, STEP)
            value = x_ref[here, :].astype(F32) + ob_ref[...]
            total = own_ref[here, :].astype(F32)
            for shift, ref in enumerate(got, 1):
                there = pl.multiple_of(lax.rem(at + shift * rows, half), 16)
                total = total + ref[pl.ds(there, STEP), :].astype(F32)
            value = value + total
            h_ref[here, :] = value
            unit, _ = unit_rows(value)
            n_ref[here, :] = (unit * g_ref[...] + b_ref[...]).astype(BF16)
            return carry

        lax.fori_loop(0, half // STEP, step, 0)

    return run(
        body,
        [((half, width), F32), ((half, width), BF16)],
        (xm, own, *arrived, out_bias, gain, bias),
        flops=20 * half * width,
        after=after,
    )


def mlp(n2, w_up, b_up, w_down, out_type, save):
    half, width = n2.shape
    hidden = w_up.shape[0]
    step = half

    def body(n_ref, wu_ref, bu_ref, wd_ref, z_ref, *saved):
        for at in range(0, half, step):
            here = slice(at, at + step)
            u = mm_nt(n_ref[here, :], wu_ref[...]) + bu_ref[...]
            square = u * u
            t = jnp.tanh(GELU_A * u * (1.0 + GELU_B * square))
            low = 0.5 * (1.0 + t)
            active = (u * low).astype(BF16)
            if save:
                slope = low + (0.5 * GELU_A) * u * (1.0 - t * t) * (1.0 + (3 * GELU_B) * square)
                saved[0][here, :] = active
                saved[1][here, :] = slope.astype(BF16)
            z_ref[here, :] = mm(active, wd_ref[...]).astype(out_type)

    outs = [((half, width), out_type)]
    if save:
        outs += [((half, hidden), BF16)] * 2
    return run(body, outs, (n2, w_up, b_up, w_down), flops=4 * half * width * hidden)


def mlp_back(g, slope, w_up, w_down, out_type, save, after=()):
    half, hidden = slope.shape
    width = w_up.shape[1]

    def body(g_ref, s_ref, wu_ref, wd_ref, z_ref, *saved):
        grad = (mm_nt(g_ref[...], wd_ref[...]) * s_ref[...].astype(F32)).astype(BF16)
        if save:
            saved[0][...] = grad
        z_ref[...] = mm(grad, wu_ref[...]).astype(out_type)

    return run(
        body,
        [((half, width), out_type)] + ([((half, hidden), BF16)] if save else []),
        (g, slope, w_up, w_down),
        flops=4 * half * width * hidden,
        after=after,
    )


def middle_back(g, h, own, arrived, gain, after=()):
    half, width = g.shape
    parts = len(arrived) + 1
    rows = half // parts

    def body(g_ref, h_ref, own_ref, *refs):
        got = refs[: parts - 1]
        gain_ref, d_ref, low_ref, sums_ref = refs[parts - 1 :]
        def step(i, sums):
            at = pl.multiple_of(i * STEP, 16)
            here = pl.ds(at, STEP)
            grad = own_ref[here, :].astype(F32)
            for shift, ref in enumerate(got, 1):
                there = pl.multiple_of(lax.rem(at + shift * rows, half), 16)
                grad = grad + ref[pl.ds(there, STEP), :].astype(F32)
            unit, inverse = unit_rows(h_ref[here, :])
            scaled = grad * gain_ref[...]
            first = jnp.mean(scaled, 1, keepdims=True)
            second = jnp.mean(scaled * unit, 1, keepdims=True)
            upstream = g_ref[here, :].astype(F32)
            total = upstream + inverse * (scaled - first - unit * second)
            d_ref[here, :] = total
            low = total.astype(BF16)
            low_ref[here, :] = low
            terms = (grad * unit, grad, upstream, low.astype(F32))
            return tuple(a + jnp.sum(t, 0, keepdims=True) for a, t in zip(sums, terms))

        zeros = (jnp.zeros((1, width), F32),) * 4
        sums = lax.fori_loop(0, rows // STEP, step, zeros)
        lax.fori_loop(rows // STEP, half // STEP, lambda i, c: (step(i, zeros), c)[1], 0)
        for i in range(4):
            sums_ref[i : i + 1, :] = sums[i]

    return run(
        body,
        [((half, width), F32), ((half, width), BF16), ((8, width), F32)],
        (g, h, own, *arrived, gain),
        flops=30 * half * width,
        after=after,
    )


def attend_back(dm, do, wout, q, k, v, lm, lo):
    half = dm.shape[0]
    total, wide = q.shape
    heads = wide // LANES
    step = total

    def body(dm_ref, do_ref, w_ref, q_ref, k_ref, v_ref, lm_ref, lo_ref,
             d_ref, up_ref, log_ref, p_ref, w_ref2):
        for index, ref in enumerate((dm_ref, do_ref)):
            here = slice(index * half, (index + 1) * half)
            grad = mm_nt(ref[...], w_ref[...]).astype(BF16)
            fill = jnp.zeros((half, LANES - HD), BF16)
            for h in range(heads):
                cols = slice(h * HD, (h + 1) * HD)
                up = jnp.concatenate([grad[:, cols], fill], axis=1)
                up_ref[here, h * LANES : (h + 1) * LANES] = up
        log_ref[0:8, 0:half] = lm_ref[...]
        log_ref[0:8, half:total] = lo_ref[...]
        dqs, dks, dvs = [], [], []
        for h in range(heads):
            lanes = slice(h * LANES, (h + 1) * LANES)
            up = up_ref[:, lanes]
            queries = q_ref[:, lanes]
            sums = jnp.zeros((1, total), F32)
            dv_h = []
            for at in range(0, total, step):
                here = slice(at, at + step)
                scores = mm_nt(k_ref[here, lanes], queries)
                probs = jnp.exp2(scores * (SCALE * LOG2E) - log_ref[h : h + 1, :])
                weighted = probs * mm_nt(v_ref[here, lanes], up)
                sums = sums + jnp.sum(weighted, 0, keepdims=True)
                p_ref[here, :] = probs
                w_ref2[here, :] = weighted
                dv_h.append(mm(probs.astype(BF16), up).astype(BF16)[:, :HD])
            dq_t = jnp.zeros((LANES, total), F32)
            dk_h = []
            for at in range(0, total, step):
                here = slice(at, at + step)
                dscores = (w_ref2[here, :] - p_ref[here, :] * sums).astype(BF16)
                dk_h.append((mm(dscores, queries) * SCALE).astype(BF16)[:, :HD])
                dq_t = dq_t + mm_tn(k_ref[here, lanes], dscores)
            dqs.append((dq_t * SCALE).T.astype(BF16)[:, :HD])
            dks.append(jnp.concatenate(dk_h, axis=0))
            dvs.append(jnp.concatenate(dv_h, axis=0))
        d_ref[...] = jnp.concatenate([*dqs, *dks, *dvs], axis=1)

    return run(
        body,
        [((total, 3 * heads * HD), BF16)],
        (dm, do, wout, q, k, v, lm, lo),
        flops=10 * total * total * LANES * heads + 2 * total * heads * HD * dm.shape[1],
        scratch=(
            pltpu.VMEM((total, wide), BF16),
            pltpu.VMEM((8, total), F32),
            pltpu.VMEM((total, total), F32),
            pltpu.VMEM((total, total), F32),
        ),
        limit=12,
    )[0]


def project_back(first_row, grad, weight, out_type):
    total = grad.shape[0]
    half = total // 2
    cols, width = weight.shape

    def body(d_ref, w_ref, z_ref):
        z_ref[...] = mm(d_ref[first_row : first_row + half, :], w_ref[...]).astype(out_type)

    return run(
        body, [((half, width), out_type)], (grad, weight), flops=2 * half * cols * width
    )[0]


def start_back(xm, dh, own, arrived, gain, after=()):
    rows, width = own.shape
    part = rows // pieces_of(rows)
    count = len(arrived)

    def body(x_ref, dh_ref, own_ref, *refs):
        got = refs[:count]
        gain_ref, d_ref, sums_ref, *low_refs = refs[count:]
        def step(i, sums):
            here = pl.ds(pl.multiple_of(i * STEP, 16), STEP)
            grad = own_ref[here, :]
            for ref in got:
                grad = grad + ref[here, :].astype(F32)
            unit, inverse = unit_rows(x_ref[here, :].astype(F32))
            scaled = grad * gain_ref[...]
            first = jnp.mean(scaled, 1, keepdims=True)
            second = jnp.mean(scaled * unit, 1, keepdims=True)
            total = dh_ref[here, :] + inverse * (scaled - first - unit * second)
            d_ref[here, :] = total
            return tuple(
                a + jnp.sum(t, 0, keepdims=True) for a, t in zip(sums, (grad * unit, grad))
            )

        sums = lax.fori_loop(0, rows // STEP, step, (jnp.zeros((1, width), F32),) * 2)
        for i in range(2):
            sums_ref[i : i + 1, :] = sums[i]
        for i, ref in enumerate(low_refs):
            ref[...] = d_ref[i * part : (i + 1) * part, :].astype(BF16)

    d, sums, *low = run(
        body,
        [((rows, width), F32), ((8, width), F32)]
        + [((part, width), BF16)] * (rows // part),
        (xm, dh, own, *arrived, gain),
        flops=30 * rows * width,
        after=after,
    )
    return d, low, sums


def finish_rows(hidden, total, arrived, out_bias, after=()):
    rows, width = total[0].shape
    part = rows // pieces_of(rows)

    def body(h_ref, total_ref, *refs):
        bias_ref, y_ref, *low_refs = refs[len(arrived) :]
        value = total_ref[...]
        for ref in refs[: len(arrived)]:
            value = value + ref[...].astype(F32)
        value = h_ref[0:rows, :] + value + bias_ref[...]
        y_ref[...] = value
        for i, ref in enumerate(low_refs):
            ref[...] = value[i * part : (i + 1) * part, :].astype(BF16)

    y, *low = run(
        body,
        [((rows, width), F32)] + [((part, width), BF16)] * (rows // part),
        (hidden, total[0], *arrived, out_bias),
        flops=4 * rows * width,
        after=after,
    )
    return y, low


def outer(pairs, low, high, after=()):
    width = pairs[0][1].shape[1]

    def body(*refs):
        out = refs[-1]
        total = None
        for i in range(len(pairs)):
            term = mm_tn(refs[2 * i][:, low:high], refs[2 * i + 1][...])
            total = term if total is None else total + term
        out[...] = total.astype(BF16)

    return run(
        body,
        [((high - low, width), BF16)],
        [array for pair in pairs for array in pair],
        flops=2 * (high - low) * width * sum(pair[0].shape[0] for pair in pairs),
        limit=16,
        after=after,
    )[0]


def add(left, right, after=()):
    def body(left_ref, right_ref, out):
        out[...] = (left_ref[...].astype(F32) + right_ref[...].astype(F32)).astype(BF16)

    return run(body, [(left.shape, BF16)], (left, right), flops=left.size, after=after)[0]


def hold(arrays, after):
    count = len(arrays)
    anywhere = pl.BlockSpec(memory_space=pl.ANY)
    return pl.pallas_call(
        lambda *refs: None,
        out_shape=[jax.ShapeDtypeStruct(a.shape, a.dtype) for a in arrays],
        in_specs=[anywhere] * (count + len(after)),
        out_specs=[anywhere] * count,
        input_output_aliases={i: i for i in range(count)},
    )(*arrays, *after)


def core_swap(value):
    size = lax.axis_size("tensor")
    return lax.ppermute(value, "tensor", [(i, i ^ 1) for i in range(size)])


def chip_shift(value, shift):
    size = lax.axis_size("tensor")
    return lax.ppermute(value, "tensor", [(i, (i + 2 * shift) % size) for i in range(size)])


def share_half(half, chips):
    return [chip_shift(half, s) for s in range(1, chips)]


def spread_block(block, chips):
    mine = [block] + [chip_shift(block, chips - p) for p in range(1, chips)]
    return mine, [core_swap(b) for b in mine]


def hand_over(pieces, chips, after=()):
    if after:
        pieces = hold(pieces, after)
    spread = [spread_block(piece, chips) for piece in pieces]
    return [[spread[j][i][p] for p in range(chips) for j in range(len(pieces))] for i in (0, 1)]


def pieces_of(rows):
    return 2 if rows % 32 == 0 and rows >= 128 else 1


def sum_blocks(mine, other, chips):
    rows = mine.shape[0] // chips

    def body(mine_ref, other_ref, own_ref, *sends):
        own_ref[...] = mine_ref[0:rows, :] + other_ref[0:rows, :].astype(F32)
        for p, ref in enumerate(sends, 1):
            here = slice(p * rows, (p + 1) * rows)
            ref[...] = (mine_ref[here, :] + other_ref[here, :].astype(F32)).astype(BF16)

    shape = (rows, mine.shape[1])
    own, *sends = run(body, [(shape, F32)] + [(shape, BF16)] * (chips - 1), (mine, other))
    return (own, *sends), [chip_shift(send, p) for p, send in enumerate(sends, 1)]


def to_section(value, step):
    pairs = [(0, 1)] if step > 0 else [(1, 0)]
    return lax.ppermute(value, "section", pairs)


class Turns:
    def __init__(self):
        self.last, self.first = (), ()

    def take(self):
        return self.last

    def end(self, *arrays):
        self.last = tuple(arrays)


def forward(source, w, info, chips, rows, save, turns):
    source = source()
    xm, q, k, v, *kept = project(
        info, source, w["gain"][0], w["bias"][0], w["qkv"], w["qkv_shift"], rows, save,
        turns.take(),
    )
    turns.first = (q,)
    half = rows // 2
    z_other, *kept_other = attend(half, q, k, v, w["wout"], BF16, save)
    z_other = core_swap(z_other)
    z_mine, *kept_mine = attend(0, q, k, v, w["wout"], F32, save)
    own = add(z_mine, z_other)
    turns.end(own)
    arrived = share_half(own, chips)
    yield
    hidden, n2m = middle(
        xm, own, arrived, w["out_bias"][0], w["gain"][1], w["bias"][1], turns.take()
    )
    n2o = core_swap(n2m)
    mine = mlp(n2m, w["w_up"], w["b_up"], w["w_down"], F32, save)
    other = mlp(n2o, w["w_up"], w["b_up"], w["w_down"], BF16, save)
    y_other = core_swap(other[0])
    total, arrived = sum_blocks(mine[0], y_other, chips)
    saved = None
    if save:
        saved = dict(
            x=xm, normed=kept[0], q=q, k=k, v=v,
            o=(kept_mine[0], kept_other[0]), l=(kept_mine[1], kept_other[1]),
            h=hidden, n2=(n2m, n2o), m=(mine[1], other[1]), slope=(mine[2], other[2]),
        )
        turns.end(mine[2], other[2])
        result, _ = finish_rows(hidden, total, arrived, w["out_bias"][1])
        return result, saved
    turns.end(*total)
    yield
    _, low = finish_rows(hidden, total, arrived, w["out_bias"][1], turns.take())
    turns.end(low[0])
    return [to_section(piece, 1) for piece in low]


def backward(source, saved, w, chips, turns, pass_on):
    gm, go = source().halves
    save = not pass_on
    z_other, *du_other = mlp_back(
        go, saved["slope"][1], w["w_up"], w["w_down"], BF16, save, turns.take()
    )
    z_other = core_swap(z_other)
    z_mine, *du_mine = mlp_back(gm, saved["slope"][0], w["w_up"], w["w_down"], F32, save)
    own = add(z_mine, z_other)
    turns.end(own)
    arrived = share_half(own, chips)
    work = dict(du=(*du_mine, *du_other))
    yield work
    dh, dhm, sums_two = middle_back(
        gm, saved["h"], own, arrived, w["gain"][1], turns.take()
    )
    dho = core_swap(dhm)
    q, k, v = saved["q"], saved["k"], saved["v"]
    dqkv = attend_back(dhm, dho, w["wout"], q, k, v, *saved["l"])
    half = gm.shape[0]
    d_other = core_swap(project_back(half, dqkv, w["qkv"], BF16))
    d_mine = project_back(0, dqkv, w["qkv"], F32)
    total, arrived = sum_blocks(d_mine, d_other, chips)
    turns.end(*total)
    work.update(dh=(dhm, dho), dqkv=dqkv)
    yield work
    dx, low, sums_one = start_back(saved["x"], dh, total[0], arrived, w["gain"][0], turns.take())
    turns.end(low[0])
    work.update(sums=(sums_one, sums_two))
    return dx, [to_section(piece, -1) for piece in low] if pass_on else None, work


def step_all(steps):
    results = [None] * len(steps)
    live = list(range(len(steps)))
    rounds = []
    while live:
        given = {}
        for i in list(live):
            try:
                given[i] = next(steps[i])
            except StopIteration as end:
                results[i] = end.value
                live.remove(i)
        rounds.append(given)
        yield results if not live else given


def finish(value):
    rows, width = value.shape
    step = 128

    def body(value_ref, out_ref):
        out_ref[...] = value_ref[...].astype(F32).reshape(step, 1, width)

    return pl.pallas_call(
        body,
        out_shape=jax.ShapeDtypeStruct((rows, 1, width), F32),
        grid=(pl.cdiv(rows, step),),
        in_specs=[pl.BlockSpec((step, width), lambda i: (i, 0))],
        out_specs=pl.BlockSpec((step, 1, width), lambda i: (i, 0, 0)),
        compiler_params=pltpu.CompilerParams(vmem_limit_bytes=8 * 2**20),
    )(value)


def per_device(inputs, norm_gain, norm_bias, w_query, b_query, w_key, w_value, b_value, w_out,
               out_bias, w_up, b_up, w_down):
    first = lax.axis_index("section") == 0
    flag = first.astype(jnp.int32)[None]
    me = lax.axis_index("tensor")
    size = lax.axis_size("tensor")
    chips = size // 2
    chip, core = me // 2, me % 2
    _, micro, images, length, cols = inputs.shape
    unit = 16 * size
    total = -(-length // unit) * unit
    rows = total // size
    pad = total - length
    places = jnp.arange(size)
    order = ((chip + places % chips) % chips) * 2 + (core + places // chips) % 2
    order = order.astype(jnp.int32)
    rel = ((places // 2 - chip) % chips + chips * ((places + core) % 2)).astype(jnp.int32)
    info = jnp.stack([rel[size - 1] * rows + rows - pad, jnp.int32(pad)])
    images_all = micro * images
    sources = order
    small = jnp.concatenate(
        [norm_gain[0], norm_bias[0], out_bias[0], jnp.zeros((2, cols), F32)], axis=0
    )
    high = lax.reduce_precision(small, 8, 7)
    middle_part = lax.reduce_precision(small - high, 8, 7)
    thirds = jnp.concatenate([high, middle_part, small - high - middle_part], axis=0)
    features = inputs[0].reshape(images_all, length, cols).transpose(0, 2, 1)
    qkv = jnp.concatenate([w_query[0].T, w_key[0].T, w_value[0].T], axis=0)
    spread = []
    for n in range(images_all):
        block = features[n]
        if n == 0:
            block = jnp.pad(block, ((0, 0), (0, pad)))
            block = jnp.concatenate([block, thirds.astype(BF16).T], axis=1)
        else:
            (block,) = hold([block], full[0][:1])
        mine, other = spread_block(block, chips)
        spread.append(mine + other)
        if n == 0:
            halves, (small,) = assemble(
                spread[0], length, sources, order, rows, small.shape[0],
                near=(qkv,),
            )
            full = {0: halves}
    turns = Turns()

    def whole(n):
        if n not in full:
            full[n], _ = assemble(spread[n], length, sources, order, rows, 0, turns.take())
        return Source(full[n])

    w = dict(
        gain=(small[0:1], small[1:2]), bias=(small[2:3], small[3:4]),
        out_bias=(small[4:5], small[5:6]),
        qkv=qkv, qkv_shift=jnp.concatenate([b_query, jnp.zeros_like(b_query), b_value], axis=1),
        wout=w_out[0], w_up=w_up[0].T, b_up=b_up, w_down=w_down[0],
    )
    span = range(images_all)

    def widen(n, pieces, chosen):
        return Source(full[n], hand_over(pieces, chips), chosen)

    *_, lows = step_all(
        [
            forward(functools.partial(whole, n), w, info, chips, total, False, turns)
            for n in span
        ]
    )
    *_, done = step_all(
        [
            forward(
                functools.partial(widen, n, lows[n], flag), w, info, chips, total, True, turns
            )
            for n in span
        ]
    )
    results, saves = [d[0] for d in done], [d[1] for d in done]
    *_, done = step_all(
        [backward(functools.partial(whole, n), saves[n], w, chips, turns, True) for n in span]
    )
    lows = [d[1] for d in done]
    grads = [collect(widen(n, lows[n], 1 - flag), total, cols * size) for n in span]
    both = (0, 1)
    hidden = w_up.shape[2]
    steps = [
        backward(functools.partial(Source, grads[n]), saves[n], w, chips, turns, False)
        for n in span
    ]
    next(steps[0])
    g_down = outer(
        [(saves[n]["m"][i], grads[n][i]) for n in span for i in both], 0, hidden, turns.take()
    )
    turns.end(g_down)
    g_down = lax.psum(g_down, "dp")
    for step in steps[1:]:
        next(step)
    steps = step_all(steps)
    works = next(steps)
    width = cols * size
    heads = b_query.shape[1]
    g_up = outer(
        [(works[n]["du"][i], saves[n]["n2"][i]) for n in span for i in both], 0, hidden,
        turns.take(),
    )
    rest = [outer([(saves[n]["o"][i], works[n]["dh"][i]) for n in span for i in both], 0, heads)]
    rest.append(outer([(works[n]["dqkv"], saves[n]["normed"]) for n in span], 0, 3 * heads))
    done = next(steps)
    works = [d[2] for d in done]
    ends = [jnp.where(first, done[n][0], results[n]) for n in span]

    def total_of(parts):
        return sum(jnp.sum(p.astype(F32), 0) for p in parts)

    wide = sum(
        jnp.stack(
            [
                works[n]["sums"][0][0], works[n]["sums"][1][0],
                works[n]["sums"][0][1], works[n]["sums"][1][1],
                works[n]["sums"][1][3], works[n]["sums"][1][2],
            ]
        )
        for n in span
    )
    wide = lax.psum(wide, "tensor")
    wide = lax.dynamic_slice_in_dim(wide, me * cols, cols, 1)
    vector = jnp.concatenate(
        [
            wide.reshape(-1),
            total_of([works[n]["dqkv"] for n in span]),
            total_of([works[n]["du"][i] for n in span for i in both]),
        ]
    )
    count = vector.size
    lines = -(-count // (16 * width)) * 16
    vector = jnp.pad(vector, (0, lines * width - count)).reshape(lines, width).astype(BF16)
    rest = hold([g_up, *rest, vector], (g_down,))
    g_up, g_out, g_qkv, vector = lax.psum(rest, "dp")
    g_query, g_key, g_value = (g_qkv[i * heads : (i + 1) * heads] for i in range(3))
    vector = vector.astype(F32).reshape(-1)
    wide = vector[: 6 * cols].reshape(6, cols)
    narrow = vector[6 * cols : count]

    ends = jnp.stack(ends).reshape(images_all, rows, size, cols)
    ends = lax.all_to_all(ends, "tensor", split_axis=2, concat_axis=1, tiled=True)
    ends = ends.reshape(images_all, total, cols)[:, :length]
    ends = ends.reshape(1, micro, images, length, cols)
    return (
        ends, wide[None, 0:2], wide[None, 2:4], g_query.T[None].astype(F32), narrow[None, :heads], g_key.T[None].astype(F32),
        g_value.T[None].astype(F32), narrow[None, 2 * heads : 3 * heads], g_out[None].astype(F32), wide[None, 4:6],
        finish(g_up).transpose(1, 2, 0),
        narrow[None, 3 * heads :], finish(g_down).transpose(1, 0, 2),
    )


def solution(mesh):
    columns = P("section", None, "tensor")
    vector = P("section", "tensor")
    stacked = P("section", "tensor", None)
    tokens = P("section", None, "dp", None, "tensor")
    weights = (columns, columns, columns, vector, columns, columns, vector, stacked, columns,
               columns, vector, stacked)
    return jax.shard_map(
        per_device, mesh=mesh, in_specs=(tokens, *weights), out_specs=(tokens, *weights),
        check_vma=False,
    )
```

```python
import functools

import jax
import jax.numpy as jnp
from jax import lax
from jax.experimental import pallas as pl
from jax.experimental.pallas import tpu as pltpu
from jax.sharding import PartitionSpec as P

HD = 72
LANES = 128
EPS = 1e-06
SCALE = HD**-0.5
LOG2E = 1.4426950408889634
FAR = -1e30
LIMIT = 6
COST = 14
STEP = 48
GELU_A = 0.7978845608028654
GELU_B = 0.044715
F32 = jnp.float32
BF16 = jnp.bfloat16
VMEM = pl.BlockSpec(memory_space=pltpu.VMEM)
SMEM = pl.BlockSpec(memory_space=pltpu.SMEM)


def run(body, outs, args, scalars=0, flops=0, scratch=(), limit=LIMIT, after=(), near=()):
    bytes_accessed = sum(a.size * a.dtype.itemsize for a in args) + sum(
        jnp.dtype(dtype).itemsize * shape[0] * shape[1] for shape, dtype in outs
    )
    count, extra = len(args), len(near) + len(after)

    def kernel(*refs):
        body(*refs[:count], *refs[count + extra :])

    return pl.pallas_call(
        kernel,
        out_shape=[jax.ShapeDtypeStruct(shape, dtype) for shape, dtype in outs],
        in_specs=[SMEM] * scalars
        + [VMEM] * (count - scalars)
        + [VMEM] * len(near)
        + [pl.BlockSpec(memory_space=pl.ANY)] * len(after),
        out_specs=[VMEM] * len(outs),
        scratch_shapes=list(scratch),
        compiler_params=pltpu.CompilerParams(vmem_limit_bytes=limit * 2**20),
        cost_estimate=pl.CostEstimate(
            flops=int(flops) * COST, bytes_accessed=int(bytes_accessed), transcendentals=0
        ),
    )(*args, *near, *after)


def mm(left, right):
    return jnp.dot(left, right, preferred_element_type=F32)


def mm_nt(left, right):
    return lax.dot_general(left, right, (((1,), (1,)), ((), ())), preferred_element_type=F32)


def mm_tn(left, right):
    return lax.dot_general(left, right, (((0,), (0,)), ((), ())), preferred_element_type=F32)


def unit_rows(x):
    center = x - jnp.mean(x, 1, keepdims=True)
    inverse = lax.rsqrt(jnp.mean(center * center, 1, keepdims=True) + EPS)
    return center * inverse, inverse


def assemble(parts, length, sources, order, rows, extra, after=(), near=()):
    count = len(parts)
    cols = parts[0].shape[0]
    half, total, width = count // 2, rows * count, cols * count

    def body(*refs):
        src_ref, order_ref = refs[:2]
        part_refs = refs[2 : 2 + count]
        mine_ref, other_ref, *small_out, wide_ref, tall_ref = refs[2 + count :]
        edge = length // LANES * LANES
        wide_ref[:, edge:] = jnp.zeros((width, wide_ref.shape[1] - edge), BF16)
        for i in range(count):
            start = pl.multiple_of(src_ref[i] * cols, 16)
            wide_ref[pl.ds(start, cols), 0 : parts[i].shape[1]] = part_refs[i][...]
        tall_ref[...] = wide_ref[...].T
        if extra:
            behind = tall_ref[total : total + 3 * extra, :].astype(F32)
            small_out[0][...] = (
                behind[0:extra] + behind[extra : 2 * extra] + behind[2 * extra :]
            )
            tall_ref[total : total + LANES, :] = jnp.zeros((LANES, width), BF16)
        for place in range(count):
            start = pl.multiple_of(order_ref[place] * rows, 16)
            out = mine_ref if place < half else other_ref
            at = (place % half) * rows
            out[at : at + rows, :] = tall_ref[pl.ds(start, rows), :]

    shape = ((half * rows, width), BF16)
    deep = total + (LANES if extra else 0)
    mine, other, *small = run(
        body,
        [shape, shape] + ([((extra, width), F32)] if extra else []),
        (sources, order, *parts),
        scalars=2,
        scratch=(pltpu.VMEM((width, deep), BF16), pltpu.VMEM((deep, width), BF16)),
        limit=10,
        after=after,
        near=near,
    )
    return (mine, other), small


class Source:
    def __init__(self, halves=None, blocks=None, flag=None):
        self.halves, self.blocks, self.flag = halves, blocks, flag

    def operands(self, which):
        scalars = [] if self.flag is None else [self.flag]
        arrays = []
        for i in which:
            arrays += [] if self.halves is None else [self.halves[i]]
            arrays += [] if self.blocks is None else self.blocks[i]
        return scalars, arrays

    def reader(self, which, scalar_refs, refs):
        refs, table = list(refs), {}
        for i in which:
            base = None if self.halves is None else refs.pop(0)
            count = 0 if self.blocks is None else len(self.blocks[i])
            table[i] = (base, [refs.pop(0) for _ in range(count)])

        def read(i, start, rows):
            base, blocks = table[i]
            value = None
            if blocks:
                size = blocks[0].shape[0]
                value = blocks[start // size][start % size : start % size + rows, :]
            if base is not None:
                at_hand = base[start : start + rows, :]
                if value is None:
                    return at_hand
                value = jnp.where(scalar_refs[0][0] != 0, at_hand, value)
            return value

        return read


def collect(source, rows, width):
    half = rows // 2
    scalars, arrays = source.operands((0, 1))

    def body(*refs):
        read = source.reader((0, 1), refs[: len(scalars)], refs[len(scalars) : -2])
        for i, out in enumerate(refs[-2:]):
            for at in range(0, half, STEP):
                out[at : at + STEP, :] = read(i, at, STEP)

    shape = ((half, width), BF16)
    return run(body, [shape, shape], (*scalars, *arrays), scalars=len(scalars), flops=rows * width)


def project(info, source, gain, bias, weights, shift, rows, save, after=()):
    cols, width = weights[0].shape
    heads = cols // HD
    scalars, arrays = source.operands((0, 1))
    count, total = len(arrays), rows
    half = total // 2
    step = STEP

    def body(*refs):
        info_ref, flags = refs[0], refs[1 : 1 + len(scalars)]
        refs = refs[1 + len(scalars) :]
        read = source.reader((0, 1), flags, refs[:count])
        g_ref, b_ref, *w_refs = refs[count : count + 5]
        s_ref, x_ref, *outs, n_ref = refs[count + 5 :]
        for index in (0, 1):
            for at in range(0, half, step):
                value = read(index, at, step)
                if index == 0:
                    x_ref[at : at + step, :] = value
                unit, _ = unit_rows(value.astype(F32))
                n_ref[index * half + at : index * half + at + step, :] = (
                    unit * g_ref[...] + b_ref[...]
                ).astype(BF16)
        row = lax.broadcasted_iota(jnp.int32, (total, LANES - HD), 0)
        lane = lax.broadcasted_iota(jnp.int32, (total, LANES - HD), 1)
        pad_start = info_ref[0]
        padded = (row >= pad_start) & (row < pad_start + info_ref[1])
        ones = jnp.where(lane == 0, 1.0, 0.0).astype(BF16)
        mask = jnp.where((lane == 0) & padded, FAR, 0.0).astype(BF16)
        normed = n_ref[...]
        for i, (out, extra) in enumerate(zip(outs[:3], (ones, mask, ones))):
            here = slice(i * cols, (i + 1) * cols)
            value = (mm_nt(normed, w_refs[i][...]) + s_ref[:, here]).astype(BF16)
            for h in range(heads):
                out[:, h * LANES : (h + 1) * LANES] = jnp.concatenate(
                    [value[:, h * HD : (h + 1) * HD], extra], axis=1
                )

    wide = ((total, heads * LANES), BF16)
    return run(
        body,
        [((half, width), BF16), wide, wide, wide] + ([((total, width), BF16)] if save else []),
        (info, *scalars, *arrays, gain, bias, *weights, shift),
        scalars=1 + len(scalars),
        flops=6 * total * width * cols,
        scratch=() if save else (pltpu.VMEM((total, width), BF16),),
        limit=LIMIT if save else LIMIT + 2,
        after=after,
    )


def attend(first_row, q, k, v, wout, out_type, save):
    total, wide = q.shape
    heads = wide // LANES
    half = total // 2
    step = half

    def body(q_ref, k_ref, v_ref, w_ref, z_ref, *saved):
        for at in range(0, half, step):
            outs, logs = [], []
            for h in range(heads):
                lanes = slice(h * LANES, (h + 1) * LANES)
                scores = mm_nt(q_ref[first_row + at : first_row + at + step, lanes], k_ref[:, lanes])
                highest = jnp.max(scores, 1, keepdims=True)
                weights = jnp.exp2((scores - highest) * (SCALE * LOG2E)).astype(BF16)
                mixed = mm(weights, v_ref[:, lanes])
                sums = mixed[:, HD : HD + 1]
                outs.append((mixed / sums).astype(BF16)[:, :HD])
                logs.append(highest * (SCALE * LOG2E) + jnp.log(sums) * LOG2E)
            mixed = jnp.concatenate(outs, axis=1)
            z_ref[at : at + step, :] = mm(mixed, w_ref[...]).astype(out_type)
            if not save:
                continue
            saved[0][at : at + step, :] = mixed
            logs = jnp.concatenate(logs + [jnp.zeros((step, LANES - heads), F32)], axis=1)
            saved[1][:, at : at + step] = logs.T[:8, :]

    return run(
        body,
        [((half, wout.shape[1]), out_type)]
        + ([((half, heads * HD), BF16), ((8, half), F32)] if save else []),
        (q, k, v, wout),
        flops=4 * half * total * LANES * heads + 2 * half * heads * HD * wout.shape[1],
    )


def middle(xm, own, arrived, out_bias, gain, bias, after=()):
    half, width = xm.shape
    parts = len(arrived) + 1
    rows = half // parts

    def body(x_ref, own_ref, *refs):
        got = refs[: parts - 1]
        ob_ref, g_ref, b_ref, h_ref, n_ref = refs[parts - 1 :]
        def step(i, carry):
            at = pl.multiple_of(i * STEP, 16)
            here = pl.ds(at, STEP)
            value = x_ref[here, :].astype(F32) + ob_ref[...]
            total = own_ref[here, :].astype(F32)
            for shift, ref in enumerate(got, 1):
                there = pl.multiple_of(lax.rem(at + shift * rows, half), 16)
                total = total + ref[pl.ds(there, STEP), :].astype(F32)
            value = value + total
            h_ref[here, :] = value
            unit, _ = unit_rows(value)
            n_ref[here, :] = (unit * g_ref[...] + b_ref[...]).astype(BF16)
            return carry

        lax.fori_loop(0, half // STEP, step, 0)

    return run(
        body,
        [((half, width), F32), ((half, width), BF16)],
        (xm, own, *arrived, out_bias, gain, bias),
        flops=20 * half * width,
        after=after,
    )


def mlp(n2, w_up, b_up, w_down, out_type, save):
    half, width = n2.shape
    hidden = w_up.shape[0]
    step = half

    def body(n_ref, wu_ref, bu_ref, wd_ref, z_ref, *saved):
        for at in range(0, half, step):
            here = slice(at, at + step)
            u = mm_nt(n_ref[here, :], wu_ref[...]) + bu_ref[...]
            square = u * u
            t = jnp.tanh(GELU_A * u * (1.0 + GELU_B * square))
            low = 0.5 * (1.0 + t)
            active = (u * low).astype(BF16)
            if save:
                slope = low + (0.5 * GELU_A) * u * (1.0 - t * t) * (1.0 + (3 * GELU_B) * square)
                saved[0][here, :] = active
                saved[1][here, :] = slope.astype(BF16)
            z_ref[here, :] = mm(active, wd_ref[...]).astype(out_type)

    outs = [((half, width), out_type)]
    if save:
        outs += [((half, hidden), BF16)] * 2
    return run(body, outs, (n2, w_up, b_up, w_down), flops=4 * half * width * hidden)


def mlp_back(g, slope, w_up, w_down, out_type, save, after=()):
    half, hidden = slope.shape
    width = w_up.shape[1]

    def body(g_ref, s_ref, wu_ref, wd_ref, z_ref, *saved):
        grad = (mm_nt(g_ref[...], wd_ref[...]) * s_ref[...].astype(F32)).astype(BF16)
        if save:
            saved[0][...] = grad
        z_ref[...] = mm(grad, wu_ref[...]).astype(out_type)

    return run(
        body,
        [((half, width), out_type)] + ([((half, hidden), BF16)] if save else []),
        (g, slope, w_up, w_down),
        flops=4 * half * width * hidden,
        after=after,
    )


def middle_back(g, h, own, arrived, gain, after=()):
    half, width = g.shape
    parts = len(arrived) + 1
    rows = half // parts

    def body(g_ref, h_ref, own_ref, *refs):
        got = refs[: parts - 1]
        gain_ref, d_ref, low_ref, sums_ref = refs[parts - 1 :]
        def step(i, sums):
            at = pl.multiple_of(i * STEP, 16)
            here = pl.ds(at, STEP)
            grad = own_ref[here, :].astype(F32)
            for shift, ref in enumerate(got, 1):
                there = pl.multiple_of(lax.rem(at + shift * rows, half), 16)
                grad = grad + ref[pl.ds(there, STEP), :].astype(F32)
            unit, inverse = unit_rows(h_ref[here, :])
            scaled = grad * gain_ref[...]
            first = jnp.mean(scaled, 1, keepdims=True)
            second = jnp.mean(scaled * unit, 1, keepdims=True)
            upstream = g_ref[here, :].astype(F32)
            total = upstream + inverse * (scaled - first - unit * second)
            d_ref[here, :] = total
            low = total.astype(BF16)
            low_ref[here, :] = low
            terms = (grad * unit, grad, upstream, low.astype(F32))
            return tuple(a + jnp.sum(t, 0, keepdims=True) for a, t in zip(sums, terms))

        zeros = (jnp.zeros((1, width), F32),) * 4
        sums = lax.fori_loop(0, rows // STEP, step, zeros)
        lax.fori_loop(rows // STEP, half // STEP, lambda i, c: (step(i, zeros), c)[1], 0)
        for i in range(4):
            sums_ref[i : i + 1, :] = sums[i]

    return run(
        body,
        [((half, width), F32), ((half, width), BF16), ((8, width), F32)],
        (g, h, own, *arrived, gain),
        flops=30 * half * width,
        after=after,
    )


def attend_back(dm, do, wout, q, k, v, lm, lo):
    half = dm.shape[0]
    total, wide = q.shape
    heads = wide // LANES
    step = total

    def body(dm_ref, do_ref, w_ref, q_ref, k_ref, v_ref, lm_ref, lo_ref,
             d_ref, up_ref, log_ref, p_ref, w_ref2):
        for index, ref in enumerate((dm_ref, do_ref)):
            here = slice(index * half, (index + 1) * half)
            grad = mm_nt(ref[...], w_ref[...]).astype(BF16)
            fill = jnp.zeros((half, LANES - HD), BF16)
            for h in range(heads):
                cols = slice(h * HD, (h + 1) * HD)
                up = jnp.concatenate([grad[:, cols], fill], axis=1)
                up_ref[here, h * LANES : (h + 1) * LANES] = up
        log_ref[0:8, 0:half] = lm_ref[...]
        log_ref[0:8, half:total] = lo_ref[...]
        dqs, dks, dvs = [], [], []
        for h in range(heads):
            lanes = slice(h * LANES, (h + 1) * LANES)
            up = up_ref[:, lanes]
            queries = q_ref[:, lanes]
            sums = jnp.zeros((1, total), F32)
            dv_h = []
            for at in range(0, total, step):
                here = slice(at, at + step)
                scores = mm_nt(k_ref[here, lanes], queries)
                probs = jnp.exp2(scores * (SCALE * LOG2E) - log_ref[h : h + 1, :])
                weighted = probs * mm_nt(v_ref[here, lanes], up)
                sums = sums + jnp.sum(weighted, 0, keepdims=True)
                p_ref[here, :] = probs
                w_ref2[here, :] = weighted
                dv_h.append(mm(probs.astype(BF16), up).astype(BF16)[:, :HD])
            dq_t = jnp.zeros((LANES, total), F32)
            dk_h = []
            for at in range(0, total, step):
                here = slice(at, at + step)
                dscores = (w_ref2[here, :] - p_ref[here, :] * sums).astype(BF16)
                dk_h.append((mm(dscores, queries) * SCALE).astype(BF16)[:, :HD])
                dq_t = dq_t + mm_tn(k_ref[here, lanes], dscores)
            dqs.append((dq_t * SCALE).T.astype(BF16)[:, :HD])
            dks.append(jnp.concatenate(dk_h, axis=0))
            dvs.append(jnp.concatenate(dv_h, axis=0))
        d_ref[...] = jnp.concatenate([*dqs, *dks, *dvs], axis=1)

    return run(
        body,
        [((total, 3 * heads * HD), BF16)],
        (dm, do, wout, q, k, v, lm, lo),
        flops=10 * total * total * LANES * heads + 2 * total * heads * HD * dm.shape[1],
        scratch=(
            pltpu.VMEM((total, wide), BF16),
            pltpu.VMEM((8, total), F32),
            pltpu.VMEM((total, total), F32),
            pltpu.VMEM((total, total), F32),
        ),
        limit=12,
    )[0]


def project_back(first_row, grad, weight, out_type):
    total = grad.shape[0]
    half = total // 2
    cols, width = weight.shape

    def body(d_ref, w_ref, z_ref):
        z_ref[...] = mm(d_ref[first_row : first_row + half, :], w_ref[...]).astype(out_type)

    return run(
        body, [((half, width), out_type)], (grad, weight), flops=2 * half * cols * width
    )[0]


def start_back(xm, dh, own, arrived, gain, after=()):
    rows, width = own.shape
    part = rows // pieces_of(rows)
    count = len(arrived)

    def body(x_ref, dh_ref, own_ref, *refs):
        got = refs[:count]
        gain_ref, d_ref, sums_ref, *low_refs = refs[count:]
        def step(i, sums):
            here = pl.ds(pl.multiple_of(i * STEP, 16), STEP)
            grad = own_ref[here, :]
            for ref in got:
                grad = grad + ref[here, :].astype(F32)
            unit, inverse = unit_rows(x_ref[here, :].astype(F32))
            scaled = grad * gain_ref[...]
            first = jnp.mean(scaled, 1, keepdims=True)
            second = jnp.mean(scaled * unit, 1, keepdims=True)
            total = dh_ref[here, :] + inverse * (scaled - first - unit * second)
            d_ref[here, :] = total
            return tuple(
                a + jnp.sum(t, 0, keepdims=True) for a, t in zip(sums, (grad * unit, grad))
            )

        sums = lax.fori_loop(0, rows // STEP, step, (jnp.zeros((1, width), F32),) * 2)
        for i in range(2):
            sums_ref[i : i + 1, :] = sums[i]
        for i, ref in enumerate(low_refs):
            ref[...] = d_ref[i * part : (i + 1) * part, :].astype(BF16)

    d, sums, *low = run(
        body,
        [((rows, width), F32), ((8, width), F32)]
        + [((part, width), BF16)] * (rows // part),
        (xm, dh, own, *arrived, gain),
        flops=30 * rows * width,
        after=after,
    )
    return d, low, sums


def finish_rows(hidden, total, arrived, out_bias, after=()):
    rows, width = total[0].shape
    part = rows // pieces_of(rows)

    def body(h_ref, total_ref, *refs):
        bias_ref, y_ref, *low_refs = refs[len(arrived) :]
        value = total_ref[...]
        for ref in refs[: len(arrived)]:
            value = value + ref[...].astype(F32)
        value = h_ref[0:rows, :] + value + bias_ref[...]
        y_ref[...] = value
        for i, ref in enumerate(low_refs):
            ref[...] = value[i * part : (i + 1) * part, :].astype(BF16)

    y, *low = run(
        body,
        [((rows, width), F32)] + [((part, width), BF16)] * (rows // part),
        (hidden, total[0], *arrived, out_bias),
        flops=4 * rows * width,
        after=after,
    )
    return y, low


def outer(pairs, low, high, after=()):
    width = pairs[0][1].shape[1]

    def body(*refs):
        out = refs[-1]
        total = None
        for i in range(len(pairs)):
            term = mm_tn(refs[2 * i][:, low:high], refs[2 * i + 1][...])
            total = term if total is None else total + term
        out[...] = total.astype(BF16)

    return run(
        body,
        [((high - low, width), BF16)],
        [array for pair in pairs for array in pair],
        flops=2 * (high - low) * width * sum(pair[0].shape[0] for pair in pairs),
        limit=16,
        after=after,
    )[0]


def add(left, right, after=()):
    def body(left_ref, right_ref, out):
        out[...] = (left_ref[...].astype(F32) + right_ref[...].astype(F32)).astype(BF16)

    return run(body, [(left.shape, BF16)], (left, right), flops=left.size, after=after)[0]


def hold(arrays, after):
    count = len(arrays)
    anywhere = pl.BlockSpec(memory_space=pl.ANY)
    return pl.pallas_call(
        lambda *refs: None,
        out_shape=[jax.ShapeDtypeStruct(a.shape, a.dtype) for a in arrays],
        in_specs=[anywhere] * (count + len(after)),
        out_specs=[anywhere] * count,
        input_output_aliases={i: i for i in range(count)},
    )(*arrays, *after)


def core_swap(value):
    size = lax.axis_size("tensor")
    return lax.ppermute(value, "tensor", [(i, i ^ 1) for i in range(size)])


def chip_shift(value, shift):
    size = lax.axis_size("tensor")
    return lax.ppermute(value, "tensor", [(i, (i + 2 * shift) % size) for i in range(size)])


def share_half(half, chips):
    return [chip_shift(half, s) for s in range(1, chips)]


def spread_block(block, chips):
    mine = [block] + [chip_shift(block, chips - p) for p in range(1, chips)]
    return mine, [core_swap(b) for b in mine]


def hand_over(pieces, chips, after=()):
    if after:
        pieces = hold(pieces, after)
    spread = [spread_block(piece, chips) for piece in pieces]
    return [[spread[j][i][p] for p in range(chips) for j in range(len(pieces))] for i in (0, 1)]


def pieces_of(rows):
    return 2 if rows % 32 == 0 and rows >= 128 else 1


def sum_blocks(mine, other, chips):
    rows = mine.shape[0] // chips

    def body(mine_ref, other_ref, own_ref, *sends):
        own_ref[...] = mine_ref[0:rows, :] + other_ref[0:rows, :].astype(F32)
        for p, ref in enumerate(sends, 1):
            here = slice(p * rows, (p + 1) * rows)
            ref[...] = (mine_ref[here, :] + other_ref[here, :].astype(F32)).astype(BF16)

    shape = (rows, mine.shape[1])
    own, *sends = run(body, [(shape, F32)] + [(shape, BF16)] * (chips - 1), (mine, other))
    return (own, *sends), [chip_shift(send, p) for p, send in enumerate(sends, 1)]


def to_section(value, step):
    pairs = [(0, 1)] if step > 0 else [(1, 0)]
    return lax.ppermute(value, "section", pairs)


class Turns:
    def __init__(self):
        self.last, self.first = (), ()

    def take(self):
        return self.last

    def end(self, *arrays):
        self.last = tuple(arrays)


def forward(source, w, info, chips, rows, save, turns):
    source = source()
    xm, q, k, v, *kept = project(
        info, source, w["gain"][0], w["bias"][0], w["three"], w["qkv_shift"], rows, save,
        turns.take(),
    )
    turns.first = (q,)
    half = rows // 2
    z_other, *kept_other = attend(half, q, k, v, w["wout"], BF16, save)
    z_other = core_swap(z_other)
    z_mine, *kept_mine = attend(0, q, k, v, w["wout"], F32, save)
    own = add(z_mine, z_other)
    turns.end(own)
    arrived = share_half(own, chips)
    yield
    hidden, n2m = middle(
        xm, own, arrived, w["out_bias"][0], w["gain"][1], w["bias"][1], turns.take()
    )
    n2o = core_swap(n2m)
    mine = mlp(n2m, w["w_up"], w["b_up"], w["w_down"], F32, save)
    other = mlp(n2o, w["w_up"], w["b_up"], w["w_down"], BF16, save)
    y_other = core_swap(other[0])
    total, arrived = sum_blocks(mine[0], y_other, chips)
    saved = None
    if save:
        saved = dict(
            x=xm, normed=kept[0], q=q, k=k, v=v,
            o=(kept_mine[0], kept_other[0]), l=(kept_mine[1], kept_other[1]),
            h=hidden, n2=(n2m, n2o), m=(mine[1], other[1]), slope=(mine[2], other[2]),
        )
        turns.end(mine[2], other[2])
        result, _ = finish_rows(hidden, total, arrived, w["out_bias"][1])
        return result, saved
    turns.end(*total)
    yield
    _, low = finish_rows(hidden, total, arrived, w["out_bias"][1], turns.take())
    turns.end(low[0])
    return [to_section(piece, 1) for piece in low]


def backward(source, saved, w, chips, turns, pass_on):
    gm, go = source().halves
    save = not pass_on
    z_other, *du_other = mlp_back(
        go, saved["slope"][1], w["w_up"], w["w_down"], BF16, save, turns.take()
    )
    z_other = core_swap(z_other)
    z_mine, *du_mine = mlp_back(gm, saved["slope"][0], w["w_up"], w["w_down"], F32, save)
    own = add(z_mine, z_other)
    turns.end(own)
    arrived = share_half(own, chips)
    work = dict(du=(*du_mine, *du_other))
    yield work
    dh, dhm, sums_two = middle_back(
        gm, saved["h"], own, arrived, w["gain"][1], turns.take()
    )
    dho = core_swap(dhm)
    q, k, v = saved["q"], saved["k"], saved["v"]
    dqkv = attend_back(dhm, dho, w["wout"], q, k, v, *saved["l"])
    half = gm.shape[0]
    d_other = core_swap(project_back(half, dqkv, w["qkv"], BF16))
    d_mine = project_back(0, dqkv, w["qkv"], F32)
    total, arrived = sum_blocks(d_mine, d_other, chips)
    turns.end(*total)
    work.update(dh=(dhm, dho), dqkv=dqkv)
    yield work
    dx, low, sums_one = start_back(saved["x"], dh, total[0], arrived, w["gain"][0], turns.take())
    turns.end(low[0])
    work.update(sums=(sums_one, sums_two))
    return dx, [to_section(piece, -1) for piece in low] if pass_on else None, work


def step_all(steps):
    results = [None] * len(steps)
    live = list(range(len(steps)))
    rounds = []
    while live:
        given = {}
        for i in list(live):
            try:
                given[i] = next(steps[i])
            except StopIteration as end:
                results[i] = end.value
                live.remove(i)
        rounds.append(given)
        yield results if not live else given


def finish(value):
    rows, width = value.shape
    step = 272

    def body(value_ref, out_ref):
        out_ref[...] = value_ref[...].astype(F32).reshape(step, 1, width)

    return pl.pallas_call(
        body,
        out_shape=jax.ShapeDtypeStruct((rows, 1, width), F32),
        grid=(pl.cdiv(rows, step),),
        in_specs=[pl.BlockSpec((step, width), lambda i: (i, 0))],
        out_specs=pl.BlockSpec((step, 1, width), lambda i: (i, 0, 0)),
        compiler_params=pltpu.CompilerParams(vmem_limit_bytes=12 * 2**20),
    )(value)


def per_device(inputs, norm_gain, norm_bias, w_query, b_query, w_key, w_value, b_value, w_out,
               out_bias, w_up, b_up, w_down):
    first = lax.axis_index("section") == 0
    flag = first.astype(jnp.int32)[None]
    me = lax.axis_index("tensor")
    size = lax.axis_size("tensor")
    chips = size // 2
    chip, core = me // 2, me % 2
    _, micro, images, length, cols = inputs.shape
    unit = 16 * size
    total = -(-length // unit) * unit
    rows = total // size
    pad = total - length
    places = jnp.arange(size)
    order = ((chip + places % chips) % chips) * 2 + (core + places // chips) % 2
    order = order.astype(jnp.int32)
    rel = ((places // 2 - chip) % chips + chips * ((places + core) % 2)).astype(jnp.int32)
    info = jnp.stack([rel[size - 1] * rows + rows - pad, jnp.int32(pad)])
    images_all = micro * images
    sources = order
    small = jnp.concatenate(
        [norm_gain[0], norm_bias[0], out_bias[0], jnp.zeros((2, cols), F32)], axis=0
    )
    high = lax.reduce_precision(small, 8, 7)
    middle_part = lax.reduce_precision(small - high, 8, 7)
    thirds = jnp.concatenate([high, middle_part, small - high - middle_part], axis=0)
    features = inputs[0].reshape(images_all, length, cols).transpose(0, 2, 1)
    three = (w_query[0].T, w_key[0].T, w_value[0].T)
    qkv = jnp.concatenate(three, axis=0)
    spread = []
    for n in range(images_all):
        block = features[n]
        if n == 0:
            block = jnp.pad(block, ((0, 0), (0, pad)))
            block = jnp.concatenate([block, thirds.astype(BF16).T], axis=1)
        else:
            (block,) = hold([block], full[0][:1])
        mine, other = spread_block(block, chips)
        spread.append(mine + other)
        if n == 0:
            halves, (small,) = assemble(
                spread[0], length, sources, order, rows, small.shape[0],
                near=three,
            )
            full = {0: halves}
    turns = Turns()

    def whole(n):
        if n not in full:
            full[n], _ = assemble(spread[n], length, sources, order, rows, 0, turns.take())
        return Source(full[n])

    w = dict(
        gain=(small[0:1], small[1:2]), bias=(small[2:3], small[3:4]),
        out_bias=(small[4:5], small[5:6]),
        three=three, qkv=qkv, qkv_shift=jnp.concatenate([b_query, jnp.zeros_like(b_query), b_value], axis=1),
        wout=w_out[0], w_up=w_up[0].T, b_up=b_up, w_down=w_down[0],
    )
    span = range(images_all)

    def widen(n, pieces, chosen):
        return Source(full[n], hand_over(pieces, chips), chosen)

    *_, lows = step_all(
        [
            forward(functools.partial(whole, n), w, info, chips, total, False, turns)
            for n in span
        ]
    )
    *_, done = step_all(
        [
            forward(
                functools.partial(widen, n, lows[n], flag), w, info, chips, total, True, turns
            )
            for n in span
        ]
    )
    results, saves = [d[0] for d in done], [d[1] for d in done]
    *_, done = step_all(
        [backward(functools.partial(whole, n), saves[n], w, chips, turns, True) for n in span]
    )
    lows = [d[1] for d in done]
    grads = [collect(widen(n, lows[n], 1 - flag), total, cols * size) for n in span]
    both = (0, 1)
    hidden = w_up.shape[2]
    steps = [
        backward(functools.partial(Source, grads[n]), saves[n], w, chips, turns, False)
        for n in span
    ]
    next(steps[0])
    g_down = outer(
        [(saves[n]["m"][i], grads[n][i]) for n in span for i in both], 0, hidden, turns.take()
    )
    turns.end(g_down)
    g_down = lax.psum(g_down, "dp")
    for step in steps[1:]:
        next(step)
    steps = step_all(steps)
    works = next(steps)
    width = cols * size
    heads = b_query.shape[1]
    g_up = outer(
        [(works[n]["du"][i], saves[n]["n2"][i]) for n in span for i in both], 0, hidden,
        turns.take(),
    )
    rest = [outer([(saves[n]["o"][i], works[n]["dh"][i]) for n in span for i in both], 0, heads)]
    rest.append(outer([(works[n]["dqkv"], saves[n]["normed"]) for n in span], 0, 3 * heads))
    done = next(steps)
    works = [d[2] for d in done]
    ends = [jnp.where(first, done[n][0], results[n]) for n in span]

    def total_of(parts):
        return sum(jnp.sum(p.astype(F32), 0) for p in parts)

    wide = sum(
        jnp.stack(
            [
                works[n]["sums"][0][0], works[n]["sums"][1][0],
                works[n]["sums"][0][1], works[n]["sums"][1][1],
                works[n]["sums"][1][3], works[n]["sums"][1][2],
            ]
        )
        for n in span
    )
    wide = lax.psum(wide, "tensor")
    wide = lax.dynamic_slice_in_dim(wide, me * cols, cols, 1)
    vector = jnp.concatenate(
        [
            wide.reshape(-1),
            total_of([works[n]["dqkv"] for n in span]),
            total_of([works[n]["du"][i] for n in span for i in both]),
        ]
    )
    count = vector.size
    lines = -(-count // (16 * width)) * 16
    vector = jnp.pad(vector, (0, lines * width - count)).reshape(lines, width).astype(BF16)
    rest = hold([g_up, *rest, vector], (g_down,))
    g_up, g_out, g_qkv, vector = lax.psum(rest, "dp")
    g_query, g_key, g_value = (g_qkv[i * heads : (i + 1) * heads] for i in range(3))
    vector = vector.astype(F32).reshape(-1)
    wide = vector[: 6 * cols].reshape(6, cols)
    narrow = vector[6 * cols : count]

    ends = jnp.stack(ends).reshape(images_all, rows, size, cols)
    ends = lax.all_to_all(ends, "tensor", split_axis=2, concat_axis=1, tiled=True)
    ends = ends.reshape(images_all, total, cols)[:, :length]
    ends = ends.reshape(1, micro, images, length, cols)
    return (
        ends, wide[None, 0:2], wide[None, 2:4], g_query.T[None].astype(F32), narrow[None, :heads], g_key.T[None].astype(F32),
        g_value.T[None].astype(F32), narrow[None, 2 * heads : 3 * heads], g_out[None].astype(F32), wide[None, 4:6],
        finish(g_up).transpose(1, 2, 0),
        narrow[None, 3 * heads :], finish(g_down).transpose(1, 0, 2),
    )


def solution(mesh):
    columns = P("section", None, "tensor")
    vector = P("section", "tensor")
    stacked = P("section", "tensor", None)
    tokens = P("section", None, "dp", None, "tensor")
    weights = (columns, columns, columns, vector, columns, columns, vector, stacked, columns,
               columns, vector, stacked)
    return jax.shard_map(
        per_device, mesh=mesh, in_specs=(tokens, *weights), out_specs=(tokens, *weights),
        check_vma=False,
    )
```
